128 devices in a mesh: section: 2 (over x_lo), rows: 8 (over y, x_hi), chan: 8 (over z, core).
Axes of the slice: x: 4 (x_hi: 2, x_lo: 2; x = x_hi * 2 + x_lo), y: 4, z: 4, core: 2. Of those that a mesh axis runs over, the one named last changes fastest.
Arguments:
- condition: float32 [12, 128, 1024], P(None, 'rows'), may hold values from -6 to 6
- target: float32 [12, 128, 1024], P(None, 'rows'), may hold values from -6 to 6
- noise_draw: float32 [12, 128, 1024], P(None, 'rows'), may hold values from -6 to 6
- sigma_index: int32 [1], replicated, may hold values from 0 to 31
- reg_first: bfloat16 [3, 3, 12, 128], P(None, None, None, 'chan'), may hold values from -0.625 to 0.625
- reg_second: bfloat16 [3, 3, 128, 12], P(None, None, 'chan'), may hold values from -0.1875 to 0.1875
- first_kernel: bfloat16 [3, 3, 24, 128], P(None, None, None, ('section', 'chan')), may hold values from -0.4375 to 0.4375
- second_kernel: bfloat16 [3, 3, 128, 128], P(None, None, None, ('section', 'chan')), may hold values from -0.1875 to 0.1875
- third_kernel: bfloat16 [3, 3, 128, 12], P(None, None, ('section', 'chan')), may hold values from -0.1875 to 0.1875
- film_scale: bfloat16 [128], P(('section', 'chan')), may hold values from -4 to 4
Outputs:
- denoised: bfloat16 [12, 128, 1024], P(None, 'rows')
- grad_first: float32 [3, 3, 24, 128], P(None, None, None, ('section', 'chan'))
- grad_second: float32 [3, 3, 128, 128], P(None, None, None, ('section', 'chan'))
- grad_third: float32 [3, 3, 128, 12], P(None, None, ('section', 'chan'))
- grad_film: float32 [128], P(('section', 'chan'))
The draws below stay inside these ranges and needn't reach their ends.
Inputs may be any that keep to these rules, and one draw needn't show every extreme that they name: `sigma_index`: an index into the table of 32 noise levels.
All inputs are finite; a program needn't handle non-finite values.
Results may differ from the reference program's by a relative error of at most 0.008.
Values may be sent and summed in bfloat16 or wider, within the bound.
No kernel may reach another device: no remote copies, remote signals or barrier semaphores. Data moves between devices by JAX's collectives and lax.ppermute only.
A program may use at most 128 MiB of HBM per device.

```python
import math
import jax
import jax.numpy as jnp
from jax import lax

C = 128
CIN = 12
COUT = 12
NW = 1024
NSIG = 32
NH = 128


def block_scale(rng, dims, split, least, high):
    level = 1.0
    for dim, parts in split:
        heights = jax.random.uniform(jax.random.fold_in(jax.random.fold_in(rng, 6), dim), (parts,), jnp.float32, least / len(split), high / len(split))
        level = level * jnp.repeat(jnp.exp(heights), dims[dim] // parts).reshape((-1,) + (1,) * (len(dims) - 1 - dim))
    return level


def scatter_about(stream_key, extent, deviation, limit, pieces=(), held_as=jnp.bfloat16):
    values = deviation * jax.random.normal(stream_key, extent, jnp.float32)
    if pieces:
        values = values * block_scale(stream_key, extent, pieces, -0.22, 0.18)
    return jnp.clip(values, -limit, limit).astype(held_as)


def setup_inputs(seed: int = 0) -> dict:
    splits = jax.random.split(jax.random.key(seed), 11)
    condition = scatter_about(splits[0], (CIN, NH, NW), 1.0, 6.0, ((1, 8),), jnp.float32)
    target = scatter_about(splits[1], (COUT, NH, NW), 1.0, 6.0, ((1, 8),), jnp.float32)
    noise_draw = scatter_about(splits[2], (COUT, NH, NW), 1.0, 6.0, ((1, 8),), jnp.float32)
    sigma_index = jax.random.randint(splits[3], (1,), 0, NSIG).astype(jnp.int32)
    reg_first = scatter_about(splits[4], (3, 3, CIN, C), (9 * CIN) ** -0.5, 0.625, ((3, 8),))
    reg_second = scatter_about(splits[5], (3, 3, C, COUT), (9 * C) ** -0.5, 0.1875, ((2, 8),))
    first_kernel = scatter_about(splits[6], (3, 3, CIN + COUT, C), (9 * (CIN + COUT)) ** -0.5, 0.4375, ((3, 16),))
    second_kernel = scatter_about(splits[7], (3, 3, C, C), (9 * C) ** -0.5, 0.1875, ((3, 16),))
    third_kernel = scatter_about(splits[8], (3, 3, C, COUT), (9 * C) ** -0.5, 0.1875, ((2, 16),))
    film_scale = scatter_about(splits[9], (C,), 1.5, 4.0, ((0, 16),))
    return {"condition": condition, "target": target, "noise_draw": noise_draw, "sigma_index": sigma_index, "reg_first": reg_first, "reg_second": reg_second, "first_kernel": first_kernel, "second_kernel": second_kernel, "third_kernel": third_kernel, "film_scale": film_scale}


sigma_low = 0.25
sigma_high = 4.0
rho_power = 7.0
sigma_data = 0.5

def noise_terms(sigma_index):
    steps_at = jnp.arange(NSIG, dtype=jnp.float32) / (NSIG - 1)
    high_root = sigma_high ** (1.0 / rho_power)
    low_root = sigma_low ** (1.0 / rho_power)
    levels = (high_root + steps_at * (low_root - high_root)) ** rho_power
    picked = jnp.arange(NSIG, dtype=jnp.int32) == sigma_index[0]
    sigma_level = jnp.sum(jnp.where(picked, levels, jnp.zeros_like(levels)))
    total_var = sigma_level * sigma_level + sigma_data * sigma_data
    skip_coef = sigma_data * sigma_data / total_var
    out_coef = sigma_level * sigma_data / jnp.sqrt(total_var)
    in_coef = 1.0 / jnp.sqrt(total_var)
    noise_coef = jnp.log(8.0 * sigma_level) / 4.0
    loss_weight = total_var / (sigma_level * sigma_data) ** 2
    return (sigma_level, skip_coef, out_coef, in_coef, noise_coef, loss_weight)

def conv_same(grid_field, kernel):
    result_conv = lax.conv_general_dilated(grid_field.astype(jnp.float32)[None], kernel.astype(jnp.float32), (1, 1), ((1, 1), (1, 1)), dimension_numbers=('NCHW', 'HWIO', 'NCHW'), preferred_element_type=jnp.float32)
    return result_conv[0]

def kernel_grad(grid_field, delta_in):
    row_total = delta_in.shape[1]
    col_total = delta_in.shape[2]
    padded = jnp.pad(grid_field.astype(jnp.float32), ((0, 0), (1, 1), (1, 1)))
    flat_delta = delta_in.astype(jnp.float32).reshape(delta_in.shape[0], row_total * col_total)
    taps_out = []
    for row_tap in range(3):
        row_list = []
        for col_tap in range(3):
            window_part = padded[:, row_tap:row_tap + row_total, col_tap:col_tap + col_total]
            window_part = window_part.reshape(grid_field.shape[0], row_total * col_total)
            row_list.append(jnp.dot(window_part, flat_delta.T, preferred_element_type=jnp.float32))
        taps_out.append(jnp.stack(row_list, 0))
    return jnp.stack(taps_out, 0)

def turned(kernel):
    return jnp.transpose(jnp.flip(kernel, (0, 1)), (0, 1, 3, 2))

def silu_slope(pre_act):
    sigmoid_at = jax.nn.sigmoid(pre_act)
    return sigmoid_at * (1.0 + pre_act * (1.0 - sigmoid_at))

def reference(condition, target, noise_draw, sigma_index, reg_first, reg_second, first_kernel, second_kernel, third_kernel, film_scale):
    sigma_level, skip_coef, out_coef, in_coef, noise_coef, loss_weight = noise_terms(sigma_index)
    grad_scale = 1.0 / math.sqrt(COUT * NH * NW)
    cond_low = condition.astype(jnp.bfloat16)
    reg_hidden = jax.nn.silu(conv_same(cond_low, reg_first)).astype(jnp.bfloat16)
    mean_field = conv_same(reg_hidden, reg_second).astype(jnp.bfloat16)
    resid_field = target - mean_field.astype(jnp.float32)
    noisy_field = resid_field + sigma_level * noise_draw
    stacked = jnp.concatenate([(in_coef * noisy_field).astype(jnp.bfloat16), cond_low], 0)
    film_gain = (1.0 + noise_coef * film_scale.astype(jnp.float32))[:, None, None]
    first_act = conv_same(stacked, first_kernel)
    hidden_one = jax.nn.silu(first_act * film_gain).astype(jnp.bfloat16)
    second_act = conv_same(hidden_one, second_kernel)
    second_hidden = jax.nn.silu(second_act).astype(jnp.bfloat16)
    out_full = conv_same(second_hidden, third_kernel)
    den_value = skip_coef * noisy_field + out_coef * out_full
    out_delta = (2.0 * loss_weight * out_coef * grad_scale * (den_value - resid_field)).astype(jnp.bfloat16)
    grad_third = kernel_grad(second_hidden, out_delta)
    second_delta = (conv_same(out_delta, turned(third_kernel)) * silu_slope(second_act)).astype(jnp.bfloat16)
    grad_second = kernel_grad(hidden_one, second_delta)
    back_first = conv_same(second_delta, turned(second_kernel))
    first_grad = back_first * silu_slope(first_act * film_gain)
    grad_film = noise_coef * lax.optimization_barrier(jnp.sum(first_grad * first_act, axis=(1, 2)))
    first_delta = (first_grad * film_gain).astype(jnp.bfloat16)
    grad_first = kernel_grad(stacked, first_delta)
    return (den_value.astype(jnp.bfloat16), grad_first, grad_second, grad_third, grad_film)
```

```python
import math

import numpy as np
import jax
import jax.numpy as jnp
from jax import lax
from jax.experimental import pallas as pl
from jax.experimental.pallas import tpu as pltpu
from jax.sharding import PartitionSpec as P

COUT = 12
NSIG = 32
NH = 128
NW = 1024
TW = 64
RIM = 8
PLANES = 5
SUB = 16
WIN = PLANES * SUB
TAPS = 9
FILM_LANE = 120
MIB = 1024 * 1024
GROUP = ("section", "chan")
f32 = jnp.float32
bf16 = jnp.bfloat16


def coef_table():
    i = np.arange(NSIG, dtype=np.float64)
    high, low = 4.0 ** (1 / 7), 0.25 ** (1 / 7)
    level = (high + i / (NSIG - 1) * (low - high)) ** 7
    total = level**2 + 0.25
    out_coef = 0.5 * level / np.sqrt(total)
    weight = total / (0.5 * level) ** 2
    table = np.zeros((NSIG, 8), np.float32)
    table[:, 0] = level
    table[:, 1] = 0.25 / total
    table[:, 2] = out_coef
    table[:, 3] = 1 / np.sqrt(total)
    table[:, 4] = np.log(8 * level) / 4
    table[:, 5] = 2 * weight * out_coef / math.sqrt(COUT * NH * NW)
    return table


def place_constants():
    sel_first = np.zeros((TAPS, 24, 256), np.float32)
    sel_low = np.zeros((TAPS, COUT, 128), np.float32)
    for tap in range(TAPS):
        for c in range(COUT):
            sel_first[tap, c, tap * COUT + c] = 1
            sel_first[tap, COUT + c, 128 + tap * COUT + c] = 1
            sel_low[tap, c, tap * COUT + c] = 1
    order = np.zeros((WIN, 128), np.float32)
    back = np.zeros((WIN, 128), np.float32)
    for t in range(PLANES):
        for s in range(SUB):
            col = PLANES * s + t
            order[t * SUB + s, col] = 1
            if RIM <= col < RIM + TW:
                back[t * SUB + s, col - RIM] = 1
                back[t * SUB + s, TW + col - RIM] = 1
    spread = np.zeros((128, 384), np.float32)
    repeat = np.zeros((128, 10 * 128), np.float32)
    for c in range(COUT):
        for g in range(TAPS):
            spread[24 + c, g * COUT + c] = 1
            for first in (0, 48, 80):
                spread[first + c, 128 + g * COUT + c] = 1
                spread[first + COUT + c, 256 + g * COUT + c] = 1
            for tap in range(TAPS):
                repeat[tap * COUT + c, tap * 128 + g * COUT + c] = 1
            repeat[(8 - g) * COUT + c, 9 * 128 + g * COUT + c] = 1
    return sel_first, sel_low, order, back, spread, repeat


def dot(a, b, ca=1, cb=0):
    return lax.dot_general(a, b, (((ca,), (cb,)), ((), ())), preferred_element_type=f32)


def sigmoid(v):
    return 1.0 / (1.0 + jnp.exp(-v))


def member():
    return lax.axis_index("section") * lax.axis_size("chan") + lax.axis_index("chan")


def pack_kernel(cond, target, noise, w1, w2, w3, r1, r2, film, sel_first, sel_low,
                own, last, leading, packed, scr, sems):
    start = member() * TW - RIM
    base = jnp.clip((start + 128) // 128 * 128 - 128, 0, NW - 256)
    base = pl.multiple_of(base, 128)
    copies = []
    for k, src in enumerate((target, noise, cond)):
        copy = pltpu.make_async_copy(src.at[:, :, pl.ds(base, 256)], scr.at[k], sems.at[k])
        copy.start()
        copies.append(copy)
    half = lax.axis_index("section") == 0
    eye = (lax.broadcasted_iota(jnp.int32, (8, 8), 0)
           == lax.broadcasted_iota(jnp.int32, (8, 8), 1)).astype(f32)
    blocks = []
    for a in range(3):
        for b in range(3):
            blocks.append(dot(eye, w2[a, b].astype(f32), 1, 1))
    first = jnp.zeros((8, 256), f32)
    third = jnp.zeros((8, 128), f32)
    reg_a = jnp.zeros((16, 128), f32)
    reg_b = jnp.zeros((16, 128), f32)
    for a in range(3):
        for b in range(3):
            tap = 3 * a + b
            first += dot(w1[a, b].astype(f32), sel_first[tap], 0, 0)
            third += dot(w3[a, b].astype(f32), sel_low[tap])
            reg_a += dot(r1[a, b].astype(f32), sel_low[tap], 0, 0)
            reg_b += dot(r2[a, b].astype(f32), sel_low[tap])
    lane = lax.broadcasted_iota(jnp.int32, (8, 128), 1)
    film_col = jnp.sum(eye * film[...].astype(f32), axis=1, keepdims=True)
    third = jnp.where(lane == FILM_LANE, film_col, third)
    blocks += [first[:, :128], first[:, 128:], third,
               jnp.where(half, reg_a[:8], reg_a[8:]), jnp.where(half, reg_b[:8], reg_b[8:])]
    for p in range(7):
        pair = jnp.concatenate(blocks[2 * p:2 * p + 2], axis=0).astype(bf16)
        for q in range(16):
            packed[q, p * 16:(p + 1) * 16, :] = pair
    offset = start - base
    shift = lax.rem(512 - offset, 256)
    for k, copy in enumerate(copies):
        copy.wait()
        rows = scr[k].reshape(COUT * 16, 256)
        moved = pltpu.roll(rows, shift, 1)[:, :128]
        col = start + lax.broadcasted_iota(jnp.int32, moved.shape, 1)
        moved = jnp.where((col >= 0) & (col < NW), moved, 0.0).reshape(COUT, 16, 128)
        own[k * COUT:(k + 1) * COUT] = moved
        last[k * COUT:(k + 1) * COUT] = moved[:, 8:]
        leading[k * COUT:(k + 1) * COUT] = moved[:, :8]


def put(ref, at, n, value):
    ref[pl.ds(at, n), 1:PLANES + 1] = value.astype(bf16)
    ref[pl.ds(at, n), 0] = pltpu.roll(value[:, PLANES - 1], 1, 1).astype(bf16)
    ref[pl.ds(at, n), PLANES + 1] = pltpu.roll(value[:, 0], SUB - 1, 1).astype(bf16)


def stack_taps(ref, at, n):
    parts = []
    for a in range(3):
        for b in range(3):
            parts.append(ref[pl.ds(at + a - 1, n), b:b + PLANES].reshape(n * WIN, 128))
    return jnp.concatenate(parts, axis=1)


def pick_taps(ref, at, n):
    lane = lax.broadcasted_iota(jnp.int32, (SUB, 128), 1)
    total = None
    for a in range(3):
        for b in range(3):
            low = (3 * a + b) * COUT
            mask = jnp.where((lane >= low) & (lane < low + COUT), 1.0, 0.0).astype(bf16)
            part = ref[pl.ds(at + a - 1, n), b:b + PLANES] * mask[None, None]
            total = part if total is None else total + part
    return total


def prep_kernel(own, before, after, order, spread, cond_taps, target9, noise9, scr, cond9, sems):
    copies = [
        pltpu.make_async_copy(before, scr.at[0:36, 0:8, :], sems.at[0]),
        pltpu.make_async_copy(own, scr.at[0:36, 8:24, :], sems.at[1]),
        pltpu.make_async_copy(after, scr.at[0:36, 24:32, :], sems.at[2]),
    ]
    for copy in copies:
        copy.start()
    scr[36:48] = jnp.zeros((12, 32, 128), f32)
    for copy in copies:
        copy.wait()
    flat = scr.reshape(48 * 32, 128)

    def row(i):
        x = flat[pl.ds(i, 48, stride=32), :]
        high = x.astype(bf16)
        rest = x[:32] - high[:32].astype(f32)
        mid = rest.astype(bf16)
        low = (rest - mid.astype(f32)).astype(bf16)
        rows = jnp.concatenate([high, mid, low, jnp.zeros((16, 128), bf16)], axis=0)
        cells = dot(order[...], rows, 1, 1).astype(bf16)
        wide = dot(cells, spread[...]).reshape(1, PLANES, SUB, 384)
        put(cond9, i, 1, wide[..., :128])
        return wide

    for i in range(1, 31):
        wide = row(i)
        if 3 <= i < 29:
            target9[i - 3:i - 2] = wide[..., 128:256]
            noise9[i - 3:i - 2] = wide[..., 256:]

    @pl.loop(0, 7)
    def _(k):
        at = 2 + 4 * k
        cond_taps[pl.ds(at - 2, 4)] = pick_taps(cond9, at, 4)


def step_kernel(index, table, cond_taps, target9, noise9, gathered, repeat, back, out,
                w2, w2t, w1, w3, w3f, w3r, r1, r2,
                hid, inp, one, two, dlt, sdl, taps_in, taps_d, resid, noisy, act, slope,
                den, grad1, film_sum, den_rows):
    level = index[0]
    sigma, skip, out_coef = table[level, 0], table[level, 1], table[level, 2]
    in_coef, noise_coef, delta_coef = table[level, 3], table[level, 4], table[level, 5]
    first_row = lax.axis_index("rows") * 16 - RIM
    first_col = member() * TW - RIM

    def block(k):
        pair = gathered[:, (k // 2) * 16:(k // 2 + 1) * 16, :].astype(f32)
        low = (k % 2) * 8
        return pair[:, low:low + 8].reshape(128, 128).astype(bf16)

    for tap in range(TAPS):
        part = block(tap)
        w2[:, tap * 128:(tap + 1) * 128] = part
        w2t[(8 - tap) * 128:(9 - tap) * 128, :] = part
    w1[:, :128] = block(9)
    w1[:, 128:] = block(10)
    w3[...] = block(11)
    r1[...] = block(12)
    wide = dot(w3[...], repeat[...]).astype(bf16)
    for tap in range(TAPS):
        w3r[tap * 128:(tap + 1) * 128, :] = wide[:, tap * 128:(tap + 1) * 128]
    w3f[...] = wide[:, 9 * 128:]
    wide = dot(block(13), repeat[:, :9 * 128]).astype(bf16)
    for tap in range(TAPS):
        r2[tap * 128:(tap + 1) * 128, :] = wide[:, tap * 128:(tap + 1) * 128]
    lane = lax.broadcasted_iota(jnp.int32, (16, 128), 1)
    pick_film = jnp.where(lane == FILM_LANE, 1.0, 0.0).astype(bf16)
    gain = 1.0 + noise_coef * dot(pick_film, w3[...], 1, 1)[0:1]

    def grid_mask(at, n):
        shape = (n, PLANES, SUB, 128)
        row = lax.broadcasted_iota(jnp.int32, shape, 0) + (at + first_row)
        col = (lax.broadcasted_iota(jnp.int32, shape, 2) * PLANES
               + lax.broadcasted_iota(jnp.int32, shape, 1) + first_col)
        return (row >= 0) & (row < NH) & (col >= 0) & (col < NW)

    def tile_mask(n):
        shape = (n, PLANES, SUB, 128)
        col = (lax.broadcasted_iota(jnp.int32, shape, 2) * PLANES
               + lax.broadcasted_iota(jnp.int32, shape, 1))
        return (col >= RIM) & (col < RIM + TW)

    def cells(value, n):
        return value.reshape(n, PLANES, SUB, 128)

    def flat(value):
        return value.reshape(-1, 128)

    def sweep(first, count, n, body):
        @pl.loop(0, count // n)
        def _(k):
            body(first + k * n, n)

    def reg_one(at, n):
        v = dot(flat(cond_taps[pl.ds(at - 2, n)]), r1[...], 1, 1)
        v = cells(v * sigmoid(v), n)
        put(hid, at, n, jnp.where(grid_mask(at, n), v, 0.0))

    sweep(2, 28, 7, reg_one)

    def reg_two(at, n):
        mean = cells(dot(stack_taps(hid, at, n), r2[...]), n).astype(bf16).astype(f32)
        rest = target9[pl.ds(at - 3, n)] - mean
        noised = rest + sigma * noise9[pl.ds(at - 3, n)]
        resid[pl.ds(at - 3, n)] = rest
        noisy[pl.ds(at - 3, n)] = noised
        put(inp, at, n, jnp.where(grid_mask(at, n), in_coef * noised, 0.0))

    sweep(3, 26, 13, reg_two)

    def conv_one(at, n):
        picked = pick_taps(inp, at, n)
        taps_in[pl.ds(at - 4, n)] = picked
        both = jnp.concatenate([flat(picked), flat(cond_taps[pl.ds(at - 2, n)])], axis=1)
        v = dot(both, w1[...], 1, 1)
        act[pl.ds(at - 4, n)] = cells(v, n)
        v = v * gain
        v = cells(v * sigmoid(v), n)
        put(one, at, n, jnp.where(grid_mask(at, n), v, 0.0))

    sweep(4, 24, 6, conv_one)

    def conv_two(at, n):
        v = dot(stack_taps(one, at, n), w2[...], 1, 1)
        s = sigmoid(v)
        slope[pl.ds(at - 5, n)] = cells(s * (1.0 + v * (1.0 - s)), n)
        put(two, at, n, jnp.where(grid_mask(at, n), cells(v * s, n), 0.0))

    sweep(5, 22, 11, conv_two)

    def conv_three(at, n):
        v = cells(dot(stack_taps(two, at, n), w3r[...]), n)
        value = skip * noisy[pl.ds(at - 3, n)] + out_coef * v
        den[pl.ds(at - 6, n)] = value.astype(bf16)
        delta = delta_coef * (value - resid[pl.ds(at - 3, n)])
        put(dlt, at, n, jnp.where(grid_mask(at, n), delta, 0.0))

    sweep(6, 20, 10, conv_three)

    def delta_two(at, n):
        picked = pick_taps(dlt, at, n)
        taps_d[pl.ds(at - 7, n)] = picked
        v = cells(dot(flat(picked), w3f[...], 1, 1), n) * slope[pl.ds(at - 5, n)]
        put(sdl, at, n, jnp.where(grid_mask(at, n), v, 0.0))

    sweep(7, 18, 6, delta_two)

    film_sum[...] = jnp.zeros((8, 128), f32)

    def delta_one(at, n):
        v = dot(stack_taps(sdl, at, n), w2t[...])
        a = flat(act[pl.ds(at - 4, n)])
        u = a * gain
        s = sigmoid(u)
        g = cells(v * (s * (1.0 + u * (1.0 - s))), n)
        g = flat(jnp.where(tile_mask(n), g, 0.0))
        film_sum[...] += jnp.sum((g * a).reshape(-1, 8, 128), axis=0)
        grad1[pl.ds(at - 8, n)] = cells(g * gain, n).astype(bf16)

    sweep(8, 16, 8, delta_one)

    inside = jnp.where(tile_mask(1), 1.0, 0.0).astype(bf16)
    own = slice(RIM, RIM + 16)
    d2 = flat(sdl[own, 1:PLANES + 1] * inside)
    g2 = dot(d2, stack_taps(one, RIM, 16), 0, 0)
    g1 = dot(flat(grad1[...]),
             jnp.concatenate([flat(taps_in[4:20]), flat(cond_taps[6:22])], axis=1), 0, 0)
    g3 = dot(flat(two[own, 1:PLANES + 1] * inside), flat(taps_d[1:17]), 0, 0)
    film = noise_coef * jnp.sum(film_sum[...], axis=0, keepdims=True)
    film = jnp.transpose(jnp.broadcast_to(film, (8, 128)))[:, 0:1]
    g3 = jnp.where(lax.broadcasted_iota(jnp.int32, (128, 128), 1) == FILM_LANE, film, g3)
    parts = [g2[:, k * 128:(k + 1) * 128] for k in range(9)] + [g1[:, :128], g1[:, 128:], g3]
    for p in range(6):
        pair = [part.reshape(16, 8, 128) for part in parts[2 * p:2 * p + 2]]
        out[:, p * 16:(p + 1) * 16, :] = jnp.concatenate(pair, axis=1).astype(bf16)

    fields = (lax.broadcasted_iota(jnp.int32, (16, 128), 0)
              == lax.broadcasted_iota(jnp.int32, (16, 128), 1)).astype(f32).astype(bf16)
    for i in range(16):
        turned = dot(fields, den[i + 2].reshape(WIN, 128), 1, 1).astype(bf16)
        den_rows[i * 16:(i + 1) * 16, :] = dot(turned, back[...])
    for c in range(6):
        left = den_rows[pl.ds(c, 16, stride=16), :]
        right = den_rows[pl.ds(c + 6, 16, stride=16), :]
        tile = jnp.where(lane < TW, left, right).astype(bf16)
        out[:, 96 + c * 16:96 + (c + 1) * 16, :] = jnp.broadcast_to(tile[None], (16, 16, 128))


def fold_kernel(parts, out):
    for p in range(6):
        total = jnp.sum(parts[:, p * 16:(p + 1) * 16, :].astype(f32), axis=0).astype(bf16)
        for q in range(8):
            out[q, p * 16:(p + 1) * 16, :] = total


def field_kernel(parts, out):
    for k in range(8):
        for c in range(6):
            a = parts[2 * k, 96 + c * 16:96 + (c + 1) * 16, :].astype(f32)
            b = parts[2 * k + 1, 96 + c * 16:96 + (c + 1) * 16, :].astype(f32)
            cols = slice(k * 128, (k + 1) * 128)
            out[c, :, cols] = jnp.concatenate([a[:, :TW], b[:, :TW]], axis=1).astype(bf16)
            out[c + 6, :, cols] = jnp.concatenate([a[:, TW:], b[:, TW:]], axis=1).astype(bf16)


def finish_kernel(parts, g1, g2, g3, film):
    def block(k):
        pair = jnp.sum(parts[:, (k // 2) * 16:(k // 2 + 1) * 16, :].astype(f32), axis=0)
        return pair[(k % 2) * 8:(k % 2) * 8 + 8]

    low, high, third = jnp.transpose(block(9)), jnp.transpose(block(10)), block(11)
    for a in range(3):
        for b in range(3):
            tap = 3 * a + b
            lanes = slice(tap * COUT, (tap + 1) * COUT)
            g2[a, b] = jnp.transpose(block(tap))
            g1[a, b, :COUT] = low[lanes]
            g1[a, b, COUT:] = high[lanes]
            g3[a, b] = third[:, (8 - tap) * COUT:(9 - tap) * COUT]
    film[...] = jnp.transpose(third)[FILM_LANE:FILM_LANE + 1]


VMEM = pl.BlockSpec(memory_space=pltpu.VMEM)
SMEM = pl.BlockSpec(memory_space=pltpu.SMEM)
ANY = pl.BlockSpec(memory_space=pl.ANY)


def kernel_call(body, ins, outs, scratch=(), limit=16, cost=None):
    return pl.pallas_call(
        body,
        in_specs=list(ins),
        out_specs=[VMEM] * len(outs),
        out_shape=[jax.ShapeDtypeStruct(shape, dtype) for shape, dtype in outs],
        scratch_shapes=list(scratch),
        compiler_params=pltpu.CompilerParams(vmem_limit_bytes=limit * MIB),
        cost_estimate=cost,
    )


def planes(rows, dtype, count=PLANES):
    return pltpu.VMEM((rows, count, SUB, 128), dtype)


def shards(condition, target, noise_draw, sigma_index, reg_first, reg_second, first_kernel,
           second_kernel, third_kernel, film_scale):
    sel_first, sel_low, order, back, spread, repeat = place_constants()
    own, last, leading, packed = kernel_call(
        pack_kernel, [ANY] * 3 + [VMEM] * 8,
        [((36, 16, 128), f32), ((36, 8, 128), f32), ((36, 8, 128), f32), ((16, 112, 128), bf16)],
        [pltpu.VMEM((3, COUT, 16, 256), f32), pltpu.SemaphoreType.DMA((3,))],
    )(condition, target, noise_draw, first_kernel, second_kernel, third_kernel, reg_first,
      reg_second, film_scale.reshape(1, 8), jnp.asarray(sel_first), jnp.asarray(sel_low))
    up = [(i, i + 1) for i in range(lax.axis_size("rows") - 1)]
    before = lax.ppermute(last, "rows", up)
    after = lax.ppermute(leading, "rows", [(j, i) for i, j in up])
    gathered = lax.all_to_all(packed, GROUP, 0, 0, tiled=True)
    cond_taps, target9, noise9 = kernel_call(
        prep_kernel, [ANY] * 3 + [VMEM] * 2,
        [((28, PLANES, SUB, 128), bf16), ((26, PLANES, SUB, 128), f32),
         ((26, PLANES, SUB, 128), f32)],
        [pltpu.VMEM((48, 32, 128), f32), planes(32, bf16, 7), pltpu.SemaphoreType.DMA((3,))],
        cost=pl.CostEstimate(flops=1 << 28, bytes_accessed=8 * MIB, transcendentals=0),
    )(own, before, after, jnp.asarray(order, bf16), jnp.asarray(spread, bf16))
    wide = [planes(32, bf16, 7) for _ in range(6)]
    out, = kernel_call(
        step_kernel, [SMEM] * 2 + [VMEM] * 6, [((16, 192, 128), bf16)],
        [pltpu.VMEM((128, 1152), bf16), pltpu.VMEM((1152, 128), bf16),
         pltpu.VMEM((128, 256), bf16), pltpu.VMEM((128, 128), bf16),
         pltpu.VMEM((128, 128), bf16), pltpu.VMEM((1152, 128), bf16),
         pltpu.VMEM((128, 128), bf16), pltpu.VMEM((1152, 128), bf16)]
        + wide
        + [planes(24, bf16), planes(18, bf16), planes(26, f32), planes(26, f32),
           planes(24, f32), planes(22, f32), planes(20, bf16), planes(16, bf16),
           pltpu.VMEM((8, 128), f32), pltpu.VMEM((256, 128), f32)],
        limit=48,
    )(sigma_index, jnp.asarray(coef_table()), cond_taps, target9, noise9, gathered,
      jnp.asarray(repeat, bf16), jnp.asarray(back, bf16))
    parts = lax.all_to_all(out, GROUP, 0, 0, tiled=True)
    folded, = kernel_call(fold_kernel, [VMEM], [((8, 96, 128), bf16)])(parts)
    denoised, = kernel_call(
        field_kernel, [VMEM], [((COUT, 16, NW), bf16)],
        cost=pl.CostEstimate(flops=1 << 26, bytes_accessed=2 * MIB, transcendentals=0),
    )(parts)
    sums = lax.all_to_all(folded, "rows", 0, 0, tiled=True)
    g1, g2, g3, film = kernel_call(
        finish_kernel, [VMEM],
        [((3, 3, 24, 8), f32), ((3, 3, 128, 8), f32), ((3, 3, 8, 12), f32), ((1, 8), f32)],
    )(sums)
    return denoised, g1, g2, g3, film.reshape(8)


def solution(mesh):
    return jax.shard_map(
        shards,
        mesh=mesh,
        in_specs=(
            P(None, "rows", None),
            P(None, "rows", None),
            P(None, "rows", None),
            P(),
            P(None, None, None, "chan"),
            P(None, None, "chan", None),
            P(None, None, None, GROUP),
            P(None, None, None, GROUP),
            P(None, None, GROUP, None),
            P(GROUP),
        ),
        out_specs=(
            P(None, "rows", None),
            P(None, None, None, GROUP),
            P(None, None, None, GROUP),
            P(None, None, GROUP, None),
            P(GROUP),
        ),
        check_vma=False,
    )
```

```python
import math

import numpy as np
import jax
import jax.numpy as jnp
from jax import lax
from jax.experimental import pallas as pl
from jax.experimental.pallas import tpu as pltpu
from jax.sharding import PartitionSpec as P

COUT = 12
NSIG = 32
NH = 128
NW = 1024
TW = 64
RIM = 8
PLANES = 5
SUB = 16
WIN = PLANES * SUB
TAPS = 9
FILM_LANE = 120
MIB = 1024 * 1024
GROUP = ("section", "chan")
f32 = jnp.float32
bf16 = jnp.bfloat16


def coef_table():
    i = np.arange(NSIG, dtype=np.float64)
    high, low = 4.0 ** (1 / 7), 0.25 ** (1 / 7)
    level = (high + i / (NSIG - 1) * (low - high)) ** 7
    total = level**2 + 0.25
    out_coef = 0.5 * level / np.sqrt(total)
    weight = total / (0.5 * level) ** 2
    table = np.zeros((NSIG, 8), np.float32)
    table[:, 0] = level
    table[:, 1] = 0.25 / total
    table[:, 2] = out_coef
    table[:, 3] = 1 / np.sqrt(total)
    table[:, 4] = np.log(8 * level) / 4
    table[:, 5] = 2 * weight * out_coef / math.sqrt(COUT * NH * NW)
    return table


def place_constants():
    order = np.zeros((WIN, 128), np.float32)
    back = np.zeros((WIN, 128), np.float32)
    for t in range(PLANES):
        for s in range(SUB):
            col = PLANES * s + t
            order[t * SUB + s, col] = 1
            if RIM <= col < RIM + TW:
                back[t * SUB + s, col - RIM] = 1
                back[t * SUB + s, TW + col - RIM] = 1
    spread = np.zeros((128, 384), np.float32)
    repeat = np.zeros((128, 10 * 128), np.float32)
    for c in range(COUT):
        for g in range(TAPS):
            spread[24 + c, g * COUT + c] = 1
            for first in (0, 48, 80):
                spread[first + c, 128 + g * COUT + c] = 1
                spread[first + COUT + c, 256 + g * COUT + c] = 1
            for tap in range(TAPS):
                repeat[tap * COUT + c, tap * 128 + g * COUT + c] = 1
            repeat[(8 - g) * COUT + c, 9 * 128 + g * COUT + c] = 1
    return order, back, spread, repeat


def dot(a, b, ca=1, cb=0):
    return lax.dot_general(a, b, (((ca,), (cb,)), ((), ())), preferred_element_type=f32)


def sigmoid(v):
    return 1.0 / (1.0 + jnp.exp(-v))


def member():
    return lax.axis_index("section") * lax.axis_size("chan") + lax.axis_index("chan")


def window_place():
    start = member() * TW - RIM
    base = jnp.clip((start + 128) // 128 * 128 - 128, 0, NW - 256)
    return start, pl.multiple_of(base, 128)


def window_copy(src, dst, sem):
    copy = pltpu.make_async_copy(src.at[:, :, pl.ds(window_place()[1], 256)], dst, sem)
    copy.start()
    return copy


def window(wide):
    start, base = window_place()
    rows = pltpu.roll(wide.reshape(COUT * 16, 256), lax.rem(512 - (start - base), 256), 1)
    rows = rows[:, :128]
    col = start + lax.broadcasted_iota(jnp.int32, rows.shape, 1)
    return jnp.where((col >= 0) & (col < NW), rows, 0.0).reshape(COUT, 16, 128)


def pack_kernel(cond, target, noise, w1_any, w2_any, w3_any, r1_any, r2_any, film_any,
                last, leading, packed, scr, w1, w2, w3, r1, r2, film, sems):
    small = []
    for k, (src, dst) in enumerate(((w2_any, w2), (w1_any, w1), (w3_any, w3), (r1_any, r1),
                                    (r2_any, r2), (film_any, film))):
        small.append(pltpu.make_async_copy(src, dst, sems.at[k]))
        small[-1].start()
    copies = [window_copy(src, scr.at[k], sems.at[6 + k])
              for k, src in enumerate((target, noise, cond))]
    half = lax.axis_index("section") == 0
    eye = (lax.broadcasted_iota(jnp.int32, (8, 8), 0)
           == lax.broadcasted_iota(jnp.int32, (8, 8), 1)).astype(f32)
    for k, copy in enumerate(copies):
        copy.wait()
        moved = window(scr[k])
        last[k * COUT:(k + 1) * COUT] = moved[:, 8:]
        leading[k * COUT:(k + 1) * COUT] = moved[:, :8]
    for copy in small:
        copy.wait()

    def place(n, at):
        lane = lax.broadcasted_iota(jnp.int32, (n, 128), 1)
        row = lax.broadcasted_iota(jnp.int32, (n, 128), 0)
        return jnp.where((lane - row == at) & (row < COUT), 1.0, 0.0)

    first_in = jnp.zeros((8, 128), f32)
    first_cond = jnp.zeros((8, 128), f32)
    third = jnp.zeros((8, 128), f32)
    reg_a = jnp.zeros((16, 128), f32)
    reg_b = jnp.zeros((16, 128), f32)
    blocks = []
    for a in range(3):
        for b in range(3):
            tap = 3 * a + b
            low = place(COUT, tap * COUT)
            lane = lax.broadcasted_iota(jnp.int32, (24, 128), 1)
            row = lax.broadcasted_iota(jnp.int32, (24, 128), 0)
            low_in = jnp.where((lane - row == tap * COUT) & (row < COUT), 1.0, 0.0)
            low_cond = jnp.where((lane - row == (tap - 1) * COUT) & (row >= COUT), 1.0, 0.0)
            blocks.append(w2[a, b].astype(f32))
            first_in += dot(w1[a, b].astype(f32), low_in)
            first_cond += dot(w1[a, b].astype(f32), low_cond)
            third += dot(w3[a, b].astype(f32), low)
            reg_a += dot(r1[a, b].astype(f32), low, 0, 0)
            reg_b += dot(r2[a, b].astype(f32), low)
    lane = lax.broadcasted_iota(jnp.int32, (8, 128), 1)
    film_col = jnp.sum(eye * film[...].astype(f32), axis=1, keepdims=True)
    third = jnp.where(lane == FILM_LANE, film_col, third)
    blocks += [first_in, first_cond, third,
               jnp.where(half, reg_a[:8], reg_a[8:]), jnp.where(half, reg_b[:8], reg_b[8:])]
    for p in range(7):
        pair = jnp.concatenate(blocks[2 * p:2 * p + 2], axis=0).astype(bf16)
        for q in range(16):
            packed[q, p * 16:(p + 1) * 16, :] = pair


def put(ref, at, n, value):
    ref[pl.ds(at, n), 1:PLANES + 1] = value.astype(bf16)
    ref[pl.ds(at, n), 0] = pltpu.roll(value[:, PLANES - 1], 1, 1).astype(bf16)
    ref[pl.ds(at, n), PLANES + 1] = pltpu.roll(value[:, 0], SUB - 1, 1).astype(bf16)


def stack_taps(ref, at, n):
    parts = []
    for a in range(3):
        for b in range(3):
            parts.append(ref[pl.ds(at + a - 1, n), b:b + PLANES].reshape(n * WIN, 128))
    return jnp.concatenate(parts, axis=1)


def pick_taps(ref, at, n):
    lane = lax.broadcasted_iota(jnp.int32, (SUB, 128), 1)
    total = None
    for a in range(3):
        for b in range(3):
            low = (3 * a + b) * COUT
            mask = jnp.where((lane >= low) & (lane < low + COUT), 1.0, 0.0).astype(bf16)
            part = ref[pl.ds(at + a - 1, n), b:b + PLANES] * mask[None, None]
            total = part if total is None else total + part
    return total


def prep_kernel(cond, target, noise, before, after, order_any, spread_any,
                cond_taps, target9, noise9, scr, wide, cond9, order, spread, sems):
    copies = [window_copy(src, wide.at[k], sems.at[k])
              for k, src in enumerate((target, noise, cond))]
    others = [
        pltpu.make_async_copy(before, scr.at[0:36, 0:8, :], sems.at[3]),
        pltpu.make_async_copy(after, scr.at[0:36, 24:32, :], sems.at[4]),
        pltpu.make_async_copy(order_any, order, sems.at[5]),
        pltpu.make_async_copy(spread_any, spread, sems.at[6]),
    ]
    for copy in others:
        copy.start()
    scr[36:48] = jnp.zeros((12, 32, 128), f32)
    for k, copy in enumerate(copies):
        copy.wait()
        scr[k * COUT:(k + 1) * COUT, 8:24] = window(wide[k])
    for copy in others:
        copy.wait()
    flat = scr.reshape(48 * 32, 128)

    def row(i):
        x = flat[pl.ds(i, 48, stride=32), :]
        high = x.astype(bf16)
        rest = x[:32] - high[:32].astype(f32)
        mid = rest.astype(bf16)
        low = (rest - mid.astype(f32)).astype(bf16)
        rows = jnp.concatenate([high, mid, low, jnp.zeros((16, 128), bf16)], axis=0)
        cells = dot(order[...], rows, 1, 1).astype(bf16)
        wide = dot(cells, spread[...]).reshape(1, PLANES, SUB, 384)
        put(cond9, i, 1, wide[..., :128])
        return wide

    for i in range(1, 31):
        wide = row(i)
        if 3 <= i < 29:
            target9[i - 3:i - 2] = wide[..., 128:256]
            noise9[i - 3:i - 2] = wide[..., 256:]

    @pl.loop(0, 7)
    def _(k):
        at = 2 + 4 * k
        cond_taps[pl.ds(at - 2, 4)] = pick_taps(cond9, at, 4)


def step_kernel(index, table, cond_any, target_any, noise_any, gathered_any, repeat_any, back_any,
                out, cond_taps, target9, noise9, gathered, repeat, back, sems, w2, w2t, w1, w3, w3f, w3r, r1, r2,
                hid, inp, one, two, dlt, sdl, taps_in, taps_d, resid, noisy, act, slope,
                den, grad1, film_sum, den_rows):
    copies = []
    for k, (src, dst) in enumerate(((gathered_any, gathered), (repeat_any, repeat),
                                    (cond_any, cond_taps), (target_any, target9),
                                    (noise_any, noise9), (back_any, back))):
        copies.append(pltpu.make_async_copy(src, dst, sems.at[k]))
        copies[-1].start()
    level = index[0]
    sigma, skip, out_coef = table[level, 0], table[level, 1], table[level, 2]
    in_coef, noise_coef, delta_coef = table[level, 3], table[level, 4], table[level, 5]
    first_row = lax.axis_index("rows") * 16 - RIM
    first_col = member() * TW - RIM

    def block(k):
        pair = gathered[:, (k // 2) * 16:(k // 2 + 1) * 16, :].astype(f32)
        low = (k % 2) * 8
        return pair[:, low:low + 8].reshape(128, 128).astype(bf16)

    copies[0].wait()
    for tap in range(TAPS):
        part = block(tap)
        w2[:, tap * 128:(tap + 1) * 128] = part
        w2t[(8 - tap) * 128:(9 - tap) * 128, :] = part
    w1[:, :128] = block(9)
    w1[:, 128:] = block(10)
    w3[...] = block(11)
    r1[...] = block(12)
    copies[1].wait()
    wide = dot(w3[...], repeat[...]).astype(bf16)
    for tap in range(TAPS):
        w3r[tap * 128:(tap + 1) * 128, :] = wide[:, tap * 128:(tap + 1) * 128]
    w3f[...] = wide[:, 9 * 128:]
    wide = dot(block(13), repeat[:, :9 * 128]).astype(bf16)
    for tap in range(TAPS):
        r2[tap * 128:(tap + 1) * 128, :] = wide[:, tap * 128:(tap + 1) * 128]
    lane = lax.broadcasted_iota(jnp.int32, (16, 128), 1)
    pick_film = jnp.where(lane == FILM_LANE, 1.0, 0.0).astype(bf16)
    gain = 1.0 + noise_coef * dot(pick_film, w3[...], 1, 1)[0:1]

    def grid_mask(at, n):
        shape = (n, PLANES, SUB, 128)
        row = lax.broadcasted_iota(jnp.int32, shape, 0) + (at + first_row)
        col = (lax.broadcasted_iota(jnp.int32, shape, 2) * PLANES
               + lax.broadcasted_iota(jnp.int32, shape, 1) + first_col)
        return (row >= 0) & (row < NH) & (col >= 0) & (col < NW)

    def tile_mask(n):
        shape = (n, PLANES, SUB, 128)
        col = (lax.broadcasted_iota(jnp.int32, shape, 2) * PLANES
               + lax.broadcasted_iota(jnp.int32, shape, 1))
        return (col >= RIM) & (col < RIM + TW)

    def cells(value, n):
        return value.reshape(n, PLANES, SUB, 128)

    def flat(value):
        return value.reshape(-1, 128)

    def sweep(first, count, n, body):
        @pl.loop(0, count // n)
        def _(k):
            body(first + k * n, n)

    def reg_one(at, n):
        v = dot(flat(cond_taps[pl.ds(at - 2, n)]), r1[...], 1, 1)
        v = cells(v * sigmoid(v), n)
        put(hid, at, n, jnp.where(grid_mask(at, n), v, 0.0))

    copies[2].wait()
    sweep(2, 28, 7, reg_one)

    def reg_two(at, n):
        mean = cells(dot(stack_taps(hid, at, n), r2[...]), n).astype(bf16).astype(f32)
        rest = target9[pl.ds(at - 3, n)] - mean
        noised = rest + sigma * noise9[pl.ds(at - 3, n)]
        resid[pl.ds(at - 3, n)] = rest
        noisy[pl.ds(at - 3, n)] = noised
        put(inp, at, n, jnp.where(grid_mask(at, n), in_coef * noised, 0.0))

    for copy in copies[3:]:
        copy.wait()
    sweep(3, 26, 13, reg_two)

    def conv_one(at, n):
        picked = pick_taps(inp, at, n)
        taps_in[pl.ds(at - 4, n)] = picked
        both = jnp.concatenate([flat(picked), flat(cond_taps[pl.ds(at - 2, n)])], axis=1)
        v = dot(both, w1[...], 1, 1)
        act[pl.ds(at - 4, n)] = cells(v, n)
        v = v * gain
        v = cells(v * sigmoid(v), n)
        put(one, at, n, jnp.where(grid_mask(at, n), v, 0.0))

    sweep(4, 24, 6, conv_one)

    def conv_two(at, n):
        v = dot(stack_taps(one, at, n), w2[...], 1, 1)
        s = sigmoid(v)
        slope[pl.ds(at - 5, n)] = cells(s * (1.0 + v * (1.0 - s)), n)
        put(two, at, n, jnp.where(grid_mask(at, n), cells(v * s, n), 0.0))

    sweep(5, 22, 11, conv_two)

    def conv_three(at, n):
        v = cells(dot(stack_taps(two, at, n), w3r[...]), n)
        value = skip * noisy[pl.ds(at - 3, n)] + out_coef * v
        den[pl.ds(at - 6, n)] = value.astype(bf16)
        delta = delta_coef * (value - resid[pl.ds(at - 3, n)])
        put(dlt, at, n, jnp.where(grid_mask(at, n), delta, 0.0))

    sweep(6, 20, 10, conv_three)

    def delta_two(at, n):
        picked = pick_taps(dlt, at, n)
        taps_d[pl.ds(at - 7, n)] = picked
        v = cells(dot(flat(picked), w3f[...], 1, 1), n) * slope[pl.ds(at - 5, n)]
        put(sdl, at, n, jnp.where(grid_mask(at, n), v, 0.0))

    sweep(7, 18, 6, delta_two)

    film_sum[...] = jnp.zeros((8, 128), f32)

    def delta_one(at, n):
        v = dot(stack_taps(sdl, at, n), w2t[...])
        a = flat(act[pl.ds(at - 4, n)])
        u = a * gain
        s = sigmoid(u)
        g = cells(v * (s * (1.0 + u * (1.0 - s))), n)
        g = flat(jnp.where(tile_mask(n), g, 0.0))
        film_sum[...] += jnp.sum((g * a).reshape(-1, 8, 128), axis=0)
        grad1[pl.ds(at - 8, n)] = cells(g * gain, n).astype(bf16)

    sweep(8, 16, 8, delta_one)

    inside = jnp.where(tile_mask(1), 1.0, 0.0).astype(bf16)
    own = slice(RIM, RIM + 16)
    d2 = flat(sdl[own, 1:PLANES + 1] * inside)
    g2 = dot(d2, stack_taps(one, RIM, 16), 0, 0)
    g1 = dot(flat(grad1[...]),
             jnp.concatenate([flat(taps_in[4:20]), flat(cond_taps[6:22])], axis=1), 0, 0)
    g3 = dot(flat(two[own, 1:PLANES + 1] * inside), flat(taps_d[1:17]), 0, 0)
    film = noise_coef * jnp.sum(film_sum[...], axis=0, keepdims=True)
    film = jnp.transpose(jnp.broadcast_to(film, (8, 128)))[:, 0:1]
    g3 = jnp.where(lax.broadcasted_iota(jnp.int32, (128, 128), 1) == FILM_LANE, film, g3)
    parts = [g2[:, k * 128:(k + 1) * 128] for k in range(9)] + [g1[:, :128], g1[:, 128:], g3]
    for p in range(6):
        pair = [part.reshape(16, 8, 128) for part in parts[2 * p:2 * p + 2]]
        out[:, p * 16:(p + 1) * 16, :] = jnp.concatenate(pair, axis=1).astype(bf16)

    fields = (lax.broadcasted_iota(jnp.int32, (16, 128), 0)
              == lax.broadcasted_iota(jnp.int32, (16, 128), 1)).astype(f32).astype(bf16)
    for i in range(16):
        turned = dot(fields, den[i + 2].reshape(WIN, 128), 1, 1).astype(bf16)
        den_rows[i * 16:(i + 1) * 16, :] = dot(turned, back[...])
    for c in range(6):
        left = den_rows[pl.ds(c, 16, stride=16), :]
        right = den_rows[pl.ds(c + 6, 16, stride=16), :]
        tile = jnp.where(lane < TW, left, right).astype(bf16)
        out[:, 96 + c * 16:96 + (c + 1) * 16, :] = jnp.broadcast_to(tile[None], (16, 16, 128))


def fold_kernel(parts, out):
    for p in range(6):
        total = jnp.sum(parts[:, p * 16:(p + 1) * 16, :].astype(f32), axis=0).astype(bf16)
        for q in range(8):
            out[q, p * 16:(p + 1) * 16, :] = total


def field_kernel(parts, out):
    for k in range(8):
        for c in range(6):
            a = parts[2 * k, 96 + c * 16:96 + (c + 1) * 16, :].astype(f32)
            b = parts[2 * k + 1, 96 + c * 16:96 + (c + 1) * 16, :].astype(f32)
            cols = slice(k * 128, (k + 1) * 128)
            out[c, :, cols] = jnp.concatenate([a[:, :TW], b[:, :TW]], axis=1).astype(bf16)
            out[c + 6, :, cols] = jnp.concatenate([a[:, TW:], b[:, TW:]], axis=1).astype(bf16)


def finish_kernel(parts, g1, g2, g3, film):
    def block(k):
        pair = jnp.sum(parts[:, (k // 2) * 16:(k // 2 + 1) * 16, :].astype(f32), axis=0)
        return pair[(k % 2) * 8:(k % 2) * 8 + 8]

    low, high, third = block(9), block(10), block(11)
    for a in range(3):
        for b in range(3):
            tap = 3 * a + b
            lanes = slice(tap * COUT, (tap + 1) * COUT)
            g2[a, b] = block(tap)
            g1[a, b, :, :COUT] = low[:, lanes]
            g1[a, b, :, COUT:] = high[:, lanes]
            g3[a, b] = third[:, (8 - tap) * COUT:(9 - tap) * COUT]
    film[...] = jnp.transpose(third)[FILM_LANE:FILM_LANE + 1]


VMEM = pl.BlockSpec(memory_space=pltpu.VMEM)
SMEM = pl.BlockSpec(memory_space=pltpu.SMEM)
ANY = pl.BlockSpec(memory_space=pl.ANY)


def kernel_call(body, ins, outs, scratch=(), limit=16, cost=None):
    return pl.pallas_call(
        body,
        in_specs=list(ins),
        out_specs=[VMEM] * len(outs),
        out_shape=[jax.ShapeDtypeStruct(shape, dtype) for shape, dtype in outs],
        scratch_shapes=list(scratch),
        compiler_params=pltpu.CompilerParams(vmem_limit_bytes=limit * MIB),
        cost_estimate=cost,
    )


def planes(rows, dtype, count=PLANES):
    return pltpu.VMEM((rows, count, SUB, 128), dtype)


def shards(condition, target, noise_draw, sigma_index, reg_first, reg_second, first_kernel,
           second_kernel, third_kernel, film_scale):
    order, back, spread, repeat = place_constants()
    last, leading, packed = kernel_call(
        pack_kernel, [ANY] * 9,
        [((36, 8, 128), f32), ((36, 8, 128), f32), ((16, 112, 128), bf16)],
        [pltpu.VMEM((3, COUT, 16, 256), f32), pltpu.VMEM((3, 3, 8, 24), bf16),
         pltpu.VMEM((3, 3, 8, 128), bf16), pltpu.VMEM((3, 3, 8, 12), bf16),
         pltpu.VMEM((3, 3, 12, 16), bf16), pltpu.VMEM((3, 3, 16, 12), bf16),
         pltpu.VMEM((1, 8), bf16), pltpu.SemaphoreType.DMA((9,))],
        limit=60,
    )(condition, target, noise_draw, jnp.swapaxes(first_kernel, 2, 3),
      jnp.swapaxes(second_kernel, 2, 3), third_kernel, reg_first, reg_second,
      film_scale.reshape(1, 8))
    up = [(i, i + 1) for i in range(lax.axis_size("rows") - 1)]
    before = lax.ppermute(last, "rows", up)
    after = lax.ppermute(leading, "rows", [(j, i) for i, j in up])
    gathered = lax.all_to_all(packed, GROUP, 0, 0, tiled=True)
    cond_taps, target9, noise9 = kernel_call(
        prep_kernel, [ANY] * 7,
        [((28, PLANES, SUB, 128), bf16), ((26, PLANES, SUB, 128), f32),
         ((26, PLANES, SUB, 128), f32)],
        [pltpu.VMEM((48, 32, 128), f32), pltpu.VMEM((3, COUT, 16, 256), f32),
         planes(32, bf16, 7), pltpu.VMEM((WIN, 128), bf16), pltpu.VMEM((128, 384), bf16),
         pltpu.SemaphoreType.DMA((7,))],
        limit=60,
        cost=pl.CostEstimate(flops=1 << 32, bytes_accessed=8 * MIB, transcendentals=0),
    )(condition, target, noise_draw, before, after, jnp.asarray(order, bf16), jnp.asarray(spread, bf16))
    wide = [planes(32, bf16, 7) for _ in range(6)]
    out, = kernel_call(
        step_kernel, [SMEM] * 2 + [ANY] * 6, [((16, 192, 128), bf16)],
        [planes(28, bf16), planes(26, f32), planes(26, f32), pltpu.VMEM((16, 112, 128), bf16),
         pltpu.VMEM((128, 1280), bf16), pltpu.VMEM((WIN, 128), bf16),
         pltpu.SemaphoreType.DMA((6,)), pltpu.VMEM((128, 1152), bf16), pltpu.VMEM((1152, 128), bf16),
         pltpu.VMEM((128, 256), bf16), pltpu.VMEM((128, 128), bf16),
         pltpu.VMEM((128, 128), bf16), pltpu.VMEM((1152, 128), bf16),
         pltpu.VMEM((128, 128), bf16), pltpu.VMEM((1152, 128), bf16)]
        + wide
        + [planes(24, bf16), planes(18, bf16), planes(26, f32), planes(26, f32),
           planes(24, f32), planes(22, f32), planes(20, bf16), planes(16, bf16),
           pltpu.VMEM((8, 128), f32), pltpu.VMEM((256, 128), f32)],
        limit=60,
    )(sigma_index, jnp.asarray(coef_table()), cond_taps, target9, noise9, gathered,
      jnp.asarray(repeat, bf16), jnp.asarray(back, bf16))
    parts = lax.all_to_all(out, GROUP, 0, 0, tiled=True)
    folded, = kernel_call(fold_kernel, [VMEM], [((8, 96, 128), bf16)])(parts)
    denoised, = kernel_call(
        field_kernel, [VMEM], [((COUT, 16, NW), bf16)],
        cost=pl.CostEstimate(flops=1 << 26, bytes_accessed=2 * MIB, transcendentals=0),
    )(parts)
    sums = lax.all_to_all(folded, "rows", 0, 0, tiled=True)
    g1, g2, g3, film = kernel_call(
        finish_kernel, [VMEM],
        [((3, 3, 8, 24), f32), ((3, 3, 8, 128), f32), ((3, 3, 8, 12), f32), ((1, 8), f32)],
    )(sums)
    return denoised, jnp.swapaxes(g1, 2, 3), jnp.swapaxes(g2, 2, 3), g3, film.reshape(8)


def solution(mesh):
    return jax.shard_map(
        shards,
        mesh=mesh,
        in_specs=(
            P(None, "rows", None),
            P(None, "rows", None),
            P(None, "rows", None),
            P(),
            P(None, None, None, "chan"),
            P(None, None, "chan", None),
            P(None, None, None, GROUP),
            P(None, None, None, GROUP),
            P(None, None, GROUP, None),
            P(GROUP),
        ),
        out_specs=(
            P(None, "rows", None),
            P(None, None, None, GROUP),
            P(None, None, None, GROUP),
            P(None, None, GROUP, None),
            P(GROUP),
        ),
        check_vma=False,
    )
```

```python
import math

import numpy as np
import jax
import jax.numpy as jnp
from jax import lax
from jax.experimental import pallas as pl
from jax.experimental.pallas import tpu as pltpu
from jax.sharding import PartitionSpec as P

COUT = 12
NSIG = 32
NH = 128
NW = 1024
TW = 64
RIM = 8
PLANES = 5
SUB = 16
WIN = PLANES * SUB
TAPS = 9
FILM_LANE = 120
MIB = 1024 * 1024
GROUP = ("section", "chan")
f32 = jnp.float32
bf16 = jnp.bfloat16


def coef_table():
    i = np.arange(NSIG, dtype=np.float64)
    high, low = 4.0 ** (1 / 7), 0.25 ** (1 / 7)
    level = (high + i / (NSIG - 1) * (low - high)) ** 7
    total = level**2 + 0.25
    out_coef = 0.5 * level / np.sqrt(total)
    weight = total / (0.5 * level) ** 2
    table = np.zeros((NSIG, 8), np.float32)
    table[:, 0] = level
    table[:, 1] = 0.25 / total
    table[:, 2] = out_coef
    table[:, 3] = 1 / np.sqrt(total)
    table[:, 4] = np.log(8 * level) / 4
    table[:, 5] = 2 * weight * out_coef / math.sqrt(COUT * NH * NW)
    return table


def place_constants():
    order = np.zeros((WIN, 128), np.float32)
    back = np.zeros((128, 128), np.float32)
    for t in range(PLANES):
        for s in range(SUB):
            col = PLANES * s + t
            order[t * SUB + s, col] = 1
            if RIM <= col < RIM + TW:
                back[t * SUB + s, col - RIM] = 1
                back[t * SUB + s, TW + col - RIM] = 1
    spread = np.zeros((128, 384), np.float32)
    repeat = np.zeros((128, 10 * 128), np.float32)
    for c in range(COUT):
        for g in range(TAPS):
            spread[24 + c, g * COUT + c] = 1
            for first in (0, 48, 80):
                spread[first + c, 128 + g * COUT + c] = 1
                spread[first + COUT + c, 256 + g * COUT + c] = 1
            for tap in range(TAPS):
                repeat[tap * COUT + c, tap * 128 + g * COUT + c] = 1
            repeat[(8 - g) * COUT + c, 9 * 128 + g * COUT + c] = 1
    return order, back, spread, repeat


def dot(a, b, ca=1, cb=0):
    return lax.dot_general(a, b, (((ca,), (cb,)), ((), ())), preferred_element_type=f32)


def sigmoid(v):
    return 0.5 * jnp.tanh(0.5 * v) + 0.5


def member():
    return lax.axis_index("section") * lax.axis_size("chan") + lax.axis_index("chan")


def window_place():
    start = member() * TW - RIM
    base = jnp.clip((start + 128) // 128 * 128 - 128, 0, NW - 256)
    return start, pl.multiple_of(base, 128)


def window_copy(src, dst, sem):
    copy = pltpu.make_async_copy(src.at[:, :, pl.ds(window_place()[1], 256)], dst, sem)
    copy.start()
    return copy


def window(wide):
    start, base = window_place()
    rows = pltpu.roll(wide.reshape(COUT * 16, 256), lax.rem(512 - (start - base), 256), 1)
    rows = rows[:, :128]
    col = start + lax.broadcasted_iota(jnp.int32, rows.shape, 1)
    return jnp.where((col >= 0) & (col < NW), rows, 0.0).reshape(COUT, 16, 128)


def pack_kernel(cond, target, noise, w1_any, w2_any, w3_any, r1_any, r2_any, film_any,
                last, leading, packed, scr, w1, w2, w3, r1, r2, film, sems):
    small = []
    for k, (src, dst) in enumerate(((w2_any, w2), (w1_any, w1), (w3_any, w3), (r1_any, r1),
                                    (r2_any, r2), (film_any, film))):
        small.append(pltpu.make_async_copy(src, dst, sems.at[k]))
        small[-1].start()
    copies = [window_copy(src, scr.at[k], sems.at[6 + k])
              for k, src in enumerate((target, noise, cond))]
    half = lax.axis_index("section") == 0
    eye = (lax.broadcasted_iota(jnp.int32, (8, 8), 0)
           == lax.broadcasted_iota(jnp.int32, (8, 8), 1)).astype(f32)
    for k, copy in enumerate(copies):
        copy.wait()
        moved = window(scr[k])
        last[k * COUT:(k + 1) * COUT] = moved[:, 8:]
        leading[k * COUT:(k + 1) * COUT] = moved[:, :8]
    for copy in small:
        copy.wait()

    def place(n, at):
        lane = lax.broadcasted_iota(jnp.int32, (n, 128), 1)
        row = lax.broadcasted_iota(jnp.int32, (n, 128), 0)
        return jnp.where((lane - row == at) & (row < COUT), 1.0, 0.0)

    first_in = jnp.zeros((8, 128), f32)
    first_cond = jnp.zeros((8, 128), f32)
    third = jnp.zeros((8, 128), f32)
    reg_a = jnp.zeros((16, 128), f32)
    reg_b = jnp.zeros((16, 128), f32)
    blocks = []
    for a in range(3):
        for b in range(3):
            tap = 3 * a + b
            low = place(COUT, tap * COUT)
            lane = lax.broadcasted_iota(jnp.int32, (24, 128), 1)
            row = lax.broadcasted_iota(jnp.int32, (24, 128), 0)
            low_in = jnp.where((lane - row == tap * COUT) & (row < COUT), 1.0, 0.0)
            low_cond = jnp.where((lane - row == (tap - 1) * COUT) & (row >= COUT), 1.0, 0.0)
            blocks.append(w2[a, b].astype(f32))
            first_in += dot(w1[a, b].astype(f32), low_in)
            first_cond += dot(w1[a, b].astype(f32), low_cond)
            third += dot(w3[a, b].astype(f32), low)
            reg_a += dot(r1[a, b].astype(f32), low, 0, 0)
            reg_b += dot(r2[a, b].astype(f32), low)
    lane = lax.broadcasted_iota(jnp.int32, (8, 128), 1)
    film_col = jnp.sum(eye * film[...].astype(f32), axis=1, keepdims=True)
    third = jnp.where(lane == FILM_LANE, film_col, third)
    blocks += [first_in, first_cond, third,
               jnp.where(half, reg_a[:8], reg_a[8:]), jnp.where(half, reg_b[:8], reg_b[8:])]
    for p in range(7):
        pair = jnp.concatenate(blocks[2 * p:2 * p + 2], axis=0).astype(bf16)
        for q in range(16):
            packed[q, p * 16:(p + 1) * 16, :] = pair


def put(ref, at, n, value):
    ref[pl.ds(at, n), 1:PLANES + 1] = value.astype(bf16)
    ref[pl.ds(at, n), 0] = pltpu.roll(value[:, PLANES - 1], 1, 1).astype(bf16)
    ref[pl.ds(at, n), PLANES + 1] = pltpu.roll(value[:, 0], SUB - 1, 1).astype(bf16)


def pick_taps(ref, at, n):
    lane = lax.broadcasted_iota(jnp.int32, (SUB, 128), 1)
    total = None
    for a in range(3):
        for b in range(3):
            low = (3 * a + b) * COUT
            mask = jnp.where((lane >= low) & (lane < low + COUT), 1.0, 0.0).astype(bf16)
            part = ref[pl.ds(at + a - 1, n), b:b + PLANES] * mask[None, None]
            total = part if total is None else total + part
    return total


def prep_kernel(cond, target, noise, before, after, order_any, spread_any,
                cond_taps, target9, noise9, scr, wide, cond9, order, spread, sems):
    copies = [window_copy(src, wide.at[k], sems.at[k])
              for k, src in enumerate((target, noise, cond))]
    others = [
        pltpu.make_async_copy(before, scr.at[0:36, 0:8, :], sems.at[3]),
        pltpu.make_async_copy(after, scr.at[0:36, 24:32, :], sems.at[4]),
        pltpu.make_async_copy(order_any, order, sems.at[5]),
        pltpu.make_async_copy(spread_any, spread, sems.at[6]),
    ]
    for copy in others:
        copy.start()
    scr[36:48] = jnp.zeros((12, 32, 128), f32)
    for k, copy in enumerate(copies):
        copy.wait()
        scr[k * COUT:(k + 1) * COUT, 8:24] = window(wide[k])
    for copy in others:
        copy.wait()
    flat = scr.reshape(48 * 32, 128)

    def row(i):
        x = flat[pl.ds(i, 48, stride=32), :]
        high = x.astype(bf16)
        rest = x[:32] - high[:32].astype(f32)
        mid = rest.astype(bf16)
        low = (rest - mid.astype(f32)).astype(bf16)
        rows = jnp.concatenate([high, mid, low, jnp.zeros((16, 128), bf16)], axis=0)
        cells = dot(order[...], rows, 1, 1).astype(bf16)
        wide = dot(cells, spread[...]).reshape(1, PLANES, SUB, 384)
        put(cond9, i, 1, wide[..., :128])
        return wide

    for i in range(1, 31):
        wide = row(i)
        if 3 <= i < 29:
            target9[(i - 3) // 2, (i - 3) % 2] = wide[0, ..., 128:256]
            noise9[(i - 3) // 2, (i - 3) % 2] = wide[0, ..., 256:]

    @pl.loop(0, 7)
    def _(k):
        at = 2 + 4 * k
        cond_taps[pl.ds(2 * k, 2)] = pick_taps(cond9, at, 4).reshape(2, 2, PLANES, SUB, 128)


def some(ref, row, k, n, base=0):
    return ref.at[pl.ds((row - base) // 2 + n * k, n), (row - base) % 2]


def put_pair(ref, row, k, n, value):
    dst = some(ref, row, k, n)
    dst[:, 1:PLANES + 1] = value.astype(bf16)
    dst[:, 0] = pltpu.roll(value[:, PLANES - 1], 1, 1).astype(bf16)
    dst[:, PLANES + 1] = pltpu.roll(value[:, 0], SUB - 1, 1).astype(bf16)


def stack_rows(ref, row, k, n):
    parts = []
    for u in range(4):
        src = some(ref, row + u - 1, k, n)
        for b in range(3):
            parts.append(src[:, b:b + PLANES].reshape(n * WIN, 128))
    return jnp.concatenate(parts, axis=1)


def pick_pair(ref, row, k, n):
    lane = lax.broadcasted_iota(jnp.int32, (SUB, 128), 1)
    total = None
    for a in range(3):
        src = some(ref, row + a - 1, k, n)
        for b in range(3):
            low = (3 * a + b) * COUT
            mask = jnp.where((lane >= low) & (lane < low + COUT), 1.0, 0.0).astype(bf16)
            part = src[:, b:b + PLANES] * mask[None, None]
            total = part if total is None else total + part
    return total


def step_kernel(index, table, cond_any, target_any, noise_any, gathered_any, repeat_any, back_any,
                out, cond_taps, target9, noise9, gathered, repeat, back, sems,
                w2, w2t, w1, w3, w3f, w3r, r1, r2,
                hid, inp, one, two, dlt, sdl, taps_in, taps_d, resid, noisy, act, slope,
                den, grad1, film_sum, den_rows, inside):
    copies = []
    for k, (src, dst) in enumerate(((gathered_any, gathered), (repeat_any, repeat),
                                    (cond_any, cond_taps), (target_any, target9),
                                    (noise_any, noise9), (back_any, back))):
        copies.append(pltpu.make_async_copy(src, dst, sems.at[k]))
        copies[-1].start()
    level = index[0]
    sigma, skip, out_coef = table[level, 0], table[level, 1], table[level, 2]
    in_coef, noise_coef, delta_coef = table[level, 3], table[level, 4], table[level, 5]
    first_row = lax.axis_index("rows") * 16 - RIM
    first_col = member() * TW - RIM
    for ref in (w2, w2t, w3r, r2):
        ref[...] = jnp.zeros(ref.shape, bf16)
    for ref in (r1, w3f):
        ref[...] = jnp.zeros(ref.shape, bf16)
    den[:, :, PLANES:] = jnp.zeros((10, 2, 8 - PLANES, SUB, 128), bf16)
    shape = (PLANES, SUB, 128)
    col = (lax.broadcasted_iota(jnp.int32, shape, 1) * PLANES
           + lax.broadcasted_iota(jnp.int32, shape, 0))
    inside[...] = jnp.where((col + first_col >= 0) & (col + first_col < NW), 1.0, 0.0)
    tile = jnp.where((col >= RIM) & (col < RIM + TW), 1.0, 0.0)

    def block(k):
        pair = gathered[:, (k // 2) * 16:(k // 2 + 1) * 16, :].astype(f32)
        low = (k % 2) * 8
        return pair[:, low:low + 8].reshape(128, 128).astype(bf16)

    def spot(tap, v):
        a, b = tap // 3, tap % 3
        at = (3 * (a + v) + b) * 128
        return slice(at, at + 128)

    halves = (slice(0, 128), slice(128, 256))
    copies[0].wait()
    for v in range(2):
        r1[halves[v], halves[v]] = block(12)
    w3[...] = block(11)
    copies[1].wait()
    wide = dot(block(13), repeat[:, :9 * 128]).astype(bf16)
    for tap in range(TAPS):
        for v in range(2):
            r2[spot(tap, v), halves[v]] = wide[:, tap * 128:(tap + 1) * 128]
    w1[:, :128] = block(9)
    w1[:, 128:] = block(10)
    for tap in range(TAPS):
        part = block(tap)
        for v in range(2):
            w2[halves[v], spot(tap, v)] = part
            w2t[spot(8 - tap, v), halves[v]] = part
    wide = dot(w3[...], repeat[...]).astype(bf16)
    for tap in range(TAPS):
        for v in range(2):
            w3r[spot(tap, v), halves[v]] = wide[:, tap * 128:(tap + 1) * 128]
    for v in range(2):
        w3f[halves[v], halves[v]] = wide[:, 9 * 128:]
    lane = lax.broadcasted_iota(jnp.int32, (16, 128), 1)
    pick_film = jnp.where(lane == FILM_LANE, 1.0, 0.0).astype(bf16)
    gain = 1.0 + noise_coef * dot(pick_film, w3[...], 1, 1)[0:1]

    def cells(value):
        return value.reshape(-1, PLANES, SUB, 128)

    def flat(value):
        return value.reshape(-1, 128)

    def sweep(count, n, body):
        @pl.loop(0, count // n)
        def _(k):
            body(k, n)

    def clear(ref):
        @pl.when(first_row < 0)
        def _():
            ref[0:4] = jnp.zeros((4, 2, PLANES + 2, SUB, 128), bf16)

        @pl.when(first_row + 32 > NH)
        def _():
            ref[12:16] = jnp.zeros((4, 2, PLANES + 2, SUB, 128), bf16)

    def reg_one(k, n):
        both = jnp.concatenate([flat(some(cond_taps, 2 + v, k, n, 2)[...]) for v in range(2)], 1)
        value = dot(both, r1[...], 1, 1)
        for v in range(2):
            x = value[:, halves[v]]
            put_pair(hid, 2 + v, k, n, cells(x * sigmoid(x)) * inside[...])

    copies[2].wait()
    sweep(14, 7, reg_one)
    clear(hid)

    def reg_two(k, n):
        value = dot(stack_rows(hid, 3, k, n), r2[...])
        for v in range(2):
            row = 3 + v
            mean = cells(value[:, halves[v]]).astype(bf16).astype(f32)
            rest = some(target9, row, k, n, 3)[...] - mean
            noised = rest + sigma * some(noise9, row, k, n, 3)[...]
            some(resid, row, k, n, 3)[...] = rest
            some(noisy, row, k, n, 3)[...] = noised
            put_pair(inp, row, k, n, in_coef * noised * inside[...])

    for copy in copies[3:]:
        copy.wait()
    sweep(13, 13, reg_two)
    clear(inp)

    def conv_one(k, n):
        for v in range(2):
            row = 4 + v
            picked = pick_pair(inp, row, k, n)
            some(taps_in, row, k, n, 4)[...] = picked
            both = jnp.concatenate([flat(picked), flat(some(cond_taps, row, k, n, 2)[...])], 1)
            value = dot(both, w1[...], 1, 1)
            some(act, row, k, n, 4)[...] = cells(value)
            u = value * gain
            put_pair(one, row, k, n, cells(u * sigmoid(u)) * inside[...])

    sweep(12, 6, conv_one)
    clear(one)

    def conv_two(k, n):
        value = dot(stack_rows(one, 5, k, n), w2[...], 1, 1)
        for v in range(2):
            x = value[:, halves[v]]
            s = sigmoid(x)
            some(slope, 5 + v, k, n, 5)[...] = cells(s * (1.0 + x * (1.0 - s)))
            put_pair(two, 5 + v, k, n, cells(x * s) * inside[...])

    sweep(11, 11, conv_two)
    clear(two)

    def conv_three(k, n):
        value = dot(stack_rows(two, 6, k, n), w3r[...])
        for v in range(2):
            row = 6 + v
            full = skip * some(noisy, row, k, n, 3)[...] + out_coef * cells(value[:, halves[v]])
            some(den, row, k, n, 6)[:, :PLANES] = full.astype(bf16)
            delta = delta_coef * (full - some(resid, row, k, n, 3)[...])
            put_pair(dlt, row, k, n, delta * inside[...])

    sweep(10, 10, conv_three)
    clear(dlt)

    def delta_two(k, n):
        parts = []
        for v in range(2):
            picked = pick_pair(dlt, 7 + v, k, n)
            some(taps_d, 7 + v, k, n, 7)[...] = picked
            parts.append(flat(picked))
        value = dot(jnp.concatenate(parts, axis=1), w3f[...], 1, 1)
        for v in range(2):
            x = cells(value[:, halves[v]]) * some(slope, 7 + v, k, n, 5)[...]
            put_pair(sdl, 7 + v, k, n, x * inside[...])

    sweep(9, 9, delta_two)
    clear(sdl)
    film_sum[...] = jnp.zeros((8, 128), f32)

    def delta_one(k, n):
        value = dot(stack_rows(sdl, 8, k, n), w2t[...])
        for v in range(2):
            a = flat(some(act, 8 + v, k, n, 4)[...])
            u = a * gain
            s = sigmoid(u)
            g = flat(cells(value[:, halves[v]] * (s * (1.0 + u * (1.0 - s)))) * tile)
            film_sum[...] += jnp.sum((g * a).reshape(-1, 8, 128), axis=0)
            some(grad1, 8 + v, k, n, 8)[...] = cells(g * gain).astype(bf16)

    sweep(8, 8, delta_one)

    tile_low = tile.astype(bf16)

    def both_rows(read):
        return jnp.concatenate([read(8), read(9)], axis=0)

    def own_cells(ref):
        return lambda row: flat(some(ref, row, 0, 8)[:, 1:PLANES + 1] * tile_low)

    def own_field(ref, base):
        return lambda row: flat(some(ref, row, 0, 8, base)[...])

    def taps_of(row):
        return jnp.concatenate([flat(some(one, row + a - 1, 0, 8)[:, b:b + PLANES])
                                for a in range(3) for b in range(3)], axis=1)

    def first_taps(row):
        return jnp.concatenate([own_field(taps_in, 4)(row), own_field(cond_taps, 2)(row)], axis=1)

    g2 = dot(both_rows(own_cells(sdl)), both_rows(taps_of), 0, 0)
    g1 = dot(both_rows(own_field(grad1, 8)), both_rows(first_taps), 0, 0)
    g3 = dot(both_rows(own_cells(two)), both_rows(own_field(taps_d, 7)), 0, 0)
    film = noise_coef * jnp.sum(film_sum[...], axis=0, keepdims=True)
    film = jnp.transpose(jnp.broadcast_to(film, (8, 128)))[:, 0:1]
    g3 = jnp.where(lax.broadcasted_iota(jnp.int32, (128, 128), 1) == FILM_LANE, film, g3)
    parts = [g2[:, k * 128:(k + 1) * 128] for k in range(9)] + [g1[:, :128], g1[:, 128:], g3]
    for p in range(6):
        pair = [part.reshape(16, 8, 128) for part in parts[2 * p:2 * p + 2]]
        out[:, p * 16:(p + 1) * 16, :] = jnp.concatenate(pair, axis=1).astype(bf16)

    fields = (lax.broadcasted_iota(jnp.int32, (16, 128), 0)
              == lax.broadcasted_iota(jnp.int32, (16, 128), 1)).astype(f32).astype(bf16)
    turned = dot(fields, den[1:9].reshape(16 * 128, 128), 1, 1).astype(bf16)
    turned = jnp.concatenate([turned[:, i * 128:(i + 1) * 128] for i in range(16)], axis=0)
    den_rows[...] = dot(turned, back[...])
    for c in range(6):
        left = den_rows[pl.ds(c, 16, stride=16), :]
        right = den_rows[pl.ds(c + 6, 16, stride=16), :]
        piece = jnp.where(lane < TW, left, right).astype(bf16)
        out[:, 96 + c * 16:96 + (c + 1) * 16, :] = jnp.broadcast_to(piece[None], (16, 16, 128))


def fold_kernel(parts, out):
    for p in range(6):
        total = jnp.sum(parts[:, p * 16:(p + 1) * 16, :].astype(f32), axis=0).astype(bf16)
        for q in range(8):
            out[q, p * 16:(p + 1) * 16, :] = total


def field_kernel(parts, out):
    for k in range(8):
        for c in range(6):
            a = parts[2 * k, 96 + c * 16:96 + (c + 1) * 16, :].astype(f32)
            b = parts[2 * k + 1, 96 + c * 16:96 + (c + 1) * 16, :].astype(f32)
            cols = slice(k * 128, (k + 1) * 128)
            out[c, :, cols] = jnp.concatenate([a[:, :TW], b[:, :TW]], axis=1).astype(bf16)
            out[c + 6, :, cols] = jnp.concatenate([a[:, TW:], b[:, TW:]], axis=1).astype(bf16)


def finish_kernel(parts, g1, g2, g3, film):
    def block(k):
        pair = jnp.sum(parts[:, (k // 2) * 16:(k // 2 + 1) * 16, :].astype(f32), axis=0)
        return pair[(k % 2) * 8:(k % 2) * 8 + 8]

    low, high, third = block(9), block(10), block(11)
    for a in range(3):
        for b in range(3):
            tap = 3 * a + b
            lanes = slice(tap * COUT, (tap + 1) * COUT)
            g2[a, b] = block(tap)
            g1[a, b, :, :COUT] = low[:, lanes]
            g1[a, b, :, COUT:] = high[:, lanes]
            g3[a, b] = third[:, (8 - tap) * COUT:(9 - tap) * COUT]
    film[...] = jnp.transpose(third)[FILM_LANE:FILM_LANE + 1]


VMEM = pl.BlockSpec(memory_space=pltpu.VMEM)
SMEM = pl.BlockSpec(memory_space=pltpu.SMEM)
ANY = pl.BlockSpec(memory_space=pl.ANY)


def kernel_call(body, ins, outs, scratch=(), limit=16, cost=None):
    return pl.pallas_call(
        body,
        in_specs=list(ins),
        out_specs=[VMEM] * len(outs),
        out_shape=[jax.ShapeDtypeStruct(shape, dtype) for shape, dtype in outs],
        scratch_shapes=list(scratch),
        compiler_params=pltpu.CompilerParams(vmem_limit_bytes=limit * MIB),
        cost_estimate=cost,
    )


def planes(rows, dtype, count=PLANES):
    return pltpu.VMEM((rows, count, SUB, 128), dtype)


def pairs(rows, dtype, count=PLANES):
    return pltpu.VMEM((rows // 2, 2, count, SUB, 128), dtype)


def shards(condition, target, noise_draw, sigma_index, reg_first, reg_second, first_kernel,
           second_kernel, third_kernel, film_scale):
    order, back, spread, repeat = place_constants()
    last, leading, packed = kernel_call(
        pack_kernel, [ANY] * 9,
        [((36, 8, 128), f32), ((36, 8, 128), f32), ((16, 112, 128), bf16)],
        [pltpu.VMEM((3, COUT, 16, 256), f32), pltpu.VMEM((3, 3, 8, 24), bf16),
         pltpu.VMEM((3, 3, 8, 128), bf16), pltpu.VMEM((3, 3, 8, 12), bf16),
         pltpu.VMEM((3, 3, 12, 16), bf16), pltpu.VMEM((3, 3, 16, 12), bf16),
         pltpu.VMEM((1, 8), bf16), pltpu.SemaphoreType.DMA((9,))],
        limit=60,
    )(condition, target, noise_draw, jnp.swapaxes(first_kernel, 2, 3),
      jnp.swapaxes(second_kernel, 2, 3), third_kernel, reg_first, reg_second,
      film_scale.reshape(1, 8))
    up = [(i, i + 1) for i in range(lax.axis_size("rows") - 1)]
    before = lax.ppermute(last, "rows", up)
    after = lax.ppermute(leading, "rows", [(j, i) for i, j in up])
    gathered = lax.all_to_all(packed, GROUP, 0, 0, tiled=True)
    cond_taps, target9, noise9 = kernel_call(
        prep_kernel, [ANY] * 7,
        [((14, 2, PLANES, SUB, 128), bf16), ((13, 2, PLANES, SUB, 128), f32),
         ((13, 2, PLANES, SUB, 128), f32)],
        [pltpu.VMEM((48, 32, 128), f32), pltpu.VMEM((3, COUT, 16, 256), f32),
         planes(32, bf16, 7), pltpu.VMEM((WIN, 128), bf16), pltpu.VMEM((128, 384), bf16),
         pltpu.SemaphoreType.DMA((7,))],
        limit=60,
        cost=pl.CostEstimate(flops=1 << 32, bytes_accessed=8 * MIB, transcendentals=0),
    )(condition, target, noise_draw, before, after, jnp.asarray(order, bf16), jnp.asarray(spread, bf16))
    wide = [pairs(32, bf16, PLANES + 2) for _ in range(6)]
    out, = kernel_call(
        step_kernel, [SMEM] * 2 + [ANY] * 6, [((16, 192, 128), bf16)],
        [pairs(28, bf16), pairs(26, f32), pairs(26, f32), pltpu.VMEM((16, 112, 128), bf16),
         pltpu.VMEM((128, 1280), bf16), pltpu.VMEM((128, 128), bf16),
         pltpu.SemaphoreType.DMA((6,)), pltpu.VMEM((256, 1536), bf16),
         pltpu.VMEM((1536, 256), bf16), pltpu.VMEM((128, 256), bf16),
         pltpu.VMEM((128, 128), bf16), pltpu.VMEM((256, 256), bf16),
         pltpu.VMEM((1536, 256), bf16), pltpu.VMEM((256, 256), bf16),
         pltpu.VMEM((1536, 256), bf16)]
        + wide
        + [pairs(24, bf16), pairs(18, bf16), pairs(26, f32), pairs(26, f32),
           pairs(24, f32), pairs(22, f32), pairs(20, bf16, 8), pairs(16, bf16),
           pltpu.VMEM((8, 128), f32), pltpu.VMEM((256, 128), f32),
           pltpu.VMEM((PLANES, SUB, 128), f32)],
        limit=60,
    )(sigma_index, jnp.asarray(coef_table()), cond_taps, target9, noise9, gathered,
      jnp.asarray(repeat, bf16), jnp.asarray(back, bf16))
    parts = lax.all_to_all(out, GROUP, 0, 0, tiled=True)
    folded, = kernel_call(fold_kernel, [VMEM], [((8, 96, 128), bf16)])(parts)
    denoised, = kernel_call(
        field_kernel, [VMEM], [((COUT, 16, NW), bf16)],
        cost=pl.CostEstimate(flops=1 << 26, bytes_accessed=2 * MIB, transcendentals=0),
    )(parts)
    sums = lax.all_to_all(folded, "rows", 0, 0, tiled=True)
    g1, g2, g3, film = kernel_call(
        finish_kernel, [VMEM],
        [((3, 3, 8, 24), f32), ((3, 3, 8, 128), f32), ((3, 3, 8, 12), f32), ((1, 8), f32)],
    )(sums)
    return denoised, jnp.swapaxes(g1, 2, 3), jnp.swapaxes(g2, 2, 3), g3, film.reshape(8)


def solution(mesh):
    return jax.shard_map(
        shards,
        mesh=mesh,
        in_specs=(
            P(None, "rows", None),
            P(None, "rows", None),
            P(None, "rows", None),
            P(),
            P(None, None, None, "chan"),
            P(None, None, "chan", None),
            P(None, None, None, GROUP),
            P(None, None, None, GROUP),
            P(None, None, GROUP, None),
            P(GROUP),
        ),
        out_specs=(
            P(None, "rows", None),
            P(None, None, None, GROUP),
            P(None, None, None, GROUP),
            P(None, None, GROUP, None),
            P(GROUP),
        ),
        check_vma=False,
    )
```

```python
import math

import numpy as np
import jax
import jax.numpy as jnp
from jax import lax
from jax.experimental import pallas as pl
from jax.experimental.pallas import tpu as pltpu
from jax.sharding import PartitionSpec as P

COUT = 12
NSIG = 32
NH = 128
NW = 1024
TW = 64
RIM = 8
PLANES = 5
SUB = 16
WIN = PLANES * SUB
TAPS = 9
FILM_LANE = 120
MIB = 1024 * 1024
GROUP = ("section", "chan")
f32 = jnp.float32
bf16 = jnp.bfloat16


def coef_table():
    i = np.arange(NSIG, dtype=np.float64)
    high, low = 4.0 ** (1 / 7), 0.25 ** (1 / 7)
    level = (high + i / (NSIG - 1) * (low - high)) ** 7
    total = level**2 + 0.25
    out_coef = 0.5 * level / np.sqrt(total)
    weight = total / (0.5 * level) ** 2
    table = np.zeros((NSIG, 8), np.float32)
    table[:, 0] = level
    table[:, 1] = 0.25 / total
    table[:, 2] = out_coef
    table[:, 3] = 1 / np.sqrt(total)
    table[:, 4] = np.log(8 * level) / 4
    table[:, 5] = 2 * weight * out_coef / math.sqrt(COUT * NH * NW)
    return table


def place_constants():
    order = np.zeros((WIN, 128), np.float32)
    back = np.zeros((128, 128), np.float32)
    for t in range(PLANES):
        for s in range(SUB):
            col = PLANES * s + t
            order[t * SUB + s, col] = 1
            if RIM <= col < RIM + TW:
                back[t * SUB + s, col - RIM] = 1
                back[t * SUB + s, TW + col - RIM] = 1
    spread = np.zeros((128, 384), np.float32)
    repeat = np.zeros((128, 10 * 128), np.float32)
    for c in range(COUT):
        for g in range(TAPS):
            spread[24 + c, g * COUT + c] = 1
            for first in (0, 48, 80):
                spread[first + c, 128 + g * COUT + c] = 1
                spread[first + COUT + c, 256 + g * COUT + c] = 1
            for tap in range(TAPS):
                repeat[tap * COUT + c, tap * 128 + g * COUT + c] = 1
            repeat[(8 - g) * COUT + c, 9 * 128 + g * COUT + c] = 1
    return order, back, spread, repeat


def dot(a, b, ca=1, cb=0):
    return lax.dot_general(a, b, (((ca,), (cb,)), ((), ())), preferred_element_type=f32)


def sigmoid(v):
    return 0.5 * jnp.tanh(0.5 * v) + 0.5


def member():
    return lax.axis_index("section") * lax.axis_size("chan") + lax.axis_index("chan")


def window_place():
    start = member() * TW - RIM
    base = jnp.clip((start + 128) // 128 * 128 - 128, 0, NW - 256)
    return start, pl.multiple_of(base, 128)


def window_copy(src, dst, sem):
    copy = pltpu.make_async_copy(src.at[:, :, pl.ds(window_place()[1], 256)], dst, sem)
    copy.start()
    return copy


def window(wide):
    start, base = window_place()
    rows = pltpu.roll(wide.reshape(COUT * 16, 256), lax.rem(512 - (start - base), 256), 1)
    rows = rows[:, :128]
    col = start + lax.broadcasted_iota(jnp.int32, rows.shape, 1)
    return jnp.where((col >= 0) & (col < NW), rows, 0.0).reshape(COUT, 16, 128)


def pack_kernel(cond, target, noise, w1_any, w2_any, w3_any, r1_any, r2_any, film_any,
                last, leading, packed, scr, w1, w2, w3, r1, r2, film, sems):
    small = []
    for k, (src, dst) in enumerate(((w2_any, w2), (w1_any, w1), (w3_any, w3), (r1_any, r1),
                                    (r2_any, r2), (film_any, film))):
        small.append(pltpu.make_async_copy(src, dst, sems.at[k]))
        small[-1].start()
    copies = [window_copy(src, scr.at[k], sems.at[6 + k])
              for k, src in enumerate((target, noise, cond))]
    half = lax.axis_index("section") == 0
    eye = (lax.broadcasted_iota(jnp.int32, (8, 8), 0)
           == lax.broadcasted_iota(jnp.int32, (8, 8), 1)).astype(f32)
    for k, copy in enumerate(copies):
        copy.wait()
        moved = window(scr[k])
        last[k * COUT:(k + 1) * COUT] = moved[:, 8:]
        leading[k * COUT:(k + 1) * COUT] = moved[:, :8]
    for copy in small:
        copy.wait()

    def place(n, at):
        lane = lax.broadcasted_iota(jnp.int32, (n, 128), 1)
        row = lax.broadcasted_iota(jnp.int32, (n, 128), 0)
        return jnp.where((lane - row == at) & (row < COUT), 1.0, 0.0)

    first_in = jnp.zeros((8, 128), f32)
    first_cond = jnp.zeros((8, 128), f32)
    third = jnp.zeros((8, 128), f32)
    reg_a = jnp.zeros((16, 128), f32)
    reg_b = jnp.zeros((16, 128), f32)
    blocks = []
    for a in range(3):
        for b in range(3):
            tap = 3 * a + b
            low = place(COUT, tap * COUT)
            lane = lax.broadcasted_iota(jnp.int32, (24, 128), 1)
            row = lax.broadcasted_iota(jnp.int32, (24, 128), 0)
            low_in = jnp.where((lane - row == tap * COUT) & (row < COUT), 1.0, 0.0)
            low_cond = jnp.where((lane - row == (tap - 1) * COUT) & (row >= COUT), 1.0, 0.0)
            blocks.append(w2[a, b].astype(f32))
            first_in += dot(w1[a, b].astype(f32), low_in)
            first_cond += dot(w1[a, b].astype(f32), low_cond)
            third += dot(w3[a, b].astype(f32), low)
            reg_a += dot(r1[a, b].astype(f32), low, 0, 0)
            reg_b += dot(r2[a, b].astype(f32), low)
    lane = lax.broadcasted_iota(jnp.int32, (8, 128), 1)
    film_col = jnp.sum(eye * film[...].astype(f32), axis=1, keepdims=True)
    third = jnp.where(lane == FILM_LANE, film_col, third)
    blocks += [first_in, first_cond, third,
               jnp.where(half, reg_a[:8], reg_a[8:]), jnp.where(half, reg_b[:8], reg_b[8:])]
    for p in range(7):
        pair = jnp.concatenate(blocks[2 * p:2 * p + 2], axis=0).astype(bf16)
        for q in range(16):
            packed[q, p * 16:(p + 1) * 16, :] = pair


def put(ref, at, n, value):
    ref[pl.ds(at, n), 1:PLANES + 1] = value.astype(bf16)
    ref[pl.ds(at, n), 0] = pltpu.roll(value[:, PLANES - 1], 1, 1).astype(bf16)
    ref[pl.ds(at, n), PLANES + 1] = pltpu.roll(value[:, 0], SUB - 1, 1).astype(bf16)


def pick_taps(ref, at, n):
    lane = lax.broadcasted_iota(jnp.int32, (SUB, 128), 1)
    total = None
    for a in range(3):
        for b in range(3):
            low = (3 * a + b) * COUT
            mask = jnp.where((lane >= low) & (lane < low + COUT), 1.0, 0.0).astype(bf16)
            part = ref[pl.ds(at + a - 1, n), b:b + PLANES] * mask[None, None]
            total = part if total is None else total + part
    return total


def prep_kernel(cond, target, noise, before, after, order_any, spread_any,
                cond_taps, fields, scr, wide, cond9, cells, order, spread, sems):
    copies = [window_copy(src, wide.at[k], sems.at[k])
              for k, src in enumerate((target, noise, cond))]
    others = [
        pltpu.make_async_copy(before, scr.at[0:36, 0:8, :], sems.at[3]),
        pltpu.make_async_copy(after, scr.at[0:36, 24:32, :], sems.at[4]),
        pltpu.make_async_copy(order_any, order, sems.at[5]),
        pltpu.make_async_copy(spread_any, spread, sems.at[6]),
    ]
    for copy in others:
        copy.start()
    scr[36:48] = jnp.zeros((12, 32, 128), f32)
    for k, copy in enumerate(copies):
        copy.wait()
        scr[k * COUT:(k + 1) * COUT, 8:24] = window(wide[k])
    for copy in others:
        copy.wait()
    flat = scr.reshape(48 * 32, 128)

    for i in range(1, 31):
        x = flat[pl.ds(i, 48, stride=32), :]
        high = x.astype(bf16)
        rest = x[:32] - high[:32].astype(f32)
        mid = rest.astype(bf16)
        low = (rest - mid.astype(f32)).astype(bf16)
        rows = jnp.concatenate([high, mid, low, jnp.zeros((16, 128), bf16)], axis=0)
        turned = dot(order[...], rows, 1, 1).astype(bf16)
        cells[(i - 1) * WIN:i * WIN] = turned
        if 3 <= i < 29:
            fields[(i - 3) // 2, (i - 3) % 2] = turned.reshape(PLANES, SUB, 128)
    count = 6
    for i in range(1, 31, count):
        wide = dot(cells[(i - 1) * WIN:(i - 1 + count) * WIN], spread[...])
        put(cond9, i, count, wide.reshape(count, PLANES, SUB, 128))

    @pl.loop(0, 7)
    def _(k):
        at = 2 + 4 * k
        cond_taps[pl.ds(2 * k, 2)] = pick_taps(cond9, at, 4).reshape(2, 2, PLANES, SUB, 128)


def some(ref, row, k, n, base=0):
    return ref.at[pl.ds((row - base) // 2 + k, n), (row - base) % 2]


def put_pair(ref, row, k, n, value):
    dst = some(ref, row, k, n)
    dst[:, 1:PLANES + 1] = value.astype(bf16)
    dst[:, 0] = pltpu.roll(value[:, PLANES - 1], 1, 1).astype(bf16)
    dst[:, PLANES + 1] = pltpu.roll(value[:, 0], SUB - 1, 1).astype(bf16)


def stack_rows(ref, row, k, n):
    parts = []
    for u in range(4):
        src = some(ref, row + u - 1, k, n)
        for b in range(3):
            parts.append(src[:, b:b + PLANES].reshape(n * WIN, 128))
    return jnp.concatenate(parts, axis=1)


def pick_pair(ref, row, k, n):
    lane = lax.broadcasted_iota(jnp.int32, (SUB, 128), 1)
    total = None
    for a in range(3):
        src = some(ref, row + a - 1, k, n)
        for b in range(3):
            low = (3 * a + b) * COUT
            mask = jnp.where((lane >= low) & (lane < low + COUT), 1.0, 0.0).astype(bf16)
            part = src[:, b:b + PLANES] * mask[None, None]
            total = part if total is None else total + part
    return total


def step_kernel(index_any, table_any, cond_any, field_any, gathered_any, repeat_any, back_any,
                spread_any, out, index, table, cond_taps, fields, gathered, repeat, back, spread, sems,
                w2, w2t, w1, w3, w3f, w3r, r1, r2,
                hid, inp, one, two, dlt, sdl, taps_in, taps_d, resid, noisy, act, slope,
                den, grad1, film_sum, den_rows, inside):
    copies = []
    for k, (src, dst) in enumerate(((gathered_any, gathered), (repeat_any, repeat),
                                    (cond_any, cond_taps), (spread_any, spread),
                                    (field_any, fields), (index_any, index),
                                    (table_any, table), (back_any, back))):
        copies.append(pltpu.make_async_copy(src, dst, sems.at[k]))
        copies[-1].start()
    first_row = lax.axis_index("rows") * 16 - RIM
    first_col = member() * TW - RIM
    for ref in (w2, w2t, w3r, r2):
        ref[...] = jnp.zeros(ref.shape, bf16)
    for ref in (r1, w3f):
        ref[...] = jnp.zeros(ref.shape, bf16)
    den[:, :, PLANES:] = jnp.zeros((10, 2, 8 - PLANES, SUB, 128), bf16)
    shape = (PLANES, SUB, 128)
    col = (lax.broadcasted_iota(jnp.int32, shape, 1) * PLANES
           + lax.broadcasted_iota(jnp.int32, shape, 0))
    inside[...] = jnp.where((col + first_col >= 0) & (col + first_col < NW), 1.0, 0.0)
    tile = jnp.where((col >= RIM) & (col < RIM + TW), 1.0, 0.0)

    def block(k):
        pair = gathered[:, (k // 2) * 16:(k // 2 + 1) * 16, :].astype(f32)
        low = (k % 2) * 8
        return pair[:, low:low + 8].reshape(128, 128).astype(bf16)

    def spot(tap, v):
        a, b = tap // 3, tap % 3
        at = (3 * (a + v) + b) * 128
        return slice(at, at + 128)

    halves = (slice(0, 128), slice(128, 256))
    copies[0].wait()
    for v in range(2):
        r1[halves[v], halves[v]] = block(12)
    w3[...] = block(11)
    copies[1].wait()
    wide = dot(block(13), repeat[:, :9 * 128]).astype(bf16)
    for tap in range(TAPS):
        for v in range(2):
            r2[spot(tap, v), halves[v]] = wide[:, tap * 128:(tap + 1) * 128]
    w1[:, :128] = block(9)
    w1[:, 128:] = block(10)
    for tap in range(TAPS):
        part = block(tap)
        for v in range(2):
            w2[halves[v], spot(tap, v)] = part
            w2t[spot(8 - tap, v), halves[v]] = part
    wide = dot(w3[...], repeat[...]).astype(bf16)
    for tap in range(TAPS):
        for v in range(2):
            w3r[spot(tap, v), halves[v]] = wide[:, tap * 128:(tap + 1) * 128]
    for v in range(2):
        w3f[halves[v], halves[v]] = wide[:, 9 * 128:]

    def cells(value):
        return value.reshape(-1, PLANES, SUB, 128)

    def flat(value):
        return value.reshape(-1, 128)

    def sweep(count, n, body):
        @pl.loop(0, count // n)
        def _(k):
            body(k * n, n)

        if count % n:
            body(count // n * n, count % n)

    def clear(ref):
        @pl.when(first_row < 0)
        def _():
            ref[0:4] = jnp.zeros((4, 2, PLANES + 2, SUB, 128), bf16)

        @pl.when(first_row + 32 > NH)
        def _():
            ref[12:16] = jnp.zeros((4, 2, PLANES + 2, SUB, 128), bf16)

    def reg_one(k, n):
        both = jnp.concatenate([flat(some(cond_taps, 2 + v, k, n, 2)[...]) for v in range(2)], 1)
        value = dot(both, r1[...], 1, 1)
        for v in range(2):
            x = value[:, halves[v]]
            put_pair(hid, 2 + v, k, n, cells(x * sigmoid(x)) * inside[...])

    copies[2].wait()
    sweep(14, 7, reg_one)
    clear(hid)

    def reg_two(k, n):
        value = dot(stack_rows(hid, 3, k, n), r2[...])
        for v in range(2):
            row = 3 + v
            mean = cells(value[:, halves[v]]).astype(bf16).astype(f32)
            both = dot(flat(some(fields, row, k, n, 3)[...]), spread[...])
            rest = cells(both[:, halves[0]]) - mean
            noised = rest + sigma * cells(both[:, halves[1]])
            some(resid, row, k, n, 3)[...] = rest
            some(noisy, row, k, n, 3)[...] = noised
            put_pair(inp, row, k, n, in_coef * noised * inside[...])

    for copy in copies[3:]:
        copy.wait()
    level = index[0]
    sigma, skip, out_coef = table[level, 0], table[level, 1], table[level, 2]
    in_coef, noise_coef, delta_coef = table[level, 3], table[level, 4], table[level, 5]
    lane = lax.broadcasted_iota(jnp.int32, (16, 128), 1)
    pick_film = jnp.where(lane == FILM_LANE, 1.0, 0.0).astype(bf16)
    gain = 1.0 + noise_coef * dot(pick_film, w3[...], 1, 1)[0:1]
    sweep(13, 13, reg_two)
    clear(inp)

    def conv_one(k, n):
        for v in range(2):
            row = 4 + v
            picked = pick_pair(inp, row, k, n)
            some(taps_in, row, k, n, 4)[...] = picked
            both = jnp.concatenate([flat(picked), flat(some(cond_taps, row, k, n, 2)[...])], 1)
            value = dot(both, w1[...], 1, 1)
            some(act, row, k, n, 4)[...] = cells(value)
            u = value * gain
            put_pair(one, row, k, n, cells(u * sigmoid(u)) * inside[...])

    sweep(12, 6, conv_one)
    clear(one)

    def conv_two(k, n):
        value = dot(stack_rows(one, 5, k, n), w2[...], 1, 1)
        for v in range(2):
            x = value[:, halves[v]]
            s = sigmoid(x)
            some(slope, 5 + v, k, n, 5)[...] = cells(s * (1.0 + x * (1.0 - s)))
            put_pair(two, 5 + v, k, n, cells(x * s) * inside[...])

    sweep(11, 11, conv_two)
    clear(two)

    def conv_three(k, n):
        value = dot(stack_rows(two, 6, k, n), w3r[...])
        for v in range(2):
            row = 6 + v
            full = skip * some(noisy, row, k, n, 3)[...] + out_coef * cells(value[:, halves[v]])
            some(den, row, k, n, 6)[:, :PLANES] = full.astype(bf16)
            delta = delta_coef * (full - some(resid, row, k, n, 3)[...])
            put_pair(dlt, row, k, n, delta * inside[...])

    sweep(10, 5, conv_three)
    clear(dlt)

    def delta_two(k, n):
        parts = []
        for v in range(2):
            picked = pick_pair(dlt, 7 + v, k, n)
            some(taps_d, 7 + v, k, n, 7)[...] = picked
            parts.append(flat(picked))
        value = dot(jnp.concatenate(parts, axis=1), w3f[...], 1, 1)
        for v in range(2):
            x = cells(value[:, halves[v]]) * some(slope, 7 + v, k, n, 5)[...]
            put_pair(sdl, 7 + v, k, n, x * inside[...])

    sweep(9, 9, delta_two)
    clear(sdl)
    film_sum[...] = jnp.zeros((8, 128), f32)

    def delta_one(k, n):
        value = dot(stack_rows(sdl, 8, k, n), w2t[...])
        for v in range(2):
            a = flat(some(act, 8 + v, k, n, 4)[...])
            u = a * gain
            s = sigmoid(u)
            g = flat(cells(value[:, halves[v]] * (s * (1.0 + u * (1.0 - s)))) * tile)
            film_sum[...] += jnp.sum((g * a).reshape(-1, 8, 128), axis=0)
            some(grad1, 8 + v, k, n, 8)[...] = cells(g * gain).astype(bf16)

    sweep(8, 8, delta_one)

    tile_low = tile.astype(bf16)

    def both_rows(read):
        return jnp.concatenate([read(8), read(9)], axis=0)

    def own_cells(ref):
        return lambda row: flat(some(ref, row, 0, 8)[:, 1:PLANES + 1] * tile_low)

    def own_field(ref, base):
        return lambda row: flat(some(ref, row, 0, 8, base)[...])

    def taps_of(row):
        return jnp.concatenate([flat(some(one, row + a - 1, 0, 8)[:, b:b + PLANES])
                                for a in range(3) for b in range(3)], axis=1)

    def first_taps(row):
        return jnp.concatenate([own_field(taps_in, 4)(row), own_field(cond_taps, 2)(row)], axis=1)

    g2 = dot(both_rows(own_cells(sdl)), both_rows(taps_of), 0, 0)
    g1 = dot(both_rows(own_field(grad1, 8)), both_rows(first_taps), 0, 0)
    g3 = dot(both_rows(own_cells(two)), both_rows(own_field(taps_d, 7)), 0, 0)
    film = noise_coef * jnp.sum(film_sum[...], axis=0, keepdims=True)
    film = jnp.transpose(jnp.broadcast_to(film, (8, 128)))[:, 0:1]
    g3 = jnp.where(lax.broadcasted_iota(jnp.int32, (128, 128), 1) == FILM_LANE, film, g3)
    parts = [g2[:, k * 128:(k + 1) * 128] for k in range(9)] + [g1[:, :128], g1[:, 128:], g3]
    for p in range(6):
        pair = [part.reshape(16, 8, 128) for part in parts[2 * p:2 * p + 2]]
        out[:, p * 16:(p + 1) * 16, :] = jnp.concatenate(pair, axis=1).astype(bf16)

    fields = (lax.broadcasted_iota(jnp.int32, (16, 128), 0)
              == lax.broadcasted_iota(jnp.int32, (16, 128), 1)).astype(f32).astype(bf16)
    turned = dot(fields, den[1:9].reshape(16 * 128, 128), 1, 1).astype(bf16)
    turned = jnp.concatenate([turned[:, i * 128:(i + 1) * 128] for i in range(16)], axis=0)
    den_rows[...] = dot(turned, back[...])
    for c in range(6):
        left = den_rows[pl.ds(c, 16, stride=16), :]
        right = den_rows[pl.ds(c + 6, 16, stride=16), :]
        piece = jnp.where(lane < TW, left, right).astype(bf16)
        out[:, 96 + c * 16:96 + (c + 1) * 16, :] = jnp.broadcast_to(piece[None], (16, 16, 128))


def fold_kernel(parts, out):
    for p in range(6):
        total = jnp.sum(parts[:, p * 16:(p + 1) * 16, :].astype(f32), axis=0).astype(bf16)
        for q in range(8):
            out[q, p * 16:(p + 1) * 16, :] = total


def field_kernel(parts, out):
    for k in range(8):
        for c in range(6):
            a = parts[2 * k, 96 + c * 16:96 + (c + 1) * 16, :].astype(f32)
            b = parts[2 * k + 1, 96 + c * 16:96 + (c + 1) * 16, :].astype(f32)
            cols = slice(k * 128, (k + 1) * 128)
            out[c, :, cols] = jnp.concatenate([a[:, :TW], b[:, :TW]], axis=1).astype(bf16)
            out[c + 6, :, cols] = jnp.concatenate([a[:, TW:], b[:, TW:]], axis=1).astype(bf16)


def finish_kernel(parts, g1, g2, g3, film):
    def block(k):
        pair = jnp.sum(parts[:, (k // 2) * 16:(k // 2 + 1) * 16, :].astype(f32), axis=0)
        return pair[(k % 2) * 8:(k % 2) * 8 + 8]

    low, high, third = block(9), block(10), block(11)
    for a in range(3):
        for b in range(3):
            tap = 3 * a + b
            lanes = slice(tap * COUT, (tap + 1) * COUT)
            g2[a, b] = block(tap)
            g1[a, b, :, :COUT] = low[:, lanes]
            g1[a, b, :, COUT:] = high[:, lanes]
            g3[a, b] = third[:, (8 - tap) * COUT:(9 - tap) * COUT]
    film[...] = jnp.transpose(third)[FILM_LANE:FILM_LANE + 1]


VMEM = pl.BlockSpec(memory_space=pltpu.VMEM)
ANY = pl.BlockSpec(memory_space=pl.ANY)


def kernel_call(body, ins, outs, scratch=(), limit=16, cost=None):
    return pl.pallas_call(
        body,
        in_specs=list(ins),
        out_specs=[VMEM] * len(outs),
        out_shape=[jax.ShapeDtypeStruct(shape, dtype) for shape, dtype in outs],
        scratch_shapes=list(scratch),
        compiler_params=pltpu.CompilerParams(vmem_limit_bytes=limit * MIB),
        cost_estimate=cost,
    )


def planes(rows, dtype, count=PLANES):
    return pltpu.VMEM((rows, count, SUB, 128), dtype)


def pairs(rows, dtype, count=PLANES):
    return pltpu.VMEM((rows // 2, 2, count, SUB, 128), dtype)


def shards(condition, target, noise_draw, sigma_index, reg_first, reg_second, first_kernel,
           second_kernel, third_kernel, film_scale):
    order, back, spread, repeat = place_constants()
    last, leading, packed = kernel_call(
        pack_kernel, [ANY] * 9,
        [((36, 8, 128), f32), ((36, 8, 128), f32), ((16, 112, 128), bf16)],
        [pltpu.VMEM((3, COUT, 16, 256), f32), pltpu.VMEM((3, 3, 8, 24), bf16),
         pltpu.VMEM((3, 3, 8, 128), bf16), pltpu.VMEM((3, 3, 8, 12), bf16),
         pltpu.VMEM((3, 3, 12, 16), bf16), pltpu.VMEM((3, 3, 16, 12), bf16),
         pltpu.VMEM((1, 8), bf16), pltpu.SemaphoreType.DMA((9,))],
        limit=60,
    )(condition, target, noise_draw, jnp.swapaxes(first_kernel, 2, 3),
      jnp.swapaxes(second_kernel, 2, 3), third_kernel, reg_first, reg_second,
      film_scale.reshape(1, 8))
    up = [(i, i + 1) for i in range(lax.axis_size("rows") - 1)]
    before = lax.ppermute(last, "rows", up)
    after = lax.ppermute(leading, "rows", [(j, i) for i, j in up])
    gathered = lax.all_to_all(packed, GROUP, 0, 0, tiled=True)
    cond_taps, fields = kernel_call(
        prep_kernel, [ANY] * 7,
        [((14, 2, PLANES, SUB, 128), bf16), ((13, 2, PLANES, SUB, 128), bf16)],
        [pltpu.VMEM((48, 32, 128), f32), pltpu.VMEM((3, COUT, 16, 256), f32),
         planes(32, bf16, 7), pltpu.VMEM((30 * WIN, 128), bf16), pltpu.VMEM((WIN, 128), bf16), pltpu.VMEM((128, 128), bf16),
         pltpu.SemaphoreType.DMA((7,))],
        limit=60,
        cost=pl.CostEstimate(flops=1 << 32, bytes_accessed=8 * MIB, transcendentals=0),
    )(condition, target, noise_draw, before, after, jnp.asarray(order, bf16), jnp.asarray(spread[:, :128], bf16))
    wide = [pairs(32, bf16, PLANES + 2) for _ in range(6)]
    out, = kernel_call(
        step_kernel, [ANY] * 8, [((16, 192, 128), bf16)],
        [pltpu.SMEM((1,), jnp.int32), pltpu.SMEM((NSIG, 8), f32), pairs(28, bf16),
         pairs(26, bf16), pltpu.VMEM((16, 112, 128), bf16), pltpu.VMEM((128, 1280), bf16),
         pltpu.VMEM((128, 128), bf16), pltpu.VMEM((128, 256), bf16),
         pltpu.SemaphoreType.DMA((8,)), pltpu.VMEM((256, 1536), bf16),
         pltpu.VMEM((1536, 256), bf16), pltpu.VMEM((128, 256), bf16),
         pltpu.VMEM((128, 128), bf16), pltpu.VMEM((256, 256), bf16),
         pltpu.VMEM((1536, 256), bf16), pltpu.VMEM((256, 256), bf16),
         pltpu.VMEM((1536, 256), bf16)]
        + wide
        + [pairs(24, bf16), pairs(18, bf16), pairs(26, f32), pairs(26, f32),
           pairs(24, f32), pairs(22, f32), pairs(20, bf16, 8), pairs(16, bf16),
           pltpu.VMEM((8, 128), f32), pltpu.VMEM((256, 128), f32),
           pltpu.VMEM((PLANES, SUB, 128), f32)],
        limit=60,
    )(sigma_index, jnp.asarray(coef_table()), cond_taps, fields, gathered,
      jnp.asarray(repeat, bf16), jnp.asarray(back, bf16), jnp.asarray(spread[:, 128:], bf16))
    parts = lax.all_to_all(out, GROUP, 0, 0, tiled=True)
    folded, = kernel_call(fold_kernel, [VMEM], [((8, 96, 128), bf16)])(parts)
    denoised, = kernel_call(
        field_kernel, [VMEM], [((COUT, 16, NW), bf16)],
        cost=pl.CostEstimate(flops=1 << 26, bytes_accessed=2 * MIB, transcendentals=0),
    )(parts)
    sums = lax.all_to_all(folded, "rows", 0, 0, tiled=True)
    g1, g2, g3, film = kernel_call(
        finish_kernel, [VMEM],
        [((3, 3, 8, 24), f32), ((3, 3, 8, 128), f32), ((3, 3, 8, 12), f32), ((1, 8), f32)],
    )(sums)
    return denoised, jnp.swapaxes(g1, 2, 3), jnp.swapaxes(g2, 2, 3), g3, film.reshape(8)


def solution(mesh):
    return jax.shard_map(
        shards,
        mesh=mesh,
        in_specs=(
            P(None, "rows", None),
            P(None, "rows", None),
            P(None, "rows", None),
            P(),
            P(None, None, None, "chan"),
            P(None, None, "chan", None),
            P(None, None, None, GROUP),
            P(None, None, None, GROUP),
            P(None, None, GROUP, None),
            P(GROUP),
        ),
        out_specs=(
            P(None, "rows", None),
            P(None, None, None, GROUP),
            P(None, None, None, GROUP),
            P(None, None, GROUP, None),
            P(GROUP),
        ),
        check_vma=False,
    )
```

```python
import math

import numpy as np
import jax
import jax.numpy as jnp
from jax import lax
from jax.experimental import pallas as pl
from jax.experimental.pallas import tpu as pltpu
from jax.sharding import PartitionSpec as P

COUT = 12
NSIG = 32
NH = 128
NW = 1024
TW = 64
RIM = 8
PLANES = 5
SUB = 16
WIN = PLANES * SUB
TAPS = 9
FILM_LANE = 120
MIB = 1024 * 1024
GROUP = ("section", "chan")
f32 = jnp.float32
bf16 = jnp.bfloat16


def coef_table():
    i = np.arange(NSIG, dtype=np.float64)
    high, low = 4.0 ** (1 / 7), 0.25 ** (1 / 7)
    level = (high + i / (NSIG - 1) * (low - high)) ** 7
    total = level**2 + 0.25
    out_coef = 0.5 * level / np.sqrt(total)
    weight = total / (0.5 * level) ** 2
    table = np.zeros((NSIG, 8), np.float32)
    table[:, 0] = level
    table[:, 1] = 0.25 / total
    table[:, 2] = out_coef
    table[:, 3] = 1 / np.sqrt(total)
    table[:, 4] = np.log(8 * level) / 4
    table[:, 5] = 2 * weight * out_coef / math.sqrt(COUT * NH * NW)
    return table


def place_constants():
    order = np.zeros((WIN, 128), np.float32)
    back = np.zeros((128, 128), np.float32)
    for t in range(PLANES):
        for s in range(SUB):
            col = PLANES * s + t
            order[t * SUB + s, col] = 1
            if RIM <= col < RIM + TW:
                back[t * SUB + s, col - RIM] = 1
                back[t * SUB + s, TW + col - RIM] = 1
    spread = np.zeros((128, 384), np.float32)
    repeat = np.zeros((128, 10 * 128), np.float32)
    for c in range(COUT):
        for g in range(TAPS):
            spread[24 + c, g * COUT + c] = 1
            for first in (0, 48, 80):
                spread[first + c, 128 + g * COUT + c] = 1
                spread[first + COUT + c, 256 + g * COUT + c] = 1
            for tap in range(TAPS):
                repeat[tap * COUT + c, tap * 128 + g * COUT + c] = 1
            repeat[(8 - g) * COUT + c, 9 * 128 + g * COUT + c] = 1
    return order, back, spread, repeat


def dot(a, b, ca=1, cb=0):
    return lax.dot_general(a, b, (((ca,), (cb,)), ((), ())), preferred_element_type=f32)


def sigmoid(v):
    return 0.5 * jnp.tanh(0.5 * v) + 0.5


def member():
    return lax.axis_index("section") * lax.axis_size("chan") + lax.axis_index("chan")


def window_place():
    start = member() * TW - RIM
    base = jnp.clip((start + 128) // 128 * 128 - 128, 0, NW - 256)
    return start, pl.multiple_of(base, 128)


def window_copy(src, dst, sem):
    copy = pltpu.make_async_copy(src.at[:, :, pl.ds(window_place()[1], 256)], dst, sem)
    copy.start()
    return copy


def window(wide):
    start, base = window_place()
    rows = pltpu.roll(wide.reshape(COUT * 16, 256), lax.rem(512 - (start - base), 256), 1)
    rows = rows[:, :128]
    col = start + lax.broadcasted_iota(jnp.int32, rows.shape, 1)
    return jnp.where((col >= 0) & (col < NW), rows, 0.0).reshape(COUT, 16, 128)


def scalar_copies(index_any, table_any, index, table, sem_a, sem_b):
    copies = [pltpu.make_async_copy(index_any, index, sem_a),
              pltpu.make_async_copy(table_any, table, sem_b)]
    for copy in copies:
        copy.start()
    return copies


def send(ref, field, low):
    high = field.astype(bf16)
    ref[:COUT] = high
    ref[COUT:2 * COUT] = (field - high.astype(f32)).astype(bf16)
    ref[2 * COUT:] = low.astype(bf16)


def pack_kernel(index_any, table_any, cond, target, noise, w1_any, w2_any, w3_any, r1_any,
                r2_any, film_any, last, leading, packed,
                index, table, scr, w1, w2, w3, r1, r2, film, sems):
    scalars = scalar_copies(index_any, table_any, index, table, sems.at[9], sems.at[10])
    small = []
    for k, (src, dst) in enumerate(((w2_any, w2), (w1_any, w1), (w3_any, w3), (r1_any, r1),
                                    (r2_any, r2), (film_any, film))):
        small.append(pltpu.make_async_copy(src, dst, sems.at[k]))
        small[-1].start()
    copies = [window_copy(src, scr.at[k], sems.at[6 + k])
              for k, src in enumerate((target, noise, cond))]
    half = lax.axis_index("section") == 0
    eye = (lax.broadcasted_iota(jnp.int32, (8, 8), 0)
           == lax.broadcasted_iota(jnp.int32, (8, 8), 1)).astype(f32)
    for copy in copies + scalars:
        copy.wait()
    draw = window(scr[1])
    noised = window(scr[0]) + table[index[0], 0] * draw
    low = window(scr[2])
    row = lax.broadcasted_iota(jnp.int32, (COUT, 8, 128), 1)
    send(last, jnp.where(row < 2, pltpu.roll(draw[:, 8:], 2, 1), noised[:, 8:]), low[:, 8:])
    send(leading, jnp.where(row >= 6, pltpu.roll(draw[:, :8], 6, 1), noised[:, :8]), low[:, :8])
    for copy in small:
        copy.wait()

    def place(n, at):
        lane = lax.broadcasted_iota(jnp.int32, (n, 128), 1)
        row = lax.broadcasted_iota(jnp.int32, (n, 128), 0)
        return jnp.where((lane - row == at) & (row < COUT), 1.0, 0.0)

    first_in = jnp.zeros((8, 128), f32)
    first_cond = jnp.zeros((8, 128), f32)
    third = jnp.zeros((8, 128), f32)
    reg_a = jnp.zeros((16, 128), f32)
    reg_b = jnp.zeros((16, 128), f32)
    blocks = []
    for a in range(3):
        for b in range(3):
            tap = 3 * a + b
            low = place(COUT, tap * COUT)
            lane = lax.broadcasted_iota(jnp.int32, (24, 128), 1)
            row = lax.broadcasted_iota(jnp.int32, (24, 128), 0)
            low_in = jnp.where((lane - row == tap * COUT) & (row < COUT), 1.0, 0.0)
            low_cond = jnp.where((lane - row == (tap - 1) * COUT) & (row >= COUT), 1.0, 0.0)
            blocks.append(w2[a, b].astype(f32))
            first_in += dot(w1[a, b].astype(f32), low_in)
            first_cond += dot(w1[a, b].astype(f32), low_cond)
            third += dot(w3[a, b].astype(f32), low)
            reg_a += dot(r1[a, b].astype(f32), low, 0, 0)
            reg_b += dot(r2[a, b].astype(f32), low)
    lane = lax.broadcasted_iota(jnp.int32, (8, 128), 1)
    film_col = jnp.sum(eye * film[...].astype(f32), axis=1, keepdims=True)
    third = jnp.where(lane == FILM_LANE, film_col, third)
    blocks += [first_in, first_cond, third,
               jnp.where(half, reg_a[:8], reg_a[8:]), jnp.where(half, reg_b[:8], reg_b[8:])]
    for p in range(7):
        pair = jnp.concatenate(blocks[2 * p:2 * p + 2], axis=0).astype(bf16)
        for q in range(16):
            packed[q, p * 16:(p + 1) * 16, :] = pair


def put(ref, at, n, value):
    ref[pl.ds(at, n), 1:PLANES + 1] = value.astype(bf16)
    ref[pl.ds(at, n), 0] = pltpu.roll(value[:, PLANES - 1], 1, 1).astype(bf16)
    ref[pl.ds(at, n), PLANES + 1] = pltpu.roll(value[:, 0], SUB - 1, 1).astype(bf16)


def pick_taps(ref, at, n):
    lane = lax.broadcasted_iota(jnp.int32, (SUB, 128), 1)
    total = None
    for a in range(3):
        for b in range(3):
            low = (3 * a + b) * COUT
            mask = jnp.where((lane >= low) & (lane < low + COUT), 1.0, 0.0).astype(bf16)
            part = ref[pl.ds(at + a - 1, n), b:b + PLANES] * mask[None, None]
            total = part if total is None else total + part
    return total


def prep_kernel(index_any, table_any, cond, target, noise, before, after, order_any, spread_any,
                cond_taps, fields, index, table, scr, wide, cond9, cells, order, spread, sems):
    copies = [window_copy(src, wide.at[k], sems.at[k])
              for k, src in enumerate((target, noise, cond))]
    others = [
        pltpu.make_async_copy(order_any, order, sems.at[3]),
        pltpu.make_async_copy(spread_any, spread, sems.at[4]),
    ]
    for copy in others:
        copy.start()
    scalars = scalar_copies(index_any, table_any, index, table, sems.at[5], sems.at[6])
    scr[36:48] = jnp.zeros((12, 32, 128), f32)
    for src, rows, shift in ((before, slice(0, 8), 6), (after, slice(24, 32), 2)):
        field = src[:COUT].astype(f32) + src[COUT:2 * COUT].astype(f32)
        scr[0:12, rows] = field
        scr[12:24, rows] = pltpu.roll(field, shift, 1)
        scr[24:36, rows] = src[2 * COUT:].astype(f32)
    for copy in copies + scalars:
        copy.wait()
    draw = window(wide[1])
    scr[0:12, 8:24] = window(wide[0]) + table[index[0], 0] * draw
    scr[12:24, 8:24] = draw
    scr[24:36, 8:24] = window(wide[2])
    for copy in others:
        copy.wait()
    flat = scr.reshape(48 * 32, 128)

    for i in range(1, 31):
        x = flat[pl.ds(i, 48, stride=32), :]
        high = x.astype(bf16)
        rest = x[:32] - high[:32].astype(f32)
        mid = rest.astype(bf16)
        low = (rest - mid.astype(f32)).astype(bf16)
        rows = jnp.concatenate([high, mid, low, jnp.zeros((16, 128), bf16)], axis=0)
        turned = dot(order[...], rows, 1, 1).astype(bf16)
        cells[(i - 1) * WIN:i * WIN] = turned
        if 3 <= i < 29:
            fields[(i - 3) // 2, (i - 3) % 2] = turned.reshape(PLANES, SUB, 128)
    count = 6
    for i in range(1, 31, count):
        wide = dot(cells[(i - 1) * WIN:(i - 1 + count) * WIN], spread[...])
        put(cond9, i, count, wide.reshape(count, PLANES, SUB, 128))

    @pl.loop(0, 7)
    def _(k):
        at = 2 + 4 * k
        cond_taps[pl.ds(2 * k, 2)] = pick_taps(cond9, at, 4).reshape(2, 2, PLANES, SUB, 128)


def some(ref, row, k, n, base=0):
    return ref.at[pl.ds((row - base) // 2 + k, n), (row - base) % 2]


def put_pair(ref, row, k, n, value):
    dst = some(ref, row, k, n)
    dst[:, 1:PLANES + 1] = value.astype(bf16)
    dst[:, 0] = pltpu.roll(value[:, PLANES - 1], 1, 1).astype(bf16)
    dst[:, PLANES + 1] = pltpu.roll(value[:, 0], SUB - 1, 1).astype(bf16)


def stack_rows(ref, row, k, n):
    parts = []
    for u in range(4):
        src = some(ref, row + u - 1, k, n)
        for b in range(3):
            parts.append(src[:, b:b + PLANES].reshape(n * WIN, 128))
    return jnp.concatenate(parts, axis=1)


def pick_pair(ref, row, k, n):
    lane = lax.broadcasted_iota(jnp.int32, (SUB, 128), 1)
    total = None
    for a in range(3):
        src = some(ref, row + a - 1, k, n)
        for b in range(3):
            low = (3 * a + b) * COUT
            mask = jnp.where((lane >= low) & (lane < low + COUT), 1.0, 0.0).astype(bf16)
            part = src[:, b:b + PLANES] * mask[None, None]
            total = part if total is None else total + part
    return total


def step_kernel(index_any, table_any, field_any, cond_taps, gathered, repeat, back, spread, out,
                index, table, fields, sems,
                w2, w2t, w1, w3, w3f, w3r, r1, r2,
                hid, inp, one, two, dlt, sdl, taps_in, taps_d, draw, noisy, act, slope,
                den, grad1, film_sum, den_rows, inside):
    copies = scalar_copies(index_any, table_any, index, table, sems.at[0], sems.at[1])
    copies.append(pltpu.make_async_copy(field_any, fields, sems.at[2]))
    copies[-1].start()
    first_row = lax.axis_index("rows") * 16 - RIM
    first_col = member() * TW - RIM
    for ref in (w2, w2t, w3r, r2):
        ref[...] = jnp.zeros(ref.shape, bf16)
    for ref in (r1, w3f):
        ref[...] = jnp.zeros(ref.shape, bf16)
    den[:, :, PLANES:] = jnp.zeros((10, 2, 8 - PLANES, SUB, 128), bf16)
    shape = (PLANES, SUB, 128)
    col = (lax.broadcasted_iota(jnp.int32, shape, 1) * PLANES
           + lax.broadcasted_iota(jnp.int32, shape, 0))
    inside[...] = jnp.where((col + first_col >= 0) & (col + first_col < NW), 1.0, 0.0)
    tile = jnp.where((col >= RIM) & (col < RIM + TW), 1.0, 0.0)

    def block(k):
        pair = gathered[:, (k // 2) * 16:(k // 2 + 1) * 16, :].astype(f32)
        low = (k % 2) * 8
        return pair[:, low:low + 8].reshape(128, 128).astype(bf16)

    def spot(tap, v):
        a, b = tap // 3, tap % 3
        at = (3 * (a + v) + b) * 128
        return slice(at, at + 128)

    halves = (slice(0, 128), slice(128, 256))
    for v in range(2):
        r1[halves[v], halves[v]] = block(12)
    w3[...] = block(11)
    wide = dot(block(13), repeat[:, :9 * 128]).astype(bf16)
    for tap in range(TAPS):
        for v in range(2):
            r2[spot(tap, v), halves[v]] = wide[:, tap * 128:(tap + 1) * 128]
    w1[:, :128] = block(9)
    w1[:, 128:] = block(10)
    for tap in range(TAPS):
        part = block(tap)
        for v in range(2):
            w2[halves[v], spot(tap, v)] = part
            w2t[spot(8 - tap, v), halves[v]] = part
    wide = dot(w3[...], repeat[...]).astype(bf16)
    for tap in range(TAPS):
        for v in range(2):
            w3r[spot(tap, v), halves[v]] = wide[:, tap * 128:(tap + 1) * 128]
    for v in range(2):
        w3f[halves[v], halves[v]] = wide[:, 9 * 128:]

    def cells(value):
        return value.reshape(-1, PLANES, SUB, 128)

    def flat(value):
        return value.reshape(-1, 128)

    def sweep(count, n, body):
        @pl.loop(0, count // n)
        def _(k):
            body(k * n, n)

        if count % n:
            body(count // n * n, count % n)

    def clear(ref):
        @pl.when(first_row < 0)
        def _():
            ref[0:4] = jnp.zeros((4, 2, PLANES + 2, SUB, 128), bf16)

        @pl.when(first_row + 32 > NH)
        def _():
            ref[12:16] = jnp.zeros((4, 2, PLANES + 2, SUB, 128), bf16)

    def reg_one(k, n):
        both = jnp.concatenate([flat(some(cond_taps, 2 + v, k, n, 2)[...]) for v in range(2)], 1)
        value = dot(both, r1[...], 1, 1)
        for v in range(2):
            x = value[:, halves[v]]
            put_pair(hid, 2 + v, k, n, cells(x * sigmoid(x)) * inside[...])

    sweep(14, 7, reg_one)
    clear(hid)

    def reg_two(k, n):
        value = dot(stack_rows(hid, 3, k, n), r2[...])
        for v in range(2):
            row = 3 + v
            mean = cells(value[:, halves[v]]).astype(bf16).astype(f32)
            both = dot(flat(some(fields, row, k, n, 3)[...]), spread[...])
            noised = cells(both[:, halves[0]]) - mean
            some(draw, row, k, n, 3)[...] = cells(both[:, halves[1]])
            some(noisy, row, k, n, 3)[...] = noised
            put_pair(inp, row, k, n, in_coef * noised * inside[...])

    for copy in copies:
        copy.wait()
    level = index[0]
    sigma, skip, out_coef = table[level, 0], table[level, 1], table[level, 2]
    in_coef, noise_coef, delta_coef = table[level, 3], table[level, 4], table[level, 5]
    lane = lax.broadcasted_iota(jnp.int32, (16, 128), 1)
    pick_film = jnp.where(lane == FILM_LANE, 1.0, 0.0).astype(bf16)
    gain = 1.0 + noise_coef * dot(pick_film, w3[...], 1, 1)[0:1]
    sweep(13, 13, reg_two)
    clear(inp)

    def conv_one(k, n):
        for v in range(2):
            row = 4 + v
            picked = pick_pair(inp, row, k, n)
            some(taps_in, row, k, n, 4)[...] = picked
            both = jnp.concatenate([flat(picked), flat(some(cond_taps, row, k, n, 2)[...])], 1)
            value = dot(both, w1[...], 1, 1)
            some(act, row, k, n, 4)[...] = cells(value)
            u = value * gain
            put_pair(one, row, k, n, cells(u * sigmoid(u)) * inside[...])

    sweep(12, 6, conv_one)
    clear(one)

    def conv_two(k, n):
        value = dot(stack_rows(one, 5, k, n), w2[...], 1, 1)
        for v in range(2):
            x = value[:, halves[v]]
            s = sigmoid(x)
            some(slope, 5 + v, k, n, 5)[...] = cells(s * (1.0 + x * (1.0 - s)))
            put_pair(two, 5 + v, k, n, cells(x * s) * inside[...])

    sweep(11, 11, conv_two)
    clear(two)

    def conv_three(k, n):
        value = dot(stack_rows(two, 6, k, n), w3r[...])
        for v in range(2):
            row = 6 + v
            noised = some(noisy, row, k, n, 3)[...]
            full = skip * noised + out_coef * cells(value[:, halves[v]])
            some(den, row, k, n, 6)[:, :PLANES] = full.astype(bf16)
            delta = delta_coef * (full - (noised - sigma * some(draw, row, k, n, 3)[...]))
            put_pair(dlt, row, k, n, delta * inside[...])

    sweep(10, 5, conv_three)
    clear(dlt)

    def delta_two(k, n):
        parts = []
        for v in range(2):
            picked = pick_pair(dlt, 7 + v, k, n)
            some(taps_d, 7 + v, k, n, 7)[...] = picked
            parts.append(flat(picked))
        value = dot(jnp.concatenate(parts, axis=1), w3f[...], 1, 1)
        for v in range(2):
            x = cells(value[:, halves[v]]) * some(slope, 7 + v, k, n, 5)[...]
            put_pair(sdl, 7 + v, k, n, x * inside[...])

    sweep(9, 9, delta_two)
    clear(sdl)
    film_sum[...] = jnp.zeros((8, 128), f32)

    def delta_one(k, n):
        value = dot(stack_rows(sdl, 8, k, n), w2t[...])
        for v in range(2):
            a = flat(some(act, 8 + v, k, n, 4)[...])
            u = a * gain
            s = sigmoid(u)
            g = flat(cells(value[:, halves[v]] * (s * (1.0 + u * (1.0 - s)))) * tile)
            film_sum[...] += jnp.sum((g * a).reshape(-1, 8, 128), axis=0)
            some(grad1, 8 + v, k, n, 8)[...] = cells(g * gain).astype(bf16)

    sweep(8, 8, delta_one)

    tile_low = tile.astype(bf16)

    def both_rows(read):
        return jnp.concatenate([read(8), read(9)], axis=0)

    def own_cells(ref):
        return lambda row: flat(some(ref, row, 0, 8)[:, 1:PLANES + 1] * tile_low)

    def own_field(ref, base):
        return lambda row: flat(some(ref, row, 0, 8, base)[...])

    def taps_of(row):
        return jnp.concatenate([flat(some(one, row + a - 1, 0, 8)[:, b:b + PLANES])
                                for a in range(3) for b in range(3)], axis=1)

    def first_taps(row):
        return jnp.concatenate([own_field(taps_in, 4)(row), own_field(cond_taps, 2)(row)], axis=1)

    g2 = dot(both_rows(own_cells(sdl)), both_rows(taps_of), 0, 0)
    g1 = dot(both_rows(own_field(grad1, 8)), both_rows(first_taps), 0, 0)
    g3 = dot(both_rows(own_cells(two)), both_rows(own_field(taps_d, 7)), 0, 0)
    film = noise_coef * jnp.sum(film_sum[...], axis=0, keepdims=True)
    film = jnp.transpose(jnp.broadcast_to(film, (8, 128)))[:, 0:1]
    g3 = jnp.where(lax.broadcasted_iota(jnp.int32, (128, 128), 1) == FILM_LANE, film, g3)
    parts = [g2[:, k * 128:(k + 1) * 128] for k in range(9)] + [g1[:, :128], g1[:, 128:], g3]
    for p in range(6):
        pair = [part.reshape(16, 8, 128) for part in parts[2 * p:2 * p + 2]]
        out[:, p * 16:(p + 1) * 16, :] = jnp.concatenate(pair, axis=1).astype(bf16)

    fields = (lax.broadcasted_iota(jnp.int32, (16, 128), 0)
              == lax.broadcasted_iota(jnp.int32, (16, 128), 1)).astype(f32).astype(bf16)
    turned = dot(fields, den[1:9].reshape(16 * 128, 128), 1, 1).astype(bf16)
    turned = jnp.concatenate([turned[:, i * 128:(i + 1) * 128] for i in range(16)], axis=0)
    den_rows[...] = dot(turned, back[...])
    for c in range(6):
        left = den_rows[pl.ds(c, 16, stride=16), :]
        right = den_rows[pl.ds(c + 6, 16, stride=16), :]
        piece = jnp.where(lane < TW, left, right).astype(bf16)
        out[:, 96 + c * 16:96 + (c + 1) * 16, :] = jnp.broadcast_to(piece[None], (16, 16, 128))


def fold_kernel(parts, out):
    for p in range(6):
        total = jnp.sum(parts[:, p * 16:(p + 1) * 16, :].astype(f32), axis=0).astype(bf16)
        for q in range(8):
            out[q, p * 16:(p + 1) * 16, :] = total


def field_kernel(parts, out):
    for k in range(8):
        for c in range(6):
            a = parts[2 * k, 96 + c * 16:96 + (c + 1) * 16, :].astype(f32)
            b = parts[2 * k + 1, 96 + c * 16:96 + (c + 1) * 16, :].astype(f32)
            cols = slice(k * 128, (k + 1) * 128)
            out[c, :, cols] = jnp.concatenate([a[:, :TW], b[:, :TW]], axis=1).astype(bf16)
            out[c + 6, :, cols] = jnp.concatenate([a[:, TW:], b[:, TW:]], axis=1).astype(bf16)


def finish_kernel(parts, g1, g2, g3, film):
    def block(k):
        pair = jnp.sum(parts[:, (k // 2) * 16:(k // 2 + 1) * 16, :].astype(f32), axis=0)
        return pair[(k % 2) * 8:(k % 2) * 8 + 8]

    low, high, third = block(9), block(10), block(11)
    for a in range(3):
        for b in range(3):
            tap = 3 * a + b
            lanes = slice(tap * COUT, (tap + 1) * COUT)
            g2[a, b] = block(tap)
            g1[a, b, :, :COUT] = low[:, lanes]
            g1[a, b, :, COUT:] = high[:, lanes]
            g3[a, b] = third[:, (8 - tap) * COUT:(9 - tap) * COUT]
    film[...] = jnp.transpose(third)[FILM_LANE:FILM_LANE + 1]


VMEM = pl.BlockSpec(memory_space=pltpu.VMEM)
ANY = pl.BlockSpec(memory_space=pl.ANY)


def kernel_call(body, ins, outs, scratch=(), limit=16, cost=None):
    return pl.pallas_call(
        body,
        in_specs=list(ins),
        out_specs=[VMEM] * len(outs),
        out_shape=[jax.ShapeDtypeStruct(shape, dtype) for shape, dtype in outs],
        scratch_shapes=list(scratch),
        compiler_params=pltpu.CompilerParams(vmem_limit_bytes=limit * MIB),
        cost_estimate=cost,
    )


def planes(rows, dtype, count=PLANES):
    return pltpu.VMEM((rows, count, SUB, 128), dtype)


def pairs(rows, dtype, count=PLANES):
    return pltpu.VMEM((rows // 2, 2, count, SUB, 128), dtype)


def shards(condition, target, noise_draw, sigma_index, reg_first, reg_second, first_kernel,
           second_kernel, third_kernel, film_scale):
    order, back, spread, repeat = place_constants()
    table = jnp.asarray(coef_table())
    last, leading, packed = kernel_call(
        pack_kernel, [ANY] * 11,
        [((36, 8, 128), bf16), ((36, 8, 128), bf16), ((16, 112, 128), bf16)],
        [pltpu.SMEM((1,), jnp.int32), pltpu.SMEM((NSIG, 8), f32),
         pltpu.VMEM((3, COUT, 16, 256), f32), pltpu.VMEM((3, 3, 8, 24), bf16),
         pltpu.VMEM((3, 3, 8, 128), bf16), pltpu.VMEM((3, 3, 8, 12), bf16),
         pltpu.VMEM((3, 3, 12, 16), bf16), pltpu.VMEM((3, 3, 16, 12), bf16),
         pltpu.VMEM((1, 8), bf16), pltpu.SemaphoreType.DMA((11,))],
        limit=60,
    )(sigma_index, table, condition, target, noise_draw, jnp.swapaxes(first_kernel, 2, 3),
      jnp.swapaxes(second_kernel, 2, 3), third_kernel, reg_first, reg_second,
      film_scale.reshape(1, 8))
    up = [(i, i + 1) for i in range(lax.axis_size("rows") - 1)]
    before = lax.ppermute(last, "rows", up)
    after = lax.ppermute(leading, "rows", [(j, i) for i, j in up])
    gathered = lax.all_to_all(packed, GROUP, 0, 0, tiled=True)
    cond_taps, fields = kernel_call(
        prep_kernel, [ANY] * 5 + [VMEM] * 2 + [ANY] * 2,
        [((14, 2, PLANES, SUB, 128), bf16), ((13, 2, PLANES, SUB, 128), bf16)],
        [pltpu.SMEM((1,), jnp.int32), pltpu.SMEM((NSIG, 8), f32),
         pltpu.VMEM((48, 32, 128), f32), pltpu.VMEM((3, COUT, 16, 256), f32),
         planes(32, bf16, 7), pltpu.VMEM((30 * WIN, 128), bf16), pltpu.VMEM((WIN, 128), bf16), pltpu.VMEM((128, 128), bf16),
         pltpu.SemaphoreType.DMA((7,))],
        limit=52,
        cost=pl.CostEstimate(flops=1 << 32, bytes_accessed=8 * MIB, transcendentals=0),
    )(sigma_index, table, condition, target, noise_draw, before, after, jnp.asarray(order, bf16), jnp.asarray(spread[:, :128], bf16))
    wide = [pairs(32, bf16, PLANES + 2) for _ in range(6)]
    out, = kernel_call(
        step_kernel, [ANY] * 3 + [VMEM] * 5, [((16, 192, 128), bf16)],
        [pltpu.SMEM((1,), jnp.int32), pltpu.SMEM((NSIG, 8), f32), pairs(26, bf16),
         pltpu.SemaphoreType.DMA((3,)), pltpu.VMEM((256, 1536), bf16),
         pltpu.VMEM((1536, 256), bf16), pltpu.VMEM((128, 256), bf16),
         pltpu.VMEM((128, 128), bf16), pltpu.VMEM((256, 256), bf16),
         pltpu.VMEM((1536, 256), bf16), pltpu.VMEM((256, 256), bf16),
         pltpu.VMEM((1536, 256), bf16)]
        + wide
        + [pairs(24, bf16), pairs(18, bf16), pairs(26, f32), pairs(26, f32),
           pairs(24, f32), pairs(22, f32), pairs(20, bf16, 8), pairs(16, bf16),
           pltpu.VMEM((8, 128), f32), pltpu.VMEM((256, 128), f32),
           pltpu.VMEM((PLANES, SUB, 128), f32)],
        limit=52,
    )(sigma_index, table, fields, cond_taps, gathered, jnp.asarray(repeat, bf16),
      jnp.asarray(back, bf16), jnp.asarray(spread[:, 128:], bf16))
    parts = lax.all_to_all(out, GROUP, 0, 0, tiled=True)
    folded, = kernel_call(fold_kernel, [VMEM], [((8, 96, 128), bf16)])(parts)
    denoised, = kernel_call(
        field_kernel, [VMEM], [((COUT, 16, NW), bf16)],
        cost=pl.CostEstimate(flops=1 << 26, bytes_accessed=2 * MIB, transcendentals=0),
    )(parts)
    sums = lax.all_to_all(folded, "rows", 0, 0, tiled=True)
    g1, g2, g3, film = kernel_call(
        finish_kernel, [VMEM],
        [((3, 3, 8, 24), f32), ((3, 3, 8, 128), f32), ((3, 3, 8, 12), f32), ((1, 8), f32)],
    )(sums)
    return denoised, jnp.swapaxes(g1, 2, 3), jnp.swapaxes(g2, 2, 3), g3, film.reshape(8)


def solution(mesh):
    return jax.shard_map(
        shards,
        mesh=mesh,
        in_specs=(
            P(None, "rows", None),
            P(None, "rows", None),
            P(None, "rows", None),
            P(),
            P(None, None, None, "chan"),
            P(None, None, "chan", None),
            P(None, None, None, GROUP),
            P(None, None, None, GROUP),
            P(None, None, GROUP, None),
            P(GROUP),
        ),
        out_specs=(
            P(None, "rows", None),
            P(None, None, None, GROUP),
            P(None, None, None, GROUP),
            P(None, None, GROUP, None),
            P(GROUP),
        ),
        check_vma=False,
    )
```

```python
import math

import numpy as np
import jax
import jax.numpy as jnp
from jax import lax
from jax.experimental import pallas as pl
from jax.experimental.pallas import tpu as pltpu
from jax.sharding import PartitionSpec as P

COUT = 12
NSIG = 32
NH = 128
NW = 1024
TW = 64
RIM = 8
PLANES = 5
SUB = 16
WIN = PLANES * SUB
TAPS = 9
FILM_LANE = 120
MIB = 1024 * 1024
GROUP = ("section", "chan")
f32 = jnp.float32
bf16 = jnp.bfloat16


def coef_table():
    i = np.arange(NSIG, dtype=np.float64)
    high, low = 4.0 ** (1 / 7), 0.25 ** (1 / 7)
    level = (high + i / (NSIG - 1) * (low - high)) ** 7
    total = level**2 + 0.25
    out_coef = 0.5 * level / np.sqrt(total)
    weight = total / (0.5 * level) ** 2
    table = np.zeros((NSIG, 8), np.float32)
    table[:, 0] = level
    table[:, 1] = 0.25 / total
    table[:, 2] = out_coef
    table[:, 3] = 1 / np.sqrt(total)
    table[:, 4] = np.log(8 * level) / 4
    table[:, 5] = 2 * weight * out_coef / math.sqrt(COUT * NH * NW)
    return table


def place_constants():
    order = np.zeros((WIN, 128), np.float32)
    back = np.zeros((128, 128), np.float32)
    for t in range(PLANES):
        for s in range(SUB):
            col = PLANES * s + t
            order[t * SUB + s, col] = 1
            if RIM <= col < RIM + TW:
                back[t * SUB + s, col - RIM] = 1
                back[t * SUB + s, TW + col - RIM] = 1
    spread = np.zeros((128, 384), np.float32)
    repeat = np.zeros((128, 10 * 128), np.float32)
    for c in range(COUT):
        for g in range(TAPS):
            spread[24 + c, g * COUT + c] = 1
            for first in (0, 48, 80):
                spread[first + c, 128 + g * COUT + c] = 1
                spread[first + COUT + c, 256 + g * COUT + c] = 1
            for tap in range(TAPS):
                repeat[tap * COUT + c, tap * 128 + g * COUT + c] = 1
            repeat[(8 - g) * COUT + c, 9 * 128 + g * COUT + c] = 1
    return order, back, spread, repeat


def dot(a, b, ca=1, cb=0):
    return lax.dot_general(a, b, (((ca,), (cb,)), ((), ())), preferred_element_type=f32)


def sigmoid(v):
    return 0.5 * jnp.tanh(0.5 * v) + 0.5


def member():
    return lax.axis_index("section") * lax.axis_size("chan") + lax.axis_index("chan")


def window_place():
    start = member() * TW - RIM
    base = jnp.clip((start + 128) // 128 * 128 - 128, 0, NW - 256)
    return start, pl.multiple_of(base, 128)


def window_copy(src, dst, sem):
    copy = pltpu.make_async_copy(src.at[:, :, pl.ds(window_place()[1], 256)], dst, sem)
    copy.start()
    return copy


def window(wide):
    start, base = window_place()
    rows = pltpu.roll(wide.reshape(COUT * 16, 256), lax.rem(512 - (start - base), 256), 1)
    rows = rows[:, :128]
    col = start + lax.broadcasted_iota(jnp.int32, rows.shape, 1)
    return jnp.where((col >= 0) & (col < NW), rows, 0.0).reshape(COUT, 16, 128)


def scalar_copies(index_any, table_any, index, table, sem_a, sem_b):
    copies = [pltpu.make_async_copy(index_any, index, sem_a),
              pltpu.make_async_copy(table_any, table, sem_b)]
    for copy in copies:
        copy.start()
    return copies


def send(ref, field, low):
    high = field.astype(bf16)
    ref[:COUT] = high
    ref[COUT:2 * COUT] = (field - high.astype(f32)).astype(bf16)
    ref[2 * COUT:] = low.astype(bf16)


def pack_kernel(index_any, table_any, cond, target, noise, w1_any, w2_any, w3_any, r1_any,
                r2_any, film_any, last, leading, packed,
                index, table, scr, w1, w2, w3, r1, r2, film, sems):
    scalars = scalar_copies(index_any, table_any, index, table, sems.at[9], sems.at[10])
    small = []
    for k, (src, dst) in enumerate(((w2_any, w2), (w1_any, w1), (w3_any, w3), (r1_any, r1),
                                    (r2_any, r2), (film_any, film))):
        small.append(pltpu.make_async_copy(src, dst, sems.at[k]))
        small[-1].start()
    copies = [window_copy(src, scr.at[k], sems.at[6 + k])
              for k, src in enumerate((target, noise, cond))]
    half = lax.axis_index("section") == 0
    eye = (lax.broadcasted_iota(jnp.int32, (8, 8), 0)
           == lax.broadcasted_iota(jnp.int32, (8, 8), 1)).astype(f32)
    for copy in copies + scalars:
        copy.wait()
    draw = window(scr[1])
    noised = window(scr[0]) + table[index[0], 0] * draw
    low = window(scr[2])
    row = lax.broadcasted_iota(jnp.int32, (COUT, 8, 128), 1)
    send(last, jnp.where(row < 2, pltpu.roll(draw[:, 8:], 2, 1), noised[:, 8:]), low[:, 8:])
    send(leading, jnp.where(row >= 6, pltpu.roll(draw[:, :8], 6, 1), noised[:, :8]), low[:, :8])
    for copy in small:
        copy.wait()

    def place(n, at):
        lane = lax.broadcasted_iota(jnp.int32, (n, 128), 1)
        row = lax.broadcasted_iota(jnp.int32, (n, 128), 0)
        return jnp.where((lane - row == at) & (row < COUT), 1.0, 0.0)

    first_in = jnp.zeros((8, 128), f32)
    first_cond = jnp.zeros((8, 128), f32)
    third = jnp.zeros((8, 128), f32)
    reg_a = jnp.zeros((16, 128), f32)
    reg_b = jnp.zeros((16, 128), f32)
    blocks = []
    for a in range(3):
        for b in range(3):
            tap = 3 * a + b
            low = place(COUT, tap * COUT)
            lane = lax.broadcasted_iota(jnp.int32, (24, 128), 1)
            row = lax.broadcasted_iota(jnp.int32, (24, 128), 0)
            low_in = jnp.where((lane - row == tap * COUT) & (row < COUT), 1.0, 0.0)
            low_cond = jnp.where((lane - row == (tap - 1) * COUT) & (row >= COUT), 1.0, 0.0)
            blocks.append(w2[a, b].astype(f32))
            first_in += dot(w1[a, b].astype(f32), low_in)
            first_cond += dot(w1[a, b].astype(f32), low_cond)
            third += dot(w3[a, b].astype(f32), low)
            reg_a += dot(r1[a, b].astype(f32), low, 0, 0)
            reg_b += dot(r2[a, b].astype(f32), low)
    lane = lax.broadcasted_iota(jnp.int32, (8, 128), 1)
    film_col = jnp.sum(eye * film[...].astype(f32), axis=1, keepdims=True)
    third = jnp.where(lane == FILM_LANE, film_col, third)
    blocks += [first_in, first_cond, third,
               jnp.where(half, reg_a[:8], reg_a[8:]), jnp.where(half, reg_b[:8], reg_b[8:])]
    for p in range(7):
        pair = jnp.concatenate(blocks[2 * p:2 * p + 2], axis=0).astype(bf16)
        for q in range(16):
            packed[q, p * 16:(p + 1) * 16, :] = pair


def put(ref, at, n, value):
    ref[pl.ds(at, n), 1:PLANES + 1] = value.astype(bf16)
    ref[pl.ds(at, n), 0] = pltpu.roll(value[:, PLANES - 1], 1, 1).astype(bf16)
    ref[pl.ds(at, n), PLANES + 1] = pltpu.roll(value[:, 0], SUB - 1, 1).astype(bf16)


def pick_taps(ref, at, n):
    lane = lax.broadcasted_iota(jnp.int32, (SUB, 128), 1)
    total = None
    for a in range(3):
        for b in range(3):
            low = (3 * a + b) * COUT
            mask = jnp.where((lane >= low) & (lane < low + COUT), 1.0, 0.0).astype(bf16)
            part = ref[pl.ds(at + a - 1, n), b:b + PLANES] * mask[None, None]
            total = part if total is None else total + part
    return total


def prep_kernel(index_any, table_any, cond, target, noise, before, after, order_any, spread_any,
                cond_taps, fields, index, table, scr, wide, cond9, cells, order, spread, sems):
    copies = [window_copy(src, wide.at[k], sems.at[k])
              for k, src in enumerate((target, noise, cond))]
    others = [
        pltpu.make_async_copy(order_any, order, sems.at[3]),
        pltpu.make_async_copy(spread_any, spread, sems.at[4]),
    ]
    for copy in others:
        copy.start()
    scalars = scalar_copies(index_any, table_any, index, table, sems.at[5], sems.at[6])
    scr[36:48] = jnp.zeros((12, 32, 128), f32)
    for src, rows, shift in ((before, slice(0, 8), 6), (after, slice(24, 32), 2)):
        field = src[:COUT].astype(f32) + src[COUT:2 * COUT].astype(f32)
        scr[0:12, rows] = field
        scr[12:24, rows] = pltpu.roll(field, shift, 1)
        scr[24:36, rows] = src[2 * COUT:].astype(f32)
    for copy in copies + scalars:
        copy.wait()
    draw = window(wide[1])
    scr[0:12, 8:24] = window(wide[0]) + table[index[0], 0] * draw
    scr[12:24, 8:24] = draw
    scr[24:36, 8:24] = window(wide[2])
    for copy in others:
        copy.wait()
    flat = scr.reshape(48 * 32, 128)

    for i in range(1, 31):
        x = flat[pl.ds(i, 48, stride=32), :]
        high = x.astype(bf16)
        rest = x[:32] - high[:32].astype(f32)
        mid = rest.astype(bf16)
        low = (rest - mid.astype(f32)).astype(bf16)
        rows = jnp.concatenate([high, mid, low, jnp.zeros((16, 128), bf16)], axis=0)
        turned = dot(order[...], rows, 1, 1).astype(bf16)
        cells[(i - 1) * WIN:i * WIN] = turned
        if 3 <= i < 29:
            fields[(i - 3) // 2, (i - 3) % 2] = turned.reshape(PLANES, SUB, 128)
    count = 6
    for i in range(1, 31, count):
        wide = dot(cells[(i - 1) * WIN:(i - 1 + count) * WIN], spread[...])
        put(cond9, i, count, wide.reshape(count, PLANES, SUB, 128))

    @pl.loop(0, 7)
    def _(k):
        at = 2 + 4 * k
        cond_taps[pl.ds(2 * k, 2)] = pick_taps(cond9, at, 4).reshape(2, 2, PLANES, SUB, 128)


def some(ref, row, k, n, base=0):
    return ref.at[pl.ds((row - base) // 2 + k, n), (row - base) % 2]


def put_pair(ref, row, k, n, value):
    dst = some(ref, row, k, n)
    dst[:, 1:PLANES + 1] = value.astype(bf16)
    dst[:, 0] = pltpu.roll(value[:, PLANES - 1], 1, 1).astype(bf16)
    dst[:, PLANES + 1] = pltpu.roll(value[:, 0], SUB - 1, 1).astype(bf16)


def stack_rows(ref, row, k, n):
    parts = []
    for u in range(4):
        src = some(ref, row + u - 1, k, n)
        for b in range(3):
            parts.append(src[:, b:b + PLANES].reshape(n * WIN, 128))
    return jnp.concatenate(parts, axis=1)


def pick_pair(ref, row, k, n):
    lane = lax.broadcasted_iota(jnp.int32, (SUB, 128), 1)
    parts = []
    for a in range(3):
        src = some(ref, row + a - 1, k, n)
        for b in range(3):
            low = (3 * a + b) * COUT
            part = src[:, b:b + PLANES]
            here = lane[None, None] < low + COUT
            parts.append((part, here))
    total = parts[8][0] * jnp.where(lane < TAPS * COUT, 1.0, 0.0).astype(bf16)[None, None]
    for part, here in parts[7::-1]:
        total = jnp.where(here, part, total)
    return total


def step_kernel(index_any, table_any, field_any, cond_taps, gathered, repeat, back, spread, out,
                index, table, fields, sems,
                w2, w2t, w1, w3, w3f, w3r, r1, r2,
                hid, inp, one, two, dlt, sdl, taps_in, taps_d, draw, noisy, act, slope,
                den, grad1, film_sum, den_rows, inside):
    copies = scalar_copies(index_any, table_any, index, table, sems.at[0], sems.at[1])
    copies.append(pltpu.make_async_copy(field_any, fields, sems.at[2]))
    copies[-1].start()
    first_row = lax.axis_index("rows") * 16 - RIM
    first_col = member() * TW - RIM
    unused = (slice(9 * 128, 12 * 128), slice(0, 3 * 128))
    for v in range(2):
        w2[v * 128:(v + 1) * 128, unused[v]] = jnp.zeros((128, 384), bf16)
        for ref in (w2t, w3r, r2):
            ref[unused[v], v * 128:(v + 1) * 128] = jnp.zeros((384, 128), bf16)
    for ref in (r1, w3f):
        ref[...] = jnp.zeros(ref.shape, bf16)
    den[:, :, PLANES:] = jnp.zeros((10, 2, 8 - PLANES, SUB, 128), bf16)
    shape = (PLANES, SUB, 128)
    col = (lax.broadcasted_iota(jnp.int32, shape, 1) * PLANES
           + lax.broadcasted_iota(jnp.int32, shape, 0))
    inside[...] = jnp.where((col + first_col >= 0) & (col + first_col < NW), 1.0, 0.0)
    tile = jnp.where((col >= RIM) & (col < RIM + TW), 1.0, 0.0)

    def block(k):
        pair = gathered[:, (k // 2) * 16:(k // 2 + 1) * 16, :].astype(f32)
        low = (k % 2) * 8
        return pair[:, low:low + 8].reshape(128, 128).astype(bf16)

    def spot(tap, v):
        a, b = tap // 3, tap % 3
        at = (3 * (a + v) + b) * 128
        return slice(at, at + 128)

    halves = (slice(0, 128), slice(128, 256))
    for v in range(2):
        r1[halves[v], halves[v]] = block(12)
    w3[...] = block(11)
    wide = dot(block(13), repeat[:, :9 * 128]).astype(bf16)
    for tap in range(TAPS):
        for v in range(2):
            r2[spot(tap, v), halves[v]] = wide[:, tap * 128:(tap + 1) * 128]
    w1[:, :128] = block(9)
    w1[:, 128:] = block(10)
    for tap in range(TAPS):
        part = block(tap)
        for v in range(2):
            w2[halves[v], spot(tap, v)] = part
            w2t[spot(8 - tap, v), halves[v]] = part
    wide = dot(w3[...], repeat[...]).astype(bf16)
    for tap in range(TAPS):
        for v in range(2):
            w3r[spot(tap, v), halves[v]] = wide[:, tap * 128:(tap + 1) * 128]
    for v in range(2):
        w3f[halves[v], halves[v]] = wide[:, 9 * 128:]

    def cells(value):
        return value.reshape(-1, PLANES, SUB, 128)

    def flat(value):
        return value.reshape(-1, 128)

    def sweep(count, n, body):
        @pl.loop(0, count // n)
        def _(k):
            body(k * n, n)

        if count % n:
            body(count // n * n, count % n)

    def clear(ref):
        zero = jnp.zeros((4, 2, PLANES + 2, SUB, 128), bf16)
        ref[pl.ds(jnp.where(first_row < 0, 0, 16), 4)] = zero
        ref[pl.ds(jnp.where(first_row + 32 > NH, 12, 16), 4)] = zero

    def reg_one(k, n):
        both = jnp.concatenate([flat(some(cond_taps, 2 + v, k, n, 2)[...]) for v in range(2)], 1)
        value = dot(both, r1[...], 1, 1)
        for v in range(2):
            x = value[:, halves[v]]
            put_pair(hid, 2 + v, k, n, cells(x * sigmoid(x)) * inside[...])

    sweep(14, 14, reg_one)
    clear(hid)

    def reg_two(k, n):
        value = dot(stack_rows(hid, 3, k, n), r2[...])
        for v in range(2):
            row = 3 + v
            mean = cells(value[:, halves[v]]).astype(bf16).astype(f32)
            both = dot(flat(some(fields, row, k, n, 3)[...]), spread[...])
            noised = cells(both[:, halves[0]]) - mean
            some(draw, row, k, n, 3)[...] = cells(both[:, halves[1]])
            some(noisy, row, k, n, 3)[...] = noised
            put_pair(inp, row, k, n, in_coef * noised * inside[...])

    for copy in copies:
        copy.wait()
    level = index[0]
    sigma, skip, out_coef = table[level, 0], table[level, 1], table[level, 2]
    in_coef, noise_coef, delta_coef = table[level, 3], table[level, 4], table[level, 5]
    lane = lax.broadcasted_iota(jnp.int32, (16, 128), 1)
    pick_film = jnp.where(lane == FILM_LANE, 1.0, 0.0).astype(bf16)
    gain = 1.0 + noise_coef * dot(pick_film, w3[...], 1, 1)[0:1]
    sweep(13, 13, reg_two)
    clear(inp)

    def conv_one(k, n):
        for v in range(2):
            row = 4 + v
            picked = pick_pair(inp, row, k, n)
            some(taps_in, row, k, n, 4)[...] = picked
            both = jnp.concatenate([flat(picked), flat(some(cond_taps, row, k, n, 2)[...])], 1)
            value = dot(both, w1[...], 1, 1)
            some(act, row, k, n, 4)[...] = cells(value)
            u = value * gain
            put_pair(one, row, k, n, cells(u * sigmoid(u)) * inside[...])

    sweep(12, 6, conv_one)
    clear(one)

    def conv_two(k, n):
        value = dot(stack_rows(one, 5, k, n), w2[...], 1, 1)
        for v in range(2):
            x = value[:, halves[v]]
            s = sigmoid(x)
            some(slope, 5 + v, k, n, 5)[...] = cells(s * (1.0 + x * (1.0 - s)))
            put_pair(two, 5 + v, k, n, cells(x * s) * inside[...])

    sweep(11, 11, conv_two)
    clear(two)

    def conv_three(k, n):
        value = dot(stack_rows(two, 6, k, n), w3r[...])
        for v in range(2):
            row = 6 + v
            noised = some(noisy, row, k, n, 3)[...]
            full = skip * noised + out_coef * cells(value[:, halves[v]])
            some(den, row, k, n, 6)[:, :PLANES] = full.astype(bf16)
            delta = delta_coef * (full - (noised - sigma * some(draw, row, k, n, 3)[...]))
            put_pair(dlt, row, k, n, delta * inside[...])

    sweep(10, 5, conv_three)
    clear(dlt)

    def delta_two(k, n):
        parts = []
        for v in range(2):
            picked = pick_pair(dlt, 7 + v, k, n)
            some(taps_d, 7 + v, k, n, 7)[...] = picked
            parts.append(flat(picked))
        value = dot(jnp.concatenate(parts, axis=1), w3f[...], 1, 1)
        for v in range(2):
            x = cells(value[:, halves[v]]) * some(slope, 7 + v, k, n, 5)[...]
            put_pair(sdl, 7 + v, k, n, x * inside[...])

    sweep(9, 9, delta_two)
    clear(sdl)
    film_sum[...] = jnp.zeros((8, 128), f32)

    def delta_one(k, n):
        value = dot(stack_rows(sdl, 8, k, n), w2t[...])
        for v in range(2):
            a = flat(some(act, 8 + v, k, n, 4)[...])
            u = a * gain
            s = sigmoid(u)
            g = flat(cells(value[:, halves[v]] * (s * (1.0 + u * (1.0 - s)))) * tile)
            film_sum[...] += jnp.sum((g * a).reshape(-1, 8, 128), axis=0)
            some(grad1, 8 + v, k, n, 8)[...] = cells(g * gain).astype(bf16)

    sweep(8, 8, delta_one)

    tile_low = tile.astype(bf16)

    def both_rows(read):
        return jnp.concatenate([read(8), read(9)], axis=0)

    def own_cells(ref):
        return lambda row: flat(some(ref, row, 0, 8)[:, 1:PLANES + 1] * tile_low)

    def own_field(ref, base):
        return lambda row: flat(some(ref, row, 0, 8, base)[...])

    def taps_of(row):
        return jnp.concatenate([flat(some(one, row + a - 1, 0, 8)[:, b:b + PLANES])
                                for a in range(3) for b in range(3)], axis=1)

    def first_taps(row):
        return jnp.concatenate([own_field(taps_in, 4)(row), own_field(cond_taps, 2)(row)], axis=1)

    g2 = dot(both_rows(own_cells(sdl)), both_rows(taps_of), 0, 0)
    g1 = dot(both_rows(own_field(grad1, 8)), both_rows(first_taps), 0, 0)
    g3 = dot(both_rows(own_cells(two)), both_rows(own_field(taps_d, 7)), 0, 0)
    film = noise_coef * jnp.sum(film_sum[...], axis=0, keepdims=True)
    film = jnp.transpose(jnp.broadcast_to(film, (8, 128)))[:, 0:1]
    g3 = jnp.where(lax.broadcasted_iota(jnp.int32, (128, 128), 1) == FILM_LANE, film, g3)
    parts = [g2[:, k * 128:(k + 1) * 128] for k in range(9)] + [g1[:, :128], g1[:, 128:], g3]
    for p in range(6):
        pair = [part.reshape(16, 8, 128) for part in parts[2 * p:2 * p + 2]]
        out[:, p * 16:(p + 1) * 16, :] = jnp.concatenate(pair, axis=1).astype(bf16)

    fields = (lax.broadcasted_iota(jnp.int32, (16, 128), 0)
              == lax.broadcasted_iota(jnp.int32, (16, 128), 1)).astype(f32).astype(bf16)
    turned = dot(fields, den[1:9].reshape(16 * 128, 128), 1, 1).astype(bf16)
    turned = jnp.concatenate([turned[:, i * 128:(i + 1) * 128] for i in range(16)], axis=0)
    den_rows[...] = dot(turned, back[...])
    for c in range(6):
        left = den_rows[pl.ds(c, 16, stride=16), :]
        right = den_rows[pl.ds(c + 6, 16, stride=16), :]
        piece = jnp.where(lane < TW, left, right).astype(bf16)
        out[:, 96 + c * 16:96 + (c + 1) * 16, :] = jnp.broadcast_to(piece[None], (16, 16, 128))


def fold_kernel(parts, out):
    for p in range(6):
        total = jnp.sum(parts[:, p * 16:(p + 1) * 16, :].astype(f32), axis=0).astype(bf16)
        for q in range(8):
            out[q, p * 16:(p + 1) * 16, :] = total


def field_kernel(parts, out):
    for k in range(8):
        for c in range(6):
            a = parts[2 * k, 96 + c * 16:96 + (c + 1) * 16, :].astype(f32)
            b = parts[2 * k + 1, 96 + c * 16:96 + (c + 1) * 16, :].astype(f32)
            cols = slice(k * 128, (k + 1) * 128)
            out[c, :, cols] = jnp.concatenate([a[:, :TW], b[:, :TW]], axis=1).astype(bf16)
            out[c + 6, :, cols] = jnp.concatenate([a[:, TW:], b[:, TW:]], axis=1).astype(bf16)


def finish_kernel(parts, g1, g2, g3, film):
    def block(k):
        pair = jnp.sum(parts[:, (k // 2) * 16:(k // 2 + 1) * 16, :].astype(f32), axis=0)
        return pair[(k % 2) * 8:(k % 2) * 8 + 8]

    low, high, third = block(9), block(10), block(11)
    for a in range(3):
        for b in range(3):
            tap = 3 * a + b
            lanes = slice(tap * COUT, (tap + 1) * COUT)
            g2[a, b] = block(tap)
            g1[a, b, :, :COUT] = low[:, lanes]
            g1[a, b, :, COUT:] = high[:, lanes]
            g3[a, b] = third[:, (8 - tap) * COUT:(9 - tap) * COUT]
    film[...] = jnp.transpose(third)[FILM_LANE:FILM_LANE + 1]


VMEM = pl.BlockSpec(memory_space=pltpu.VMEM)
ANY = pl.BlockSpec(memory_space=pl.ANY)


def kernel_call(body, ins, outs, scratch=(), limit=16, cost=None):
    return pl.pallas_call(
        body,
        in_specs=list(ins),
        out_specs=[VMEM] * len(outs),
        out_shape=[jax.ShapeDtypeStruct(shape, dtype) for shape, dtype in outs],
        scratch_shapes=list(scratch),
        compiler_params=pltpu.CompilerParams(vmem_limit_bytes=limit * MIB),
        cost_estimate=cost,
    )


def planes(rows, dtype, count=PLANES):
    return pltpu.VMEM((rows, count, SUB, 128), dtype)


def pairs(rows, dtype, count=PLANES):
    return pltpu.VMEM((rows // 2, 2, count, SUB, 128), dtype)


def shards(condition, target, noise_draw, sigma_index, reg_first, reg_second, first_kernel,
           second_kernel, third_kernel, film_scale):
    order, back, spread, repeat = place_constants()
    table = jnp.asarray(coef_table())
    last, leading, packed = kernel_call(
        pack_kernel, [ANY] * 11,
        [((36, 8, 128), bf16), ((36, 8, 128), bf16), ((16, 112, 128), bf16)],
        [pltpu.SMEM((1,), jnp.int32), pltpu.SMEM((NSIG, 8), f32),
         pltpu.VMEM((3, COUT, 16, 256), f32), pltpu.VMEM((3, 3, 8, 24), bf16),
         pltpu.VMEM((3, 3, 8, 128), bf16), pltpu.VMEM((3, 3, 8, 12), bf16),
         pltpu.VMEM((3, 3, 12, 16), bf16), pltpu.VMEM((3, 3, 16, 12), bf16),
         pltpu.VMEM((1, 8), bf16), pltpu.SemaphoreType.DMA((11,))],
        limit=60,
    )(sigma_index, table, condition, target, noise_draw, jnp.swapaxes(first_kernel, 2, 3),
      jnp.swapaxes(second_kernel, 2, 3), third_kernel, reg_first, reg_second,
      film_scale.reshape(1, 8))
    up = [(i, i + 1) for i in range(lax.axis_size("rows") - 1)]
    before = lax.ppermute(last, "rows", up)
    after = lax.ppermute(leading, "rows", [(j, i) for i, j in up])
    gathered = lax.all_to_all(packed, GROUP, 0, 0, tiled=True)
    cond_taps, fields = kernel_call(
        prep_kernel, [ANY] * 5 + [VMEM] * 2 + [ANY] * 2,
        [((14, 2, PLANES, SUB, 128), bf16), ((13, 2, PLANES, SUB, 128), bf16)],
        [pltpu.SMEM((1,), jnp.int32), pltpu.SMEM((NSIG, 8), f32),
         pltpu.VMEM((48, 32, 128), f32), pltpu.VMEM((3, COUT, 16, 256), f32),
         planes(32, bf16, 7), pltpu.VMEM((30 * WIN, 128), bf16), pltpu.VMEM((WIN, 128), bf16), pltpu.VMEM((128, 128), bf16),
         pltpu.SemaphoreType.DMA((7,))],
        limit=52,
        cost=pl.CostEstimate(flops=1 << 32, bytes_accessed=8 * MIB, transcendentals=0),
    )(sigma_index, table, condition, target, noise_draw, before, after, jnp.asarray(order, bf16), jnp.asarray(spread[:, :128], bf16))
    wide = [pairs(40, bf16, PLANES + 2) for _ in range(6)]
    out, = kernel_call(
        step_kernel, [ANY] * 3 + [VMEM] * 5, [((16, 192, 128), bf16)],
        [pltpu.SMEM((1,), jnp.int32), pltpu.SMEM((NSIG, 8), f32), pairs(26, bf16),
         pltpu.SemaphoreType.DMA((3,)), pltpu.VMEM((256, 1536), bf16),
         pltpu.VMEM((1536, 256), bf16), pltpu.VMEM((128, 256), bf16),
         pltpu.VMEM((128, 128), bf16), pltpu.VMEM((256, 256), bf16),
         pltpu.VMEM((1536, 256), bf16), pltpu.VMEM((256, 256), bf16),
         pltpu.VMEM((1536, 256), bf16)]
        + wide
        + [pairs(24, bf16), pairs(18, bf16), pairs(26, f32), pairs(26, f32),
           pairs(24, f32), pairs(22, f32), pairs(20, bf16, 8), pairs(16, bf16),
           pltpu.VMEM((8, 128), f32), pltpu.VMEM((256, 128), f32),
           pltpu.VMEM((PLANES, SUB, 128), f32)],
        limit=52,
    )(sigma_index, table, fields, cond_taps, gathered, jnp.asarray(repeat, bf16),
      jnp.asarray(back, bf16), jnp.asarray(spread[:, 128:], bf16))
    parts = lax.all_to_all(out, GROUP, 0, 0, tiled=True)
    folded, = kernel_call(fold_kernel, [VMEM], [((8, 96, 128), bf16)])(parts)
    denoised, = kernel_call(
        field_kernel, [VMEM], [((COUT, 16, NW), bf16)],
        cost=pl.CostEstimate(flops=1 << 26, bytes_accessed=2 * MIB, transcendentals=0),
    )(parts)
    sums = lax.all_to_all(folded, "rows", 0, 0, tiled=True)
    g1, g2, g3, film = kernel_call(
        finish_kernel, [VMEM],
        [((3, 3, 8, 24), f32), ((3, 3, 8, 128), f32), ((3, 3, 8, 12), f32), ((1, 8), f32)],
    )(sums)
    return denoised, jnp.swapaxes(g1, 2, 3), jnp.swapaxes(g2, 2, 3), g3, film.reshape(8)


def solution(mesh):
    return jax.shard_map(
        shards,
        mesh=mesh,
        in_specs=(
            P(None, "rows", None),
            P(None, "rows", None),
            P(None, "rows", None),
            P(),
            P(None, None, None, "chan"),
            P(None, None, "chan", None),
            P(None, None, None, GROUP),
            P(None, None, None, GROUP),
            P(None, None, GROUP, None),
            P(GROUP),
        ),
        out_specs=(
            P(None, "rows", None),
            P(None, None, None, GROUP),
            P(None, None, None, GROUP),
            P(None, None, GROUP, None),
            P(GROUP),
        ),
        check_vma=False,
    )
```

```python
import math

import numpy as np
import jax
import jax.numpy as jnp
from jax import lax
from jax.experimental import pallas as pl
from jax.experimental.pallas import tpu as pltpu
from jax.sharding import PartitionSpec as P

COUT = 12
NSIG = 32
NH = 128
NW = 1024
TW = 64
RIM = 8
PLANES = 5
SUB = 16
WIN = PLANES * SUB
TAPS = 9
FILM_LANE = 120
MIB = 1024 * 1024
GROUP = ("section", "chan")
f32 = jnp.float32
bf16 = jnp.bfloat16


def coef_table():
    i = np.arange(NSIG, dtype=np.float64)
    high, low = 4.0 ** (1 / 7), 0.25 ** (1 / 7)
    level = (high + i / (NSIG - 1) * (low - high)) ** 7
    total = level**2 + 0.25
    out_coef = 0.5 * level / np.sqrt(total)
    weight = total / (0.5 * level) ** 2
    table = np.zeros((NSIG, 8), np.float32)
    table[:, 0] = level
    table[:, 1] = 0.25 / total
    table[:, 2] = out_coef
    table[:, 3] = 1 / np.sqrt(total)
    table[:, 4] = np.log(8 * level) / 4
    table[:, 5] = 2 * weight * out_coef / math.sqrt(COUT * NH * NW)
    return table


def place_constants():
    order = np.zeros((WIN, 128), np.float32)
    back = np.zeros((128, 128), np.float32)
    for t in range(PLANES):
        for s in range(SUB):
            col = PLANES * s + t
            order[t * SUB + s, col] = 1
            if RIM <= col < RIM + TW:
                back[t * SUB + s, col - RIM] = 1
                back[t * SUB + s, TW + col - RIM] = 1
    spread = np.zeros((128, 384), np.float32)
    repeat = np.zeros((128, 10 * 128), np.float32)
    for c in range(COUT):
        for g in range(TAPS):
            spread[24 + c, g * COUT + c] = 1
            for first in (0, 48, 80):
                spread[first + c, 128 + g * COUT + c] = 1
                spread[first + COUT + c, 256 + g * COUT + c] = 1
            for tap in range(TAPS):
                repeat[tap * COUT + c, tap * 128 + g * COUT + c] = 1
            repeat[(8 - g) * COUT + c, 9 * 128 + g * COUT + c] = 1
    return order, back, spread, repeat


def dot(a, b, ca=1, cb=0):
    return lax.dot_general(a, b, (((ca,), (cb,)), ((), ())), preferred_element_type=f32)


def sigmoid(v):
    return 0.5 * jnp.tanh(0.5 * v) + 0.5


def member():
    return lax.axis_index("section") * lax.axis_size("chan") + lax.axis_index("chan")


def window_place():
    start = member() * TW - RIM
    base = jnp.clip((start + 128) // 128 * 128 - 128, 0, NW - 256)
    return start, pl.multiple_of(base, 128)


def window_copy(src, dst, sem):
    copy = pltpu.make_async_copy(src.at[:, :, pl.ds(window_place()[1], 256)], dst, sem)
    copy.start()
    return copy


def window(wide):
    start, base = window_place()
    rows = pltpu.roll(wide.reshape(COUT * 16, 256), lax.rem(512 - (start - base), 256), 1)
    rows = rows[:, :128]
    col = start + lax.broadcasted_iota(jnp.int32, rows.shape, 1)
    return jnp.where((col >= 0) & (col < NW), rows, 0.0).reshape(COUT, 16, 128)


def scalar_copies(index_any, table_any, index, table, sem_a, sem_b):
    copies = [pltpu.make_async_copy(index_any, index, sem_a),
              pltpu.make_async_copy(table_any, table, sem_b)]
    for copy in copies:
        copy.start()
    return copies


def send(ref, field, low):
    high = field.astype(bf16)
    ref[:COUT] = high
    ref[COUT:2 * COUT] = (field - high.astype(f32)).astype(bf16)
    ref[2 * COUT:] = low.astype(bf16)


def pack_kernel(index_any, table_any, cond, target, noise, w1_any, w2_any, w3_any, r1_any,
                r2_any, film_any, last_any, leading_any, packed_any,
                last, leading, packed, index, table, scr, w1, w2, w3, r1, r2, film, sems):
    scalars = scalar_copies(index_any, table_any, index, table, sems.at[9], sems.at[10])
    copies = [window_copy(src, scr.at[k], sems.at[6 + k])
              for k, src in enumerate((target, noise, cond))]
    small = []
    for k, (src, dst) in enumerate(((w2_any, w2), (w1_any, w1), (w3_any, w3), (r1_any, r1),
                                    (r2_any, r2), (film_any, film))):
        small.append(pltpu.make_async_copy(src, dst, sems.at[k]))
        small[-1].start()
    half = lax.axis_index("section") == 0
    eye = (lax.broadcasted_iota(jnp.int32, (8, 8), 0)
           == lax.broadcasted_iota(jnp.int32, (8, 8), 1)).astype(f32)
    for copy in small:
        copy.wait()

    def place(n, at):
        lane = lax.broadcasted_iota(jnp.int32, (n, 128), 1)
        row = lax.broadcasted_iota(jnp.int32, (n, 128), 0)
        return jnp.where((lane - row == at) & (row < COUT), 1.0, 0.0)

    first_in = jnp.zeros((8, 128), f32)
    first_cond = jnp.zeros((8, 128), f32)
    third = jnp.zeros((8, 128), f32)
    reg_a = jnp.zeros((16, 128), f32)
    reg_b = jnp.zeros((16, 128), f32)
    blocks = []
    for a in range(3):
        for b in range(3):
            tap = 3 * a + b
            low = place(COUT, tap * COUT)
            lane = lax.broadcasted_iota(jnp.int32, (24, 128), 1)
            row = lax.broadcasted_iota(jnp.int32, (24, 128), 0)
            low_in = jnp.where((lane - row == tap * COUT) & (row < COUT), 1.0, 0.0)
            low_cond = jnp.where((lane - row == (tap - 1) * COUT) & (row >= COUT), 1.0, 0.0)
            blocks.append(w2[a, b].astype(f32))
            first_in += dot(w1[a, b].astype(f32), low_in)
            first_cond += dot(w1[a, b].astype(f32), low_cond)
            third += dot(w3[a, b].astype(f32), low)
            reg_a += dot(r1[a, b].astype(f32), low, 0, 0)
            reg_b += dot(r2[a, b].astype(f32), low)
    lane = lax.broadcasted_iota(jnp.int32, (8, 128), 1)
    film_col = jnp.sum(eye * film[...].astype(f32), axis=1, keepdims=True)
    third = jnp.where(lane == FILM_LANE, film_col, third)
    blocks += [first_in, first_cond, third,
               jnp.where(half, reg_a[:8], reg_a[8:]), jnp.where(half, reg_b[:8], reg_b[8:])]
    for p in range(7):
        pair = jnp.concatenate(blocks[2 * p:2 * p + 2], axis=0).astype(bf16)
        packed[p * 16:(p + 1) * 16, :] = pair
    results = [pltpu.make_async_copy(packed, packed_any.at[q], sems.at[11 + q])
               for q in range(16)]
    for copy in results:
        copy.start()
    for copy in copies + scalars:
        copy.wait()
    draw = window(scr[1])
    noised = window(scr[0]) + table[index[0], 0] * draw
    low = window(scr[2])
    row = lax.broadcasted_iota(jnp.int32, (COUT, 8, 128), 1)
    send(last, jnp.where(row < 2, pltpu.roll(draw[:, 8:], 2, 1), noised[:, 8:]), low[:, 8:])
    send(leading, jnp.where(row >= 6, pltpu.roll(draw[:, :8], 6, 1), noised[:, :8]), low[:, :8])
    for k, (src, dst) in enumerate(((last, last_any), (leading, leading_any))):
        results.append(pltpu.make_async_copy(src, dst, sems.at[27 + k]))
        results[-1].start()
    for copy in results:
        copy.wait()


def put(ref, at, n, value):
    ref[pl.ds(at, n), 1:PLANES + 1] = value.astype(bf16)
    ref[pl.ds(at, n), 0] = pltpu.roll(value[:, PLANES - 1], 1, 1).astype(bf16)
    ref[pl.ds(at, n), PLANES + 1] = pltpu.roll(value[:, 0], SUB - 1, 1).astype(bf16)


def pick_taps(ref, at, n):
    lane = lax.broadcasted_iota(jnp.int32, (SUB, 128), 1)
    total = None
    for a in range(3):
        for b in range(3):
            low = (3 * a + b) * COUT
            mask = jnp.where((lane >= low) & (lane < low + COUT), 1.0, 0.0).astype(bf16)
            part = ref[pl.ds(at + a - 1, n), b:b + PLANES] * mask[None, None]
            total = part if total is None else total + part
    return total


def prep_kernel(index_any, table_any, cond, target, noise, before, after, order_any, spread_any,
                cond_taps, fields, index, table, scr, wide, cond9, cells, order, spread, sems):
    copies = [window_copy(src, wide.at[k], sems.at[k])
              for k, src in enumerate((target, noise, cond))]
    others = [
        pltpu.make_async_copy(order_any, order, sems.at[3]),
        pltpu.make_async_copy(spread_any, spread, sems.at[4]),
    ]
    for copy in others:
        copy.start()
    scalars = scalar_copies(index_any, table_any, index, table, sems.at[5], sems.at[6])
    scr[36:48] = jnp.zeros((12, 32, 128), f32)
    for src, rows, shift in ((before, slice(0, 8), 6), (after, slice(24, 32), 2)):
        field = src[:COUT].astype(f32) + src[COUT:2 * COUT].astype(f32)
        scr[0:12, rows] = field
        scr[12:24, rows] = pltpu.roll(field, shift, 1)
        scr[24:36, rows] = src[2 * COUT:].astype(f32)
    for copy in copies + scalars:
        copy.wait()
    draw = window(wide[1])
    scr[0:12, 8:24] = window(wide[0]) + table[index[0], 0] * draw
    scr[12:24, 8:24] = draw
    scr[24:36, 8:24] = window(wide[2])
    for copy in others:
        copy.wait()
    flat = scr.reshape(48 * 32, 128)

    for i in range(1, 31):
        x = flat[pl.ds(i, 48, stride=32), :]
        high = x.astype(bf16)
        rest = x[:32] - high[:32].astype(f32)
        mid = rest.astype(bf16)
        low = (rest - mid.astype(f32)).astype(bf16)
        rows = jnp.concatenate([high, mid, low, jnp.zeros((16, 128), bf16)], axis=0)
        turned = dot(order[...], rows, 1, 1).astype(bf16)
        cells[(i - 1) * WIN:i * WIN] = turned
        if 3 <= i < 29:
            fields[(i - 3) // 2, (i - 3) % 2] = turned.reshape(PLANES, SUB, 128)
    count = 6
    for i in range(1, 31, count):
        wide = dot(cells[(i - 1) * WIN:(i - 1 + count) * WIN], spread[...])
        put(cond9, i, count, wide.reshape(count, PLANES, SUB, 128))

    @pl.loop(0, 7)
    def _(k):
        at = 2 + 4 * k
        cond_taps[pl.ds(2 * k, 2)] = pick_taps(cond9, at, 4).reshape(2, 2, PLANES, SUB, 128)


def some(ref, row, k, n, base=0):
    return ref.at[pl.ds((row - base) // 2 + k, n), (row - base) % 2]


def put_pair(ref, row, k, n, value):
    dst = some(ref, row, k, n)
    dst[:, 1:PLANES + 1] = value.astype(bf16)
    dst[:, 0] = pltpu.roll(value[:, PLANES - 1], 1, 1).astype(bf16)
    dst[:, PLANES + 1] = pltpu.roll(value[:, 0], SUB - 1, 1).astype(bf16)


def stack_rows(ref, row, k, n):
    parts = []
    for u in range(4):
        src = some(ref, row + u - 1, k, n)
        for b in range(3):
            parts.append(src[:, b:b + PLANES].reshape(n * WIN, 128))
    return jnp.concatenate(parts, axis=1)


def pick_pair(ref, row, k, n):
    lane = lax.broadcasted_iota(jnp.int32, (SUB, 128), 1)
    parts = []
    for a in range(3):
        src = some(ref, row + a - 1, k, n)
        for b in range(3):
            low = (3 * a + b) * COUT
            part = src[:, b:b + PLANES]
            here = lane[None, None] < low + COUT
            parts.append((part, here))
    total = parts[8][0] * jnp.where(lane < TAPS * COUT, 1.0, 0.0).astype(bf16)[None, None]
    for part, here in parts[7::-1]:
        total = jnp.where(here, part, total)
    return total


def step_kernel(index_any, table_any, field_any, cond_taps, gathered, repeat, back, spread,
                out_any, out, index, table, fields, sems,
                w2, w2t, w1, w3, w3f, w3r, r1, r2,
                hid, inp, one, two, dlt, sdl, taps_in, taps_d, draw, noisy, act, slope,
                den, grad1, film_sum, den_rows, inside):
    copies = scalar_copies(index_any, table_any, index, table, sems.at[0], sems.at[1])
    copies.append(pltpu.make_async_copy(field_any, fields, sems.at[2]))
    copies[-1].start()
    first_row = lax.axis_index("rows") * 16 - RIM
    first_col = member() * TW - RIM
    unused = (slice(9 * 128, 12 * 128), slice(0, 3 * 128))
    for v in range(2):
        w2[v * 128:(v + 1) * 128, unused[v]] = jnp.zeros((128, 384), bf16)
        for ref in (w2t, w3r, r2):
            ref[unused[v], v * 128:(v + 1) * 128] = jnp.zeros((384, 128), bf16)
    for ref in (r1, w3f):
        ref[...] = jnp.zeros(ref.shape, bf16)
    den[:, :, PLANES:] = jnp.zeros((10, 2, 8 - PLANES, SUB, 128), bf16)
    shape = (PLANES, SUB, 128)
    col = (lax.broadcasted_iota(jnp.int32, shape, 1) * PLANES
           + lax.broadcasted_iota(jnp.int32, shape, 0))
    inside[...] = jnp.where((col + first_col >= 0) & (col + first_col < NW), 1.0, 0.0)
    tile = jnp.where((col >= RIM) & (col < RIM + TW), 1.0, 0.0)

    def block(k):
        pair = gathered[:, (k // 2) * 16:(k // 2 + 1) * 16, :].astype(f32)
        low = (k % 2) * 8
        return pair[:, low:low + 8].reshape(128, 128).astype(bf16)

    def spot(tap, v):
        a, b = tap // 3, tap % 3
        at = (3 * (a + v) + b) * 128
        return slice(at, at + 128)

    halves = (slice(0, 128), slice(128, 256))
    for v in range(2):
        r1[halves[v], halves[v]] = block(12)
    w3[...] = block(11)
    wide = dot(block(13), repeat[:, :9 * 128]).astype(bf16)
    for tap in range(TAPS):
        for v in range(2):
            r2[spot(tap, v), halves[v]] = wide[:, tap * 128:(tap + 1) * 128]
    w1[:, :128] = block(9)
    w1[:, 128:] = block(10)
    for tap in range(TAPS):
        part = block(tap)
        for v in range(2):
            w2[halves[v], spot(tap, v)] = part
            w2t[spot(8 - tap, v), halves[v]] = part
    wide = dot(w3[...], repeat[...]).astype(bf16)
    for tap in range(TAPS):
        for v in range(2):
            w3r[spot(tap, v), halves[v]] = wide[:, tap * 128:(tap + 1) * 128]
    for v in range(2):
        w3f[halves[v], halves[v]] = wide[:, 9 * 128:]

    def cells(value):
        return value.reshape(-1, PLANES, SUB, 128)

    def flat(value):
        return value.reshape(-1, 128)

    def sweep(count, n, body):
        @pl.loop(0, count // n)
        def _(k):
            body(k * n, n)

        if count % n:
            body(count // n * n, count % n)

    def clear(ref):
        zero = jnp.zeros((4, 2, PLANES + 2, SUB, 128), bf16)
        ref[pl.ds(jnp.where(first_row < 0, 0, 16), 4)] = zero
        ref[pl.ds(jnp.where(first_row + 32 > NH, 12, 16), 4)] = zero

    def reg_one(k, n):
        both = jnp.concatenate([flat(some(cond_taps, 2 + v, k, n, 2)[...]) for v in range(2)], 1)
        value = dot(both, r1[...], 1, 1)
        for v in range(2):
            x = value[:, halves[v]]
            put_pair(hid, 2 + v, k, n, cells(x * sigmoid(x)) * inside[...])

    sweep(14, 14, reg_one)
    clear(hid)

    def reg_two(k, n):
        value = dot(stack_rows(hid, 3, k, n), r2[...])
        for v in range(2):
            row = 3 + v
            mean = cells(value[:, halves[v]]).astype(bf16).astype(f32)
            both = dot(flat(some(fields, row, k, n, 3)[...]), spread[...])
            noised = cells(both[:, halves[0]]) - mean
            some(draw, row, k, n, 3)[...] = cells(both[:, halves[1]])
            some(noisy, row, k, n, 3)[...] = noised
            put_pair(inp, row, k, n, in_coef * noised * inside[...])

    for copy in copies:
        copy.wait()
    level = index[0]
    sigma, skip, out_coef = table[level, 0], table[level, 1], table[level, 2]
    in_coef, noise_coef, delta_coef = table[level, 3], table[level, 4], table[level, 5]
    lane = lax.broadcasted_iota(jnp.int32, (16, 128), 1)
    pick_film = jnp.where(lane == FILM_LANE, 1.0, 0.0).astype(bf16)
    gain = 1.0 + noise_coef * dot(pick_film, w3[...], 1, 1)[0:1]
    sweep(13, 13, reg_two)
    clear(inp)

    def conv_one(k, n):
        for v in range(2):
            row = 4 + v
            picked = pick_pair(inp, row, k, n)
            some(taps_in, row, k, n, 4)[...] = picked
            both = jnp.concatenate([flat(picked), flat(some(cond_taps, row, k, n, 2)[...])], 1)
            value = dot(both, w1[...], 1, 1)
            some(act, row, k, n, 4)[...] = cells(value)
            u = value * gain
            put_pair(one, row, k, n, cells(u * sigmoid(u)) * inside[...])

    sweep(12, 6, conv_one)
    clear(one)

    def conv_two(k, n):
        value = dot(stack_rows(one, 5, k, n), w2[...], 1, 1)
        for v in range(2):
            x = value[:, halves[v]]
            s = sigmoid(x)
            some(slope, 5 + v, k, n, 5)[...] = cells(s * (1.0 + x * (1.0 - s)))
            put_pair(two, 5 + v, k, n, cells(x * s) * inside[...])

    sweep(11, 11, conv_two)
    clear(two)

    def conv_three(k, n):
        value = dot(stack_rows(two, 6, k, n), w3r[...])
        for v in range(2):
            row = 6 + v
            noised = some(noisy, row, k, n, 3)[...]
            full = skip * noised + out_coef * cells(value[:, halves[v]])
            some(den, row, k, n, 6)[:, :PLANES] = full.astype(bf16)
            delta = delta_coef * (full - (noised - sigma * some(draw, row, k, n, 3)[...]))
            put_pair(dlt, row, k, n, delta * inside[...])

    sweep(10, 5, conv_three)
    clear(dlt)
    fields = (lax.broadcasted_iota(jnp.int32, (16, 128), 0)
              == lax.broadcasted_iota(jnp.int32, (16, 128), 1)).astype(f32).astype(bf16)
    turned = dot(fields, den[1:9].reshape(16 * 128, 128), 1, 1).astype(bf16)
    turned = jnp.concatenate([turned[:, i * 128:(i + 1) * 128] for i in range(16)], axis=0)
    den_rows[...] = dot(turned, back[...])
    for c in range(6):
        left = den_rows[pl.ds(c, 16, stride=16), :]
        right = den_rows[pl.ds(c + 6, 16, stride=16), :]
        piece = jnp.where(lane < TW, left, right).astype(bf16)
        out[:, 96 + c * 16:96 + (c + 1) * 16, :] = jnp.broadcast_to(piece[None], (16, 16, 128))
    den_out = pltpu.make_async_copy(out.at[:, 96:192], out_any.at[:, 96:192], sems.at[3])
    den_out.start()

    def delta_two(k, n):
        parts = []
        for v in range(2):
            picked = pick_pair(dlt, 7 + v, k, n)
            some(taps_d, 7 + v, k, n, 7)[...] = picked
            parts.append(flat(picked))
        value = dot(jnp.concatenate(parts, axis=1), w3f[...], 1, 1)
        for v in range(2):
            x = cells(value[:, halves[v]]) * some(slope, 7 + v, k, n, 5)[...]
            put_pair(sdl, 7 + v, k, n, x * inside[...])

    sweep(9, 9, delta_two)
    clear(sdl)
    film_sum[...] = jnp.zeros((8, 128), f32)

    def delta_one(k, n):
        value = dot(stack_rows(sdl, 8, k, n), w2t[...])
        for v in range(2):
            a = flat(some(act, 8 + v, k, n, 4)[...])
            u = a * gain
            s = sigmoid(u)
            g = flat(cells(value[:, halves[v]] * (s * (1.0 + u * (1.0 - s)))) * tile)
            film_sum[...] += jnp.sum((g * a).reshape(-1, 8, 128), axis=0)
            some(grad1, 8 + v, k, n, 8)[...] = cells(g * gain).astype(bf16)

    sweep(8, 8, delta_one)

    tile_low = tile.astype(bf16)

    def both_rows(read):
        return jnp.concatenate([read(8), read(9)], axis=0)

    def own_cells(ref):
        return lambda row: flat(some(ref, row, 0, 8)[:, 1:PLANES + 1] * tile_low)

    def own_field(ref, base):
        return lambda row: flat(some(ref, row, 0, 8, base)[...])

    def taps_of(row):
        return jnp.concatenate([flat(some(one, row + a - 1, 0, 8)[:, b:b + PLANES])
                                for a in range(3) for b in range(3)], axis=1)

    def first_taps(row):
        return jnp.concatenate([own_field(taps_in, 4)(row), own_field(cond_taps, 2)(row)], axis=1)

    g2 = dot(both_rows(own_cells(sdl)), both_rows(taps_of), 0, 0)
    g1 = dot(both_rows(own_field(grad1, 8)), both_rows(first_taps), 0, 0)
    g3 = dot(both_rows(own_cells(two)), both_rows(own_field(taps_d, 7)), 0, 0)
    film = noise_coef * jnp.sum(film_sum[...], axis=0, keepdims=True)
    film = jnp.transpose(jnp.broadcast_to(film, (8, 128)))[:, 0:1]
    g3 = jnp.where(lax.broadcasted_iota(jnp.int32, (128, 128), 1) == FILM_LANE, film, g3)
    parts = [g2[:, k * 128:(k + 1) * 128] for k in range(9)] + [g1[:, :128], g1[:, 128:], g3]
    for p in range(6):
        pair = [part.reshape(16, 8, 128) for part in parts[2 * p:2 * p + 2]]
        out[:, p * 16:(p + 1) * 16, :] = jnp.concatenate(pair, axis=1).astype(bf16)
    grads_out = pltpu.make_async_copy(out.at[:, 0:96], out_any.at[:, 0:96], sems.at[4])
    grads_out.start()
    grads_out.wait()
    den_out.wait()


def fold_kernel(parts, out):
    for p in range(6):
        total = jnp.sum(parts[:, p * 16:(p + 1) * 16, :].astype(f32), axis=0).astype(bf16)
        for q in range(8):
            out[q, p * 16:(p + 1) * 16, :] = total


def field_kernel(parts, out):
    for k in range(8):
        for c in range(6):
            a = parts[2 * k, 96 + c * 16:96 + (c + 1) * 16, :].astype(f32)
            b = parts[2 * k + 1, 96 + c * 16:96 + (c + 1) * 16, :].astype(f32)
            cols = slice(k * 128, (k + 1) * 128)
            out[c, :, cols] = jnp.concatenate([a[:, :TW], b[:, :TW]], axis=1).astype(bf16)
            out[c + 6, :, cols] = jnp.concatenate([a[:, TW:], b[:, TW:]], axis=1).astype(bf16)


def finish_kernel(parts, g1, g2, g3, film):
    def block(k):
        pair = jnp.sum(parts[:, (k // 2) * 16:(k // 2 + 1) * 16, :].astype(f32), axis=0)
        return pair[(k % 2) * 8:(k % 2) * 8 + 8]

    low, high, third = block(9), block(10), block(11)
    for a in range(3):
        for b in range(3):
            tap = 3 * a + b
            lanes = slice(tap * COUT, (tap + 1) * COUT)
            g2[a, b] = block(tap)
            g1[a, b, :, :COUT] = low[:, lanes]
            g1[a, b, :, COUT:] = high[:, lanes]
            g3[a, b] = third[:, (8 - tap) * COUT:(9 - tap) * COUT]
    film[...] = jnp.transpose(third)[FILM_LANE:FILM_LANE + 1]


VMEM = pl.BlockSpec(memory_space=pltpu.VMEM)
ANY = pl.BlockSpec(memory_space=pl.ANY)


def kernel_call(body, ins, outs, scratch=(), limit=16, cost=None, out_space=VMEM):
    return pl.pallas_call(
        body,
        in_specs=list(ins),
        out_specs=[out_space] * len(outs),
        out_shape=[jax.ShapeDtypeStruct(shape, dtype) for shape, dtype in outs],
        scratch_shapes=list(scratch),
        compiler_params=pltpu.CompilerParams(vmem_limit_bytes=limit * MIB),
        cost_estimate=cost,
    )


def planes(rows, dtype, count=PLANES):
    return pltpu.VMEM((rows, count, SUB, 128), dtype)


def pairs(rows, dtype, count=PLANES):
    return pltpu.VMEM((rows // 2, 2, count, SUB, 128), dtype)


def shards(condition, target, noise_draw, sigma_index, reg_first, reg_second, first_kernel,
           second_kernel, third_kernel, film_scale):
    order, back, spread, repeat = place_constants()
    table = jnp.asarray(coef_table())
    last, leading, packed = kernel_call(
        pack_kernel, [ANY] * 11,
        [((36, 8, 128), bf16), ((36, 8, 128), bf16), ((16, 112, 128), bf16)],
        [pltpu.VMEM((36, 8, 128), bf16), pltpu.VMEM((36, 8, 128), bf16),
         pltpu.VMEM((112, 128), bf16), pltpu.SMEM((1,), jnp.int32), pltpu.SMEM((NSIG, 8), f32),
         pltpu.VMEM((3, COUT, 16, 256), f32), pltpu.VMEM((3, 3, 8, 24), bf16),
         pltpu.VMEM((3, 3, 8, 128), bf16), pltpu.VMEM((3, 3, 8, 12), bf16),
         pltpu.VMEM((3, 3, 12, 16), bf16), pltpu.VMEM((3, 3, 16, 12), bf16),
         pltpu.VMEM((1, 8), bf16), pltpu.SemaphoreType.DMA((29,))],
        limit=60, out_space=ANY,
    )(sigma_index, table, condition, target, noise_draw, jnp.swapaxes(first_kernel, 2, 3),
      jnp.swapaxes(second_kernel, 2, 3), third_kernel, reg_first, reg_second,
      film_scale.reshape(1, 8))
    up = [(i, i + 1) for i in range(lax.axis_size("rows") - 1)]
    before = lax.ppermute(last, "rows", up)
    after = lax.ppermute(leading, "rows", [(j, i) for i, j in up])
    gathered = lax.all_to_all(packed, GROUP, 0, 0, tiled=True)
    cond_taps, fields = kernel_call(
        prep_kernel, [ANY] * 5 + [VMEM] * 2 + [ANY] * 2,
        [((14, 2, PLANES, SUB, 128), bf16), ((13, 2, PLANES, SUB, 128), bf16)],
        [pltpu.SMEM((1,), jnp.int32), pltpu.SMEM((NSIG, 8), f32),
         pltpu.VMEM((48, 32, 128), f32), pltpu.VMEM((3, COUT, 16, 256), f32),
         planes(32, bf16, 7), pltpu.VMEM((30 * WIN, 128), bf16), pltpu.VMEM((WIN, 128), bf16), pltpu.VMEM((128, 128), bf16),
         pltpu.SemaphoreType.DMA((7,))],
        limit=52,
        cost=pl.CostEstimate(flops=1 << 32, bytes_accessed=8 * MIB, transcendentals=0),
    )(sigma_index, table, condition, target, noise_draw, before, after, jnp.asarray(order, bf16), jnp.asarray(spread[:, :128], bf16))
    wide = [pairs(40, bf16, PLANES + 2) for _ in range(6)]
    out, = kernel_call(
        step_kernel, [ANY] * 3 + [VMEM] * 5, [((16, 192, 128), bf16)],
        [pltpu.VMEM((16, 192, 128), bf16), pltpu.SMEM((1,), jnp.int32),
         pltpu.SMEM((NSIG, 8), f32), pairs(26, bf16),
         pltpu.SemaphoreType.DMA((5,)), pltpu.VMEM((256, 1536), bf16),
         pltpu.VMEM((1536, 256), bf16), pltpu.VMEM((128, 256), bf16),
         pltpu.VMEM((128, 128), bf16), pltpu.VMEM((256, 256), bf16),
         pltpu.VMEM((1536, 256), bf16), pltpu.VMEM((256, 256), bf16),
         pltpu.VMEM((1536, 256), bf16)]
        + wide
        + [pairs(24, bf16), pairs(18, bf16), pairs(26, f32), pairs(26, f32),
           pairs(24, f32), pairs(22, f32), pairs(20, bf16, 8), pairs(16, bf16),
           pltpu.VMEM((8, 128), f32), pltpu.VMEM((256, 128), f32),
           pltpu.VMEM((PLANES, SUB, 128), f32)],
        limit=52, out_space=ANY,
    )(sigma_index, table, fields, cond_taps, gathered, jnp.asarray(repeat, bf16),
      jnp.asarray(back, bf16), jnp.asarray(spread[:, 128:], bf16))
    parts = lax.all_to_all(out, GROUP, 0, 0, tiled=True)
    folded, = kernel_call(fold_kernel, [VMEM], [((8, 96, 128), bf16)])(parts)
    denoised, = kernel_call(
        field_kernel, [VMEM], [((COUT, 16, NW), bf16)],
        cost=pl.CostEstimate(flops=1 << 26, bytes_accessed=2 * MIB, transcendentals=0),
    )(parts)
    sums = lax.all_to_all(folded, "rows", 0, 0, tiled=True)
    g1, g2, g3, film = kernel_call(
        finish_kernel, [VMEM],
        [((3, 3, 8, 24), f32), ((3, 3, 8, 128), f32), ((3, 3, 8, 12), f32), ((1, 8), f32)],
    )(sums)
    return denoised, jnp.swapaxes(g1, 2, 3), jnp.swapaxes(g2, 2, 3), g3, film.reshape(8)


def solution(mesh):
    return jax.shard_map(
        shards,
        mesh=mesh,
        in_specs=(
            P(None, "rows", None),
            P(None, "rows", None),
            P(None, "rows", None),
            P(),
            P(None, None, None, "chan"),
            P(None, None, "chan", None),
            P(None, None, None, GROUP),
            P(None, None, None, GROUP),
            P(None, None, GROUP, None),
            P(GROUP),
        ),
        out_specs=(
            P(None, "rows", None),
            P(None, None, None, GROUP),
            P(None, None, None, GROUP),
            P(None, None, GROUP, None),
            P(GROUP),
        ),
        check_vma=False,
    )
```

```python
import math

import numpy as np
import jax
import jax.numpy as jnp
from jax import lax
from jax.experimental import pallas as pl
from jax.experimental.pallas import tpu as pltpu
from jax.sharding import PartitionSpec as P

COUT = 12
NSIG = 32
NH = 128
NW = 1024
TW = 64
RIM = 8
PLANES = 5
SUB = 16
WIN = PLANES * SUB
TAPS = 9
FILM_LANE = 120
MIB = 1024 * 1024
GROUP = ("section", "chan")
f32 = jnp.float32
bf16 = jnp.bfloat16


def coef_table():
    i = np.arange(NSIG, dtype=np.float64)
    high, low = 4.0 ** (1 / 7), 0.25 ** (1 / 7)
    level = (high + i / (NSIG - 1) * (low - high)) ** 7
    total = level**2 + 0.25
    out_coef = 0.5 * level / np.sqrt(total)
    weight = total / (0.5 * level) ** 2
    table = np.zeros((NSIG, 8), np.float32)
    table[:, 0] = level
    table[:, 1] = 0.25 / total
    table[:, 2] = out_coef
    table[:, 3] = 1 / np.sqrt(total)
    table[:, 4] = np.log(8 * level) / 4
    table[:, 5] = 2 * weight * out_coef / math.sqrt(COUT * NH * NW)
    return table


def place_constants():
    order = np.zeros((WIN, 128), np.float32)
    back = np.zeros((128, 128), np.float32)
    for t in range(PLANES):
        for s in range(SUB):
            col = PLANES * s + t
            order[t * SUB + s, col] = 1
            if RIM <= col < RIM + TW:
                back[t * SUB + s, col - RIM] = 1
                back[t * SUB + s, TW + col - RIM] = 1
    spread = np.zeros((128, 384), np.float32)
    repeat = np.zeros((128, 10 * 128), np.float32)
    for c in range(COUT):
        for g in range(TAPS):
            spread[24 + c, g * COUT + c] = 1
            for first in (0, 48, 80):
                spread[first + c, 128 + g * COUT + c] = 1
                spread[first + COUT + c, 256 + g * COUT + c] = 1
            for tap in range(TAPS):
                repeat[tap * COUT + c, tap * 128 + g * COUT + c] = 1
            repeat[(8 - g) * COUT + c, 9 * 128 + g * COUT + c] = 1
    return order, back, spread, repeat


def dot(a, b, ca=1, cb=0):
    return lax.dot_general(a, b, (((ca,), (cb,)), ((), ())), preferred_element_type=f32)


def sigmoid(v):
    return 0.5 * jnp.tanh(0.5 * v) + 0.5


def member():
    return lax.axis_index("section") * lax.axis_size("chan") + lax.axis_index("chan")


def window_place():
    start = member() * TW - RIM
    base = jnp.clip((start + 128) // 128 * 128 - 128, 0, NW - 256)
    return start, pl.multiple_of(base, 128)


def window_copy(src, dst, sem):
    copy = pltpu.make_async_copy(src.at[:, :, pl.ds(window_place()[1], 256)], dst, sem)
    copy.start()
    return copy


def window(wide):
    start, base = window_place()
    rows = pltpu.roll(wide.reshape(COUT * 16, 256), lax.rem(512 - (start - base), 256), 1)
    rows = rows[:, :128]
    col = start + lax.broadcasted_iota(jnp.int32, rows.shape, 1)
    return jnp.where((col >= 0) & (col < NW), rows, 0.0).reshape(COUT, 16, 128)


def scalar_copies(index_any, table_any, index, table, sem_a, sem_b):
    copies = [pltpu.make_async_copy(index_any, index, sem_a),
              pltpu.make_async_copy(table_any, table, sem_b)]
    for copy in copies:
        copy.start()
    return copies


def send(ref, field, low):
    high = field.astype(bf16)
    ref[:COUT] = high
    ref[COUT:2 * COUT] = (field - high.astype(f32)).astype(bf16)
    ref[2 * COUT:] = low.astype(bf16)


def pack_kernel(index_any, table_any, cond, target, noise, w1_any, w2_any, w3_any, r1_any,
                r2_any, film_any, last_any, leading_any, packed_any,
                last, leading, packed, index, table, scr, w1, w2, w3, r1, r2, film, sems):
    scalars = scalar_copies(index_any, table_any, index, table, sems.at[9], sems.at[10])
    copies = [window_copy(src, scr.at[k], sems.at[6 + k])
              for k, src in enumerate((target, noise, cond))]
    small = []
    for k, (src, dst) in enumerate(((w2_any, w2), (w1_any, w1), (w3_any, w3), (r1_any, r1),
                                    (r2_any, r2), (film_any, film))):
        small.append(pltpu.make_async_copy(src, dst, sems.at[k]))
        small[-1].start()
    half = lax.axis_index("section") == 0
    eye = (lax.broadcasted_iota(jnp.int32, (8, 8), 0)
           == lax.broadcasted_iota(jnp.int32, (8, 8), 1)).astype(f32)
    for copy in small:
        copy.wait()

    def place(n, at):
        lane = lax.broadcasted_iota(jnp.int32, (n, 128), 1)
        row = lax.broadcasted_iota(jnp.int32, (n, 128), 0)
        return jnp.where((lane - row == at) & (row < COUT), 1.0, 0.0)

    first_in = jnp.zeros((8, 128), f32)
    first_cond = jnp.zeros((8, 128), f32)
    third = jnp.zeros((8, 128), f32)
    reg_a = jnp.zeros((16, 128), f32)
    reg_b = jnp.zeros((16, 128), f32)
    blocks = []
    for a in range(3):
        for b in range(3):
            tap = 3 * a + b
            low = place(COUT, tap * COUT)
            lane = lax.broadcasted_iota(jnp.int32, (24, 128), 1)
            row = lax.broadcasted_iota(jnp.int32, (24, 128), 0)
            low_in = jnp.where((lane - row == tap * COUT) & (row < COUT), 1.0, 0.0)
            low_cond = jnp.where((lane - row == (tap - 1) * COUT) & (row >= COUT), 1.0, 0.0)
            blocks.append(w2[a, b].astype(f32))
            first_in += dot(w1[a, b].astype(f32), low_in)
            first_cond += dot(w1[a, b].astype(f32), low_cond)
            third += dot(w3[a, b].astype(f32), low)
            reg_a += dot(r1[a, b].astype(f32), low, 0, 0)
            reg_b += dot(r2[a, b].astype(f32), low)
    lane = lax.broadcasted_iota(jnp.int32, (8, 128), 1)
    film_col = jnp.sum(eye * film[...].astype(f32), axis=1, keepdims=True)
    third = jnp.where(lane == FILM_LANE, film_col, third)
    blocks += [first_in, first_cond, third,
               jnp.where(half, reg_a[:8], reg_a[8:]), jnp.where(half, reg_b[:8], reg_b[8:])]
    for p in range(7):
        pair = jnp.concatenate(blocks[2 * p:2 * p + 2], axis=0).astype(bf16)
        packed[p * 16:(p + 1) * 16, :] = pair
    results = [pltpu.make_async_copy(packed, packed_any.at[q], sems.at[11 + q])
               for q in range(16)]
    for copy in results:
        copy.start()
    for copy in copies + scalars:
        copy.wait()
    draw = window(scr[1])
    noised = window(scr[0]) + table[index[0], 0] * draw
    low = window(scr[2])
    row = lax.broadcasted_iota(jnp.int32, (COUT, 8, 128), 1)
    send(last, jnp.where(row < 2, pltpu.roll(draw[:, 8:], 2, 1), noised[:, 8:]), low[:, 8:])
    send(leading, jnp.where(row >= 6, pltpu.roll(draw[:, :8], 6, 1), noised[:, :8]), low[:, :8])
    for k, (src, dst) in enumerate(((last, last_any), (leading, leading_any))):
        results.append(pltpu.make_async_copy(src, dst, sems.at[27 + k]))
        results[-1].start()
    for copy in results:
        copy.wait()


def put(ref, at, n, value):
    ref[pl.ds(at, n), 1:PLANES + 1] = value.astype(bf16)
    ref[pl.ds(at, n), 0] = pltpu.roll(value[:, PLANES - 1], 1, 1).astype(bf16)
    ref[pl.ds(at, n), PLANES + 1] = pltpu.roll(value[:, 0], SUB - 1, 1).astype(bf16)


def pick_taps(ref, at, n):
    lane = lax.broadcasted_iota(jnp.int32, (SUB, 128), 1)
    total = None
    for a in range(3):
        for b in range(3):
            low = (3 * a + b) * COUT
            mask = jnp.where((lane >= low) & (lane < low + COUT), 1.0, 0.0).astype(bf16)
            part = ref[pl.ds(at + a - 1, n), b:b + PLANES] * mask[None, None]
            total = part if total is None else total + part
    return total


def prep_kernel(index_any, table_any, cond, target, noise, before, after, order_any, spread_any,
                cond_taps, fields, index, table, scr, wide, cond9, cells, order, spread, sems):
    copies = [window_copy(src, wide.at[k], sems.at[k])
              for k, src in enumerate((target, noise, cond))]
    others = [
        pltpu.make_async_copy(order_any, order, sems.at[3]),
        pltpu.make_async_copy(spread_any, spread, sems.at[4]),
    ]
    for copy in others:
        copy.start()
    scalars = scalar_copies(index_any, table_any, index, table, sems.at[5], sems.at[6])
    scr[36:48] = jnp.zeros((12, 32, 128), f32)
    for src, rows, shift in ((before, slice(0, 8), 6), (after, slice(24, 32), 2)):
        field = src[:COUT].astype(f32) + src[COUT:2 * COUT].astype(f32)
        scr[0:12, rows] = field
        scr[12:24, rows] = pltpu.roll(field, shift, 1)
        scr[24:36, rows] = src[2 * COUT:].astype(f32)
    for copy in copies + scalars:
        copy.wait()
    draw = window(wide[1])
    scr[0:12, 8:24] = window(wide[0]) + table[index[0], 0] * draw
    scr[12:24, 8:24] = draw
    scr[24:36, 8:24] = window(wide[2])
    for copy in others:
        copy.wait()
    flat = scr.reshape(48 * 32, 128)

    for i in range(1, 31):
        x = flat[pl.ds(i, 48, stride=32), :]
        high = x.astype(bf16)
        rest = x[:32] - high[:32].astype(f32)
        mid = rest.astype(bf16)
        low = (rest - mid.astype(f32)).astype(bf16)
        rows = jnp.concatenate([high, mid, low, jnp.zeros((16, 128), bf16)], axis=0)
        turned = dot(order[...], rows, 1, 1).astype(bf16)
        cells[(i - 1) * WIN:i * WIN] = turned
        if 3 <= i < 29:
            fields[(i - 3) // 2, (i - 3) % 2] = turned.reshape(PLANES, SUB, 128)
    count = 6
    for i in range(1, 31, count):
        wide = dot(cells[(i - 1) * WIN:(i - 1 + count) * WIN], spread[...])
        put(cond9, i, count, wide.reshape(count, PLANES, SUB, 128))

    @pl.loop(0, 7)
    def _(k):
        at = 2 + 4 * k
        cond_taps[pl.ds(2 * k, 2)] = pick_taps(cond9, at, 4).reshape(2, 2, PLANES, SUB, 128)


def some(ref, row, k, n, base=0):
    return ref.at[pl.ds((row - base) // 2 + k, n), (row - base) % 2]


def put_pair(ref, row, k, n, value):
    dst = some(ref, row, k, n)
    dst[:, 1:PLANES + 1] = value.astype(bf16)
    dst[:, 0] = pltpu.roll(value[:, PLANES - 1], 1, 1).astype(bf16)
    dst[:, PLANES + 1] = pltpu.roll(value[:, 0], SUB - 1, 1).astype(bf16)


def stack_rows(ref, row, k, n):
    parts = []
    for u in range(4):
        src = some(ref, row + u - 1, k, n)
        for b in range(3):
            parts.append(src[:, b:b + PLANES].reshape(n * WIN, 128))
    return jnp.concatenate(parts, axis=1)


def pick_pair(ref, row, k, n):
    lane = lax.broadcasted_iota(jnp.int32, (SUB, 128), 1)
    parts = []
    for a in range(3):
        src = some(ref, row + a - 1, k, n)
        for b in range(3):
            low = (3 * a + b) * COUT
            part = src[:, b:b + PLANES]
            here = lane[None, None] < low + COUT
            parts.append((part, here))
    total = parts[8][0] * jnp.where(lane < TAPS * COUT, 1.0, 0.0).astype(bf16)[None, None]
    for part, here in parts[7::-1]:
        total = jnp.where(here, part, total)
    return total


def step_kernel(index_any, table_any, field_any, cond_taps, gathered, repeat, back, spread,
                out_any, out, index, table, fields, sems,
                w2, w2t, w1, w3, w3f, w3r, r1, r2,
                hid, inp, one, two, dlt, sdl, taps_in, taps_d, draw, noisy, act, slope,
                den, grad1, film_sum, den_rows, inside):
    copies = scalar_copies(index_any, table_any, index, table, sems.at[0], sems.at[1])
    copies.append(pltpu.make_async_copy(field_any, fields, sems.at[2]))
    copies[-1].start()
    first_row = lax.axis_index("rows") * 16 - RIM
    first_col = member() * TW - RIM
    unused = (slice(9 * 128, 12 * 128), slice(0, 3 * 128))
    for v in range(2):
        w2[v * 128:(v + 1) * 128, unused[v]] = jnp.zeros((128, 384), bf16)
        for ref in (w2t, w3r, r2):
            ref[unused[v], v * 128:(v + 1) * 128] = jnp.zeros((384, 128), bf16)
    for ref in (r1, w3f):
        ref[...] = jnp.zeros(ref.shape, bf16)
    den[:, :, PLANES:] = jnp.zeros((10, 2, 8 - PLANES, SUB, 128), bf16)
    shape = (PLANES, SUB, 128)
    col = (lax.broadcasted_iota(jnp.int32, shape, 1) * PLANES
           + lax.broadcasted_iota(jnp.int32, shape, 0))
    inside[...] = jnp.where((col + first_col >= 0) & (col + first_col < NW), 1.0, 0.0)
    tile = jnp.where((col >= RIM) & (col < RIM + TW), 1.0, 0.0)

    def block(k):
        pair = gathered[:, (k // 2) * 16:(k // 2 + 1) * 16, :].astype(f32)
        low = (k % 2) * 8
        return pair[:, low:low + 8].reshape(128, 128).astype(bf16)

    def spot(tap, v):
        a, b = tap // 3, tap % 3
        at = (3 * (a + v) + b) * 128
        return slice(at, at + 128)

    halves = (slice(0, 128), slice(128, 256))
    for v in range(2):
        r1[halves[v], halves[v]] = block(12)
    w3[...] = block(11)
    wide = dot(block(13), repeat[:, :9 * 128]).astype(bf16)
    for tap in range(TAPS):
        for v in range(2):
            r2[spot(tap, v), halves[v]] = wide[:, tap * 128:(tap + 1) * 128]

    def cells(value):
        return value.reshape(-1, PLANES, SUB, 128)

    def flat(value):
        return value.reshape(-1, 128)

    def sweep(count, n, body):
        if count // n == 1:
            body(0, n)
        else:
            @pl.loop(0, count // n)
            def _(k):
                body(k * n, n)

        if count % n:
            body(count // n * n, count % n)

    def clear(ref):
        zero = jnp.zeros((4, 2, PLANES + 2, SUB, 128), bf16)
        ref[pl.ds(jnp.where(first_row < 0, 0, 16), 4)] = zero
        ref[pl.ds(jnp.where(first_row + 32 > NH, 12, 16), 4)] = zero

    def reg_one(k, n):
        both = jnp.concatenate([flat(some(cond_taps, 2 + v, k, n, 2)[...]) for v in range(2)], 1)
        value = dot(both, r1[...], 1, 1)
        for v in range(2):
            x = value[:, halves[v]]
            put_pair(hid, 2 + v, k, n, cells(x * sigmoid(x)) * inside[...])

    sweep(14, 14, reg_one)
    clear(hid)

    def reg_two(k, n):
        value = dot(stack_rows(hid, 3, k, n), r2[...])
        for v in range(2):
            row = 3 + v
            mean = cells(value[:, halves[v]]).astype(bf16).astype(f32)
            both = dot(flat(some(fields, row, k, n, 3)[...]), spread[...])
            noised = cells(both[:, halves[0]]) - mean
            some(draw, row, k, n, 3)[...] = cells(both[:, halves[1]])
            some(noisy, row, k, n, 3)[...] = noised
            put_pair(inp, row, k, n, in_coef * noised * inside[...])

    for copy in copies:
        copy.wait()
    level = index[0]
    sigma, skip, out_coef = table[level, 0], table[level, 1], table[level, 2]
    in_coef, noise_coef, delta_coef = table[level, 3], table[level, 4], table[level, 5]
    lane = lax.broadcasted_iota(jnp.int32, (16, 128), 1)
    pick_film = jnp.where(lane == FILM_LANE, 1.0, 0.0).astype(bf16)
    gain = 1.0 + noise_coef * dot(pick_film, w3[...], 1, 1)[0:1]
    w1[:, :128] = block(9)
    w1[:, 128:] = block(10)
    for tap in range(TAPS):
        part = block(tap)
        for v in range(2):
            w2[halves[v], spot(tap, v)] = part
            w2t[spot(8 - tap, v), halves[v]] = part
    wide = dot(w3[...], repeat[...]).astype(bf16)
    for tap in range(TAPS):
        for v in range(2):
            w3r[spot(tap, v), halves[v]] = wide[:, tap * 128:(tap + 1) * 128]
    for v in range(2):
        w3f[halves[v], halves[v]] = wide[:, 9 * 128:]
    sweep(13, 13, reg_two)
    clear(inp)

    def conv_one(k, n):
        for v in range(2):
            row = 4 + v
            picked = pick_pair(inp, row, k, n)
            some(taps_in, row, k, n, 4)[...] = picked
            both = jnp.concatenate([flat(picked), flat(some(cond_taps, row, k, n, 2)[...])], 1)
            value = dot(both, w1[...], 1, 1)
            some(act, row, k, n, 4)[...] = cells(value)
            u = value * gain
            put_pair(one, row, k, n, cells(u * sigmoid(u)) * inside[...])

    sweep(12, 6, conv_one)
    clear(one)

    def conv_two(k, n):
        value = dot(stack_rows(one, 5, k, n), w2[...], 1, 1)
        for v in range(2):
            x = value[:, halves[v]]
            s = sigmoid(x)
            some(slope, 5 + v, k, n, 5)[...] = cells(s * (1.0 + x * (1.0 - s)))
            put_pair(two, 5 + v, k, n, cells(x * s) * inside[...])

    sweep(11, 11, conv_two)
    clear(two)

    def conv_three(k, n):
        value = dot(stack_rows(two, 6, k, n), w3r[...])
        for v in range(2):
            row = 6 + v
            noised = some(noisy, row, k, n, 3)[...]
            full = skip * noised + out_coef * cells(value[:, halves[v]])
            some(den, row, k, n, 6)[:, :PLANES] = full.astype(bf16)
            delta = delta_coef * (full - (noised - sigma * some(draw, row, k, n, 3)[...]))
            put_pair(dlt, row, k, n, delta * inside[...])

    sweep(10, 5, conv_three)
    clear(dlt)
    fields = (lax.broadcasted_iota(jnp.int32, (16, 128), 0)
              == lax.broadcasted_iota(jnp.int32, (16, 128), 1)).astype(f32).astype(bf16)
    turned = dot(fields, den[1:9].reshape(16 * 128, 128), 1, 1).astype(bf16)
    turned = jnp.concatenate([turned[:, i * 128:(i + 1) * 128] for i in range(16)], axis=0)
    den_rows[...] = dot(turned, back[...])
    for c in range(6):
        left = den_rows[pl.ds(c, 16, stride=16), :]
        right = den_rows[pl.ds(c + 6, 16, stride=16), :]
        piece = jnp.where(lane < TW, left, right).astype(bf16)
        out[:, 96 + c * 16:96 + (c + 1) * 16, :] = jnp.broadcast_to(piece[None], (16, 16, 128))
    den_out = pltpu.make_async_copy(out.at[:, 96:192], out_any.at[:, 96:192], sems.at[3])
    den_out.start()

    def delta_two(k, n):
        parts = []
        for v in range(2):
            picked = pick_pair(dlt, 7 + v, k, n)
            some(taps_d, 7 + v, k, n, 7)[...] = picked
            parts.append(flat(picked))
        value = dot(jnp.concatenate(parts, axis=1), w3f[...], 1, 1)
        for v in range(2):
            x = cells(value[:, halves[v]]) * some(slope, 7 + v, k, n, 5)[...]
            put_pair(sdl, 7 + v, k, n, x * inside[...])

    sweep(9, 9, delta_two)
    clear(sdl)
    film_sum[...] = jnp.zeros((8, 128), f32)

    def delta_one(k, n):
        value = dot(stack_rows(sdl, 8, k, n), w2t[...])
        for v in range(2):
            a = flat(some(act, 8 + v, k, n, 4)[...])
            u = a * gain
            s = sigmoid(u)
            g = flat(cells(value[:, halves[v]] * (s * (1.0 + u * (1.0 - s)))) * tile)
            film_sum[...] += jnp.sum((g * a).reshape(-1, 8, 128), axis=0)
            some(grad1, 8 + v, k, n, 8)[...] = cells(g * gain).astype(bf16)

    sweep(8, 8, delta_one)

    tile_low = tile.astype(bf16)

    def both_rows(read):
        return jnp.concatenate([read(8), read(9)], axis=0)

    def own_cells(ref):
        return lambda row: flat(some(ref, row, 0, 8)[:, 1:PLANES + 1] * tile_low)

    def own_field(ref, base):
        return lambda row: flat(some(ref, row, 0, 8, base)[...])

    def taps_of(row):
        return jnp.concatenate([flat(some(one, row + a - 1, 0, 8)[:, b:b + PLANES])
                                for a in range(3) for b in range(3)], axis=1)

    def first_taps(row):
        return jnp.concatenate([own_field(taps_in, 4)(row), own_field(cond_taps, 2)(row)], axis=1)

    g2 = dot(both_rows(own_cells(sdl)), both_rows(taps_of), 0, 0)
    g1 = dot(both_rows(own_field(grad1, 8)), both_rows(first_taps), 0, 0)
    g3 = dot(both_rows(own_cells(two)), both_rows(own_field(taps_d, 7)), 0, 0)
    film = noise_coef * jnp.sum(film_sum[...], axis=0, keepdims=True)
    film = jnp.transpose(jnp.broadcast_to(film, (8, 128)))[:, 0:1]
    g3 = jnp.where(lax.broadcasted_iota(jnp.int32, (128, 128), 1) == FILM_LANE, film, g3)
    parts = [g2[:, k * 128:(k + 1) * 128] for k in range(9)] + [g1[:, :128], g1[:, 128:], g3]
    for p in range(6):
        pair = [part.reshape(16, 8, 128) for part in parts[2 * p:2 * p + 2]]
        out[:, p * 16:(p + 1) * 16, :] = jnp.concatenate(pair, axis=1).astype(bf16)
    grads_out = pltpu.make_async_copy(out.at[:, 0:96], out_any.at[:, 0:96], sems.at[4])
    grads_out.start()
    grads_out.wait()
    den_out.wait()


def fold_kernel(parts, out):
    for p in range(6):
        total = jnp.sum(parts[:, p * 16:(p + 1) * 16, :].astype(f32), axis=0).astype(bf16)
        for q in range(8):
            out[q, p * 16:(p + 1) * 16, :] = total


def field_kernel(parts, out):
    for k in range(8):
        for c in range(6):
            a = parts[2 * k, 96 + c * 16:96 + (c + 1) * 16, :].astype(f32)
            b = parts[2 * k + 1, 96 + c * 16:96 + (c + 1) * 16, :].astype(f32)
            cols = slice(k * 128, (k + 1) * 128)
            out[c, :, cols] = jnp.concatenate([a[:, :TW], b[:, :TW]], axis=1).astype(bf16)
            out[c + 6, :, cols] = jnp.concatenate([a[:, TW:], b[:, TW:]], axis=1).astype(bf16)


def finish_kernel(parts, g1, g2, g3, film):
    def block(k):
        pair = jnp.sum(parts[:, (k // 2) * 16:(k // 2 + 1) * 16, :].astype(f32), axis=0)
        return pair[(k % 2) * 8:(k % 2) * 8 + 8]

    low, high, third = block(9), block(10), block(11)
    for a in range(3):
        for b in range(3):
            tap = 3 * a + b
            lanes = slice(tap * COUT, (tap + 1) * COUT)
            g2[a, b] = block(tap)
            g1[a, b, :, :COUT] = low[:, lanes]
            g1[a, b, :, COUT:] = high[:, lanes]
            g3[a, b] = third[:, (8 - tap) * COUT:(9 - tap) * COUT]
    film[...] = jnp.transpose(third)[FILM_LANE:FILM_LANE + 1]


VMEM = pl.BlockSpec(memory_space=pltpu.VMEM)
ANY = pl.BlockSpec(memory_space=pl.ANY)


def kernel_call(body, ins, outs, scratch=(), limit=16, cost=None, out_space=VMEM):
    return pl.pallas_call(
        body,
        in_specs=list(ins),
        out_specs=[out_space] * len(outs),
        out_shape=[jax.ShapeDtypeStruct(shape, dtype) for shape, dtype in outs],
        scratch_shapes=list(scratch),
        compiler_params=pltpu.CompilerParams(vmem_limit_bytes=limit * MIB),
        cost_estimate=cost,
    )


def planes(rows, dtype, count=PLANES):
    return pltpu.VMEM((rows, count, SUB, 128), dtype)


def pairs(rows, dtype, count=PLANES):
    return pltpu.VMEM((rows // 2, 2, count, SUB, 128), dtype)


def shards(condition, target, noise_draw, sigma_index, reg_first, reg_second, first_kernel,
           second_kernel, third_kernel, film_scale):
    order, back, spread, repeat = place_constants()
    table = jnp.asarray(coef_table())
    last, leading, packed = kernel_call(
        pack_kernel, [ANY] * 11,
        [((36, 8, 128), bf16), ((36, 8, 128), bf16), ((16, 112, 128), bf16)],
        [pltpu.VMEM((36, 8, 128), bf16), pltpu.VMEM((36, 8, 128), bf16),
         pltpu.VMEM((112, 128), bf16), pltpu.SMEM((1,), jnp.int32), pltpu.SMEM((NSIG, 8), f32),
         pltpu.VMEM((3, COUT, 16, 256), f32), pltpu.VMEM((3, 3, 8, 24), bf16),
         pltpu.VMEM((3, 3, 8, 128), bf16), pltpu.VMEM((3, 3, 8, 12), bf16),
         pltpu.VMEM((3, 3, 12, 16), bf16), pltpu.VMEM((3, 3, 16, 12), bf16),
         pltpu.VMEM((1, 8), bf16), pltpu.SemaphoreType.DMA((29,))],
        limit=60, out_space=ANY,
    )(sigma_index, table, condition, target, noise_draw, jnp.swapaxes(first_kernel, 2, 3),
      jnp.swapaxes(second_kernel, 2, 3), third_kernel, reg_first, reg_second,
      film_scale.reshape(1, 8))
    up = [(i, i + 1) for i in range(lax.axis_size("rows") - 1)]
    before = lax.ppermute(last, "rows", up)
    after = lax.ppermute(leading, "rows", [(j, i) for i, j in up])
    gathered = lax.all_to_all(packed, GROUP, 0, 0, tiled=True)
    cond_taps, fields = kernel_call(
        prep_kernel, [ANY] * 5 + [VMEM] * 2 + [ANY] * 2,
        [((14, 2, PLANES, SUB, 128), bf16), ((13, 2, PLANES, SUB, 128), bf16)],
        [pltpu.SMEM((1,), jnp.int32), pltpu.SMEM((NSIG, 8), f32),
         pltpu.VMEM((48, 32, 128), f32), pltpu.VMEM((3, COUT, 16, 256), f32),
         planes(32, bf16, 7), pltpu.VMEM((30 * WIN, 128), bf16), pltpu.VMEM((WIN, 128), bf16), pltpu.VMEM((128, 128), bf16),
         pltpu.SemaphoreType.DMA((7,))],
        limit=52,
        cost=pl.CostEstimate(flops=1 << 32, bytes_accessed=8 * MIB, transcendentals=0),
    )(sigma_index, table, condition, target, noise_draw, before, after, jnp.asarray(order, bf16), jnp.asarray(spread[:, :128], bf16))
    wide = [pairs(40, bf16, PLANES + 2) for _ in range(6)]
    out, = kernel_call(
        step_kernel, [ANY] * 3 + [VMEM] * 5, [((16, 192, 128), bf16)],
        [pltpu.VMEM((16, 192, 128), bf16), pltpu.SMEM((1,), jnp.int32),
         pltpu.SMEM((NSIG, 8), f32), pairs(26, bf16),
         pltpu.SemaphoreType.DMA((5,)), pltpu.VMEM((256, 1536), bf16),
         pltpu.VMEM((1536, 256), bf16), pltpu.VMEM((128, 256), bf16),
         pltpu.VMEM((128, 128), bf16), pltpu.VMEM((256, 256), bf16),
         pltpu.VMEM((1536, 256), bf16), pltpu.VMEM((256, 256), bf16),
         pltpu.VMEM((1536, 256), bf16)]
        + wide
        + [pairs(24, bf16), pairs(18, bf16), pairs(26, f32), pairs(26, f32),
           pairs(24, f32), pairs(22, f32), pairs(20, bf16, 8), pairs(16, bf16),
           pltpu.VMEM((8, 128), f32), pltpu.VMEM((256, 128), f32),
           pltpu.VMEM((PLANES, SUB, 128), f32)],
        limit=52, out_space=ANY,
    )(sigma_index, table, fields, cond_taps, gathered, jnp.asarray(repeat, bf16),
      jnp.asarray(back, bf16), jnp.asarray(spread[:, 128:], bf16))
    parts = lax.all_to_all(out, GROUP, 0, 0, tiled=True)
    folded, = kernel_call(fold_kernel, [VMEM], [((8, 96, 128), bf16)])(parts)
    denoised, = kernel_call(
        field_kernel, [VMEM], [((COUT, 16, NW), bf16)],
        cost=pl.CostEstimate(flops=1 << 26, bytes_accessed=2 * MIB, transcendentals=0),
    )(parts)
    sums = lax.all_to_all(folded, "rows", 0, 0, tiled=True)
    g1, g2, g3, film = kernel_call(
        finish_kernel, [VMEM],
        [((3, 3, 8, 24), f32), ((3, 3, 8, 128), f32), ((3, 3, 8, 12), f32), ((1, 8), f32)],
    )(sums)
    return denoised, jnp.swapaxes(g1, 2, 3), jnp.swapaxes(g2, 2, 3), g3, film.reshape(8)


def solution(mesh):
    return jax.shard_map(
        shards,
        mesh=mesh,
        in_specs=(
            P(None, "rows", None),
            P(None, "rows", None),
            P(None, "rows", None),
            P(),
            P(None, None, None, "chan"),
            P(None, None, "chan", None),
            P(None, None, None, GROUP),
            P(None, None, None, GROUP),
            P(None, None, GROUP, None),
            P(GROUP),
        ),
        out_specs=(
            P(None, "rows", None),
            P(None, None, None, GROUP),
            P(None, None, None, GROUP),
            P(None, None, GROUP, None),
            P(GROUP),
        ),
        check_vma=False,
    )
```
